32 devices in a mesh: line: 4 (over y, x), patch: 8 (over z, core).
Axes of the slice: x: 2, y: 2, z: 4, core: 2. Of those that a mesh axis runs over, the one named last changes fastest.
Arguments:
- newton_residual: float32 [8, 48, 8, 128], P('line', None, 'patch'), may hold values from -24 to 24
- diag_block: bfloat16 [8, 48, 48, 8, 128], P('line', None, None, 'patch'), may hold values from -0.6 to 5
- lower: bfloat16 [8, 48, 48, 8, 128], P('line', None, None, 'patch'), may hold values from -1.296875 to 1.296875
- upper: bfloat16 [8, 48, 48, 8, 128], P('line', None, None, 'patch'), may hold values from -1.296875 to 1.296875
- west: bfloat16 [8, 48, 48, 8, 128], P('line', None, None, 'patch'), may hold values from -0.5390625 to 0.5390625
- east: bfloat16 [8, 48, 48, 8, 128], P('line', None, None, 'patch'), may hold values from -0.5390625 to 0.5390625
- pivot_inverse: bfloat16 [8, 48, 48, 8, 128], P('line', None, None, 'patch'), may hold values from -0.05 to 0.34
Outputs:
- newton_step: float32 [8, 48, 8, 128], P('line', None, 'patch')
The draws below stay inside these ranges and needn't reach their ends.
All inputs are finite; a program needn't handle non-finite values.
Results may differ from the reference program's by a relative error of at most 0.0003.
Values sent between devices are 32-bit elements; how exact they have to be, the bound alone decides.
No kernel may reach another device: no remote copies, remote signals or barrier semaphores. Data moves between devices by JAX's collectives and lax.ppermute only.
A program may use at most 64 MiB of HBM per device.

```python
import math
import jax
import jax.numpy as jnp
from jax import lax

BLOCK = 48
ACROSS = 128
ITERS = 4
LEN = 8
ROWS = 8


def draw_diag_block(key, part):
    first_key, second_key = jax.random.split(jax.random.fold_in(key, 11))
    diagonal = jax.random.uniform(first_key, (LEN, BLOCK, ROWS, ACROSS), jnp.float32, 3.0, 5.0)
    spread = jnp.clip(jax.random.normal(second_key, (LEN, BLOCK, BLOCK, ROWS, ACROSS), jnp.float32), -4.0, 4.0)
    spread = spread / math.sqrt(BLOCK)
    identity = jnp.eye(BLOCK, dtype=jnp.float32)[None, :, :, None, None]
    whole = spread * (1.0 - identity) + identity * diagonal[:, :, None, :, :]
    return whole.astype(jnp.bfloat16)


def draw_pivot_inverse(key, part):
    first_key, second_key = jax.random.split(jax.random.fold_in(key, 23))
    diagonal = jnp.exp(jax.random.uniform(first_key, (LEN, BLOCK, ROWS, ACROSS), jnp.float32, math.log(0.2), math.log(0.33)))
    spread = jnp.clip(jax.random.normal(second_key, (LEN, BLOCK, BLOCK, ROWS, ACROSS), jnp.float32), -4.0, 4.0)
    spread = spread * (0.08 / math.sqrt(BLOCK))
    identity = jnp.eye(BLOCK, dtype=jnp.float32)[None, :, :, None, None]
    whole = spread * (1.0 - identity) + identity * diagonal[:, :, None, :, :]
    return whole.astype(jnp.bfloat16)


def block_levels(rng, dims, pieces, low, high):
    level = 1.0
    for position, parts in pieces:
        steps = jax.random.uniform(jax.random.fold_in(jax.random.fold_in(rng, 6), position), (parts,), jnp.float32, low / len(pieces), high / len(pieces))
        level = level * jnp.repeat(jnp.exp(steps), dims[position] // parts).reshape((-1,) + (1,) * (len(dims) - 1 - position))
    return level


def bell_draw(rng, extent, deviation, most, shards=(), held_as=jnp.bfloat16):
    array = deviation * jax.random.normal(rng, extent, jnp.float32)
    if shards:
        array = array * block_levels(rng, extent, shards, -0.22, 0.18)
    return jnp.clip(array, -most, most).astype(held_as)


def setup_inputs(seed: int = 0) -> dict:
    splits = jax.random.split(jax.random.key(seed), 8)
    return {
        "newton_residual": bell_draw(splits[0], (LEN, BLOCK, ROWS, ACROSS), 4.0, 24.0, ((0, 4), (2, 8)), jnp.float32),
        "diag_block": draw_diag_block(jax.random.fold_in(splits[7], 71), 0),
        "lower": bell_draw(splits[2], (LEN, BLOCK, BLOCK, ROWS, ACROSS), 0.22, 1.296875, ((0, 4), (3, 8))),
        "upper": bell_draw(splits[3], (LEN, BLOCK, BLOCK, ROWS, ACROSS), 0.22, 1.296875, ((0, 4), (3, 8))),
        "west": bell_draw(splits[4], (LEN, BLOCK, BLOCK, ROWS, ACROSS), 0.09, 0.5390625, ((0, 4), (3, 8))),
        "east": bell_draw(splits[5], (LEN, BLOCK, BLOCK, ROWS, ACROSS), 0.09, 0.5390625, ((0, 4), (3, 8))),
        "pivot_inverse": draw_pivot_inverse(jax.random.fold_in(splits[7], 71), 0),
    }


def block_apply(block_mat, vector):
    return lax.map(lambda couple: lax.optimization_barrier(jnp.sum(couple[0].astype(jnp.float32) * couple[1][None], axis=1)), (block_mat, vector))

def single_apply(block_mat, vector):
    return lax.optimization_barrier(jnp.sum(block_mat.astype(jnp.float32) * vector[None], axis=1))

def operator_apply(field, diag_block, lower, upper, west, east):
    zero_layer = jnp.zeros_like(field[:1])
    below = jnp.concatenate([zero_layer, field[:-1]], axis=0)
    above = jnp.concatenate([field[1:], zero_layer], axis=0)
    zero_row = jnp.zeros_like(field[:, :, :1])
    before = jnp.concatenate([zero_row, field[:, :, :-1]], axis=2)
    after = jnp.concatenate([field[:, :, 1:], zero_row], axis=2)
    total = block_apply(diag_block, field) + block_apply(lower, below) + block_apply(upper, above)
    return total + block_apply(west, before) + block_apply(east, after)

def line_solve(vector, lower, upper, pivot):
    count = vector.shape[0]
    previous = jnp.zeros_like(vector[0])
    forward = []
    for k in range(count):
        previous = single_apply(pivot[k], vector[k] - single_apply(lower[k], previous))
        forward.append(previous)
    following = jnp.zeros_like(vector[0])
    result = [None] * count
    for k in reversed(range(count)):
        following = forward[k] - single_apply(pivot[k], single_apply(upper[k], following))
        result[k] = following
    return jnp.stack(result)

def least_squares(hess, beta):
    width = hess.shape[1]
    hess_rows = [hess[i] for i in range(width + 1)]
    target = [beta] + [jnp.zeros((), jnp.float32) for i in range(width)]
    for j in range(width):
        first = hess_rows[j][j]
        second = hess_rows[j + 1][j]
        radius = jnp.sqrt(first * first + second * second)
        cosine = first / radius
        sine_part = second / radius
        upper_row = cosine * hess_rows[j] + sine_part * hess_rows[j + 1]
        lower_row = cosine * hess_rows[j + 1] - sine_part * hess_rows[j]
        hess_rows[j] = upper_row
        hess_rows[j + 1] = lower_row
        top_value = cosine * target[j] + sine_part * target[j + 1]
        low_value = cosine * target[j + 1] - sine_part * target[j]
        target[j] = top_value
        target[j + 1] = low_value
    solution = [None] * width
    for i in reversed(range(width)):
        accum_value = target[i]
        for k in range(i + 1, width):
            accum_value = accum_value - hess_rows[i][k] * solution[k]
        solution[i] = accum_value / hess_rows[i][i]
    return solution

def reference(newton_residual, diag_block, lower, upper, west, east, pivot_inverse):
    beta = jnp.sqrt(jnp.sum(newton_residual * newton_residual))
    basis = [newton_residual / beta]
    directions = []
    columns = []
    for j in range(ITERS):
        direction = line_solve(basis[j], lower, upper, pivot_inverse)
        directions.append(direction)
        image = operator_apply(direction, diag_block, lower, upper, west, east)
        projections = jnp.stack([jnp.sum(member * image) for member in basis])
        for i in range(j + 1):
            image = image - projections[i] * basis[i]
        new_norm = jnp.sqrt(jnp.sum(image * image))
        basis.append(image / new_norm)
        columns.append(jnp.concatenate([projections, new_norm[None], jnp.zeros((ITERS - 1 - j,), jnp.float32)]))
    hess = jnp.stack(columns, axis=1)
    coeffs = least_squares(hess, beta)
    newton_step = coeffs[0] * directions[0]
    for j in range(1, ITERS):
        newton_step = newton_step + coeffs[j] * directions[j]
    return newton_step
```

```python
import jax
import jax.numpy as jnp
from jax import lax
from jax.experimental import pallas as pl
from jax.experimental.pallas import tpu as pltpu
from jax.sharding import PartitionSpec as P

ITERS = 4


def single_apply(block_mat, vector):
    return jnp.sum(block_mat.astype(jnp.float32) * vector[None], axis=1)


def block_apply(block_mat, vector):
    return jnp.sum(block_mat.astype(jnp.float32) * vector[:, None], axis=2)


def sweep_down(vector, lower, pivot, incoming):
    previous = incoming
    forward = []
    for k in range(vector.shape[0]):
        previous = single_apply(pivot[k], vector[k] - single_apply(lower[k], previous))
        forward.append(previous)
    return forward


def sweep_up(forward, upper, pivot, incoming):
    count = len(forward)
    following = incoming
    result = [None] * count
    coupled = [None] * count
    for k in reversed(range(count)):
        coupled[k] = single_apply(upper[k], following)
        following = forward[k] - single_apply(pivot[k], coupled[k])
        result[k] = following
    return result, coupled


def precondition(vector, lower, upper, pivot):
    count = lax.axis_size("line")
    incoming = jnp.zeros_like(vector[0])
    for turn in range(count - 1):
        outgoing = sweep_down(vector, lower, pivot, incoming)[-1]
        incoming = incoming + lax.ppermute(outgoing, "line", [(turn, turn + 1)])
    forward = sweep_down(vector, lower, pivot, incoming)
    incoming = jnp.zeros_like(vector[0])
    for turn in reversed(range(count - 1)):
        outgoing = sweep_up(forward, upper, pivot, incoming)[0][0]
        incoming = incoming + lax.ppermute(outgoing, "line", [(turn + 1, turn)])
    result, coupled = sweep_up(forward, upper, pivot, incoming)
    return jnp.stack(result), jnp.stack(coupled)


def rows_beside(field, across):
    count = lax.axis_size("patch")
    even = [(i, i + 1) for i in range(0, count - 1, 2)]
    odd = [(i, i + 1) for i in range(1, count - 1, 2)]
    is_even = lax.axis_index("patch") % 2 == 0
    first, last = field[..., :across], field[..., -across:]
    several = field.shape[-1] > across
    to_far = jnp.where(is_even, first, last) if several else field
    to_near = jnp.where(is_even, last, first) if several else field
    far = lax.ppermute(to_far, "patch", odd + [(b, a) for a, b in odd])
    near = lax.ppermute(to_near, "patch", even + [(b, a) for a, b in even])
    before, after = jnp.where(is_even, far, near), jnp.where(is_even, near, far)
    if several:
        before = jnp.concatenate([before, field[..., :-across]], axis=-1)
        after = jnp.concatenate([field[..., across:], after], axis=-1)
    return before, after


def pairs_of(count):
    return [(i, j) for i in range(count) for j in range(i, count)]


def gram_kernel(*refs):
    ins, out = refs[:-1], refs[-1]
    lane = lax.broadcasted_iota(jnp.int32, (1, 128), 1)
    total = jnp.zeros((1, 128), jnp.float32)
    vectors = [ref[...] for ref in ins]
    for place, (i, j) in enumerate(pairs_of(len(vectors))):
        part = jnp.sum(vectors[i] * vectors[j], axis=0, keepdims=True)
        total = jnp.where(lane == place, jnp.sum(part, axis=1, keepdims=True), total)
    out[...] = jnp.broadcast_to(total, out.shape)


def finish_kernel(parts_ref, *refs):
    directions, out = refs[:-1], refs[-1]
    width = len(directions)
    total = jnp.sum(parts_ref[...], axis=0, keepdims=True)
    lane = lax.broadcasted_iota(jnp.int32, total.shape, 1)
    gram = {}
    for place, pair in enumerate(pairs_of(width + 1)):
        value = jnp.sum(jnp.where(lane == place, total, 0.0), axis=1, keepdims=True)
        gram[pair] = gram[pair[::-1]] = value
    half = [[gram[j + 1, i] + gram[j, i] for i in range(width + 1)] for j in range(width)]
    normal = [[half[j][i + 1] + half[j][i] for i in range(width)] for j in range(width)]
    right = [half[j][0] for j in range(width)]
    for i in range(width):
        inverse = 1.0 / normal[i][i]
        for j in range(i + 1, width):
            factor = normal[j][i] * inverse
            for k in range(i, width):
                normal[j][k] = normal[j][k] - factor * normal[i][k]
            right[j] = right[j] - factor * right[i]
    coeffs = [None] * width
    for i in reversed(range(width)):
        value = right[i]
        for k in range(i + 1, width):
            value = value - normal[i][k] * coeffs[k]
        coeffs[i] = value / normal[i][i]
    step = coeffs[0] * directions[0][...]
    for j in range(1, width):
        step = step + coeffs[j] * directions[j][...]
    out[...] = step


def per_device(newton_residual, diag_block, lower, upper, west, east, pivot_inverse):
    shape = newton_residual.shape
    count, block, rows, across = shape
    wide = rows * across

    def flat(matrix):
        return matrix.reshape(count, block, block, wide)

    diag_block, lower, upper, west, east, pivot = map(
        flat, (diag_block, lower, upper, west, east, pivot_inverse)
    )
    line = lax.axis_size("line")
    devices = line * lax.axis_size("patch")
    basis = [newton_residual.reshape(count, block, wide)]
    directions = []
    for j in range(ITERS):
        direction, coupled = precondition(basis[j], lower, upper, pivot)
        directions.append(direction)
        before, after = rows_beside(direction, across)
        below = lax.ppermute(direction[-1], "line", [(i, i + 1) for i in range(line - 1)])
        image = coupled - basis[j] + block_apply(diag_block, direction)
        image = image + block_apply(lower, jnp.concatenate([below[None], direction[:-1]]))
        image = image + block_apply(west, before) + block_apply(east, after)
        basis.append(image)
    sums = pl.pallas_call(
        gram_kernel,
        out_shape=jax.ShapeDtypeStruct((devices, 128), jnp.float32),
    )(*[member.reshape(count * block, wide) for member in basis])
    sums = lax.all_to_all(sums, ("line", "patch"), 0, 0, tiled=True)
    step = pl.pallas_call(
        finish_kernel,
        out_shape=jax.ShapeDtypeStruct((count * block, wide), jnp.float32),
    )(sums, *[direction.reshape(count * block, wide) for direction in directions])
    return step.reshape(shape)


def solution(mesh):
    blocks = P("line", None, None, "patch", None)
    field = P("line", None, "patch", None)
    return jax.shard_map(
        per_device, mesh=mesh, in_specs=(field,) + (blocks,) * 6, out_specs=field, check_vma=False
    )
```

```python
import jax
import jax.numpy as jnp
from jax import lax
from jax.experimental import pallas as pl
from jax.experimental.pallas import tpu as pltpu
from jax.sharding import PartitionSpec as P

ITERS = 4


def single_apply(block_mat, vector):
    return jnp.sum(block_mat.astype(jnp.float32) * vector[None], axis=1)


def block_apply(block_mat, vector):
    return jnp.sum(block_mat.astype(jnp.float32) * vector[:, None], axis=2)


def sweep_down(vector, lower, pivot, entry):
    forward = [single_apply(pivot[0], vector[0] + single_apply(lower[0], entry))]
    for k in range(1, vector.shape[0]):
        forward.append(single_apply(pivot[k], vector[k] - single_apply(lower[k], forward[-1])))
    return forward


def sweep_up(forward, upper, pivot, incoming):
    count = len(forward)
    following = incoming
    result = [None] * count
    coupled = [None] * count
    for k in reversed(range(count)):
        coupled[k] = single_apply(upper[k], following)
        following = forward[k] - single_apply(pivot[k], coupled[k])
        result[k] = following
    return result, coupled


def precondition(vector, last, lower, upper, pivot):
    count = lax.axis_size("line")
    incoming = jnp.zeros((1 if last is None else 2,) + vector.shape[1:], vector.dtype)

    def entry():
        return -incoming[0] if last is None else incoming[1] - incoming[0]

    for turn in range(count - 1):
        outgoing = sweep_down(vector, lower, pivot, entry())[-1]
        message = outgoing[None] if last is None else jnp.stack([outgoing, last])
        incoming = incoming + lax.ppermute(message, "line", [(turn, turn + 1)])
    forward = sweep_down(vector, lower, pivot, entry())
    below = None if last is None else incoming[1]
    incoming = jnp.zeros_like(vector[0])
    for turn in reversed(range(count - 1)):
        outgoing = sweep_up(forward, upper, pivot, incoming)[0][0]
        incoming = incoming + lax.ppermute(outgoing, "line", [(turn + 1, turn)])
    result, coupled = sweep_up(forward, upper, pivot, incoming)
    return jnp.stack(result), jnp.stack(coupled), below


def rows_beside(field, across):
    count = lax.axis_size("patch")
    even = [(i, i + 1) for i in range(0, count - 1, 2)]
    odd = [(i, i + 1) for i in range(1, count - 1, 2)]
    is_even = lax.axis_index("patch") % 2 == 0
    first, last = field[..., :across], field[..., -across:]
    several = field.shape[-1] > across
    to_far = jnp.where(is_even, first, last) if several else field
    to_near = jnp.where(is_even, last, first) if several else field
    far = lax.ppermute(to_far, "patch", odd + [(b, a) for a, b in odd])
    near = lax.ppermute(to_near, "patch", even + [(b, a) for a, b in even])
    before, after = jnp.where(is_even, far, near), jnp.where(is_even, near, far)
    if several:
        before = jnp.concatenate([before, field[..., :-across]], axis=-1)
        after = jnp.concatenate([field[..., across:], after], axis=-1)
    return before, after


def pairs_of(count):
    return [(i, j) for i in range(count) for j in range(i, count)]


def gram_kernel(*refs):
    ins, out = refs[:-1], refs[-1]
    lane = lax.broadcasted_iota(jnp.int32, (1, 128), 1)
    total = jnp.zeros((1, 128), jnp.float32)
    vectors = [ref[...] for ref in ins]
    for place, (i, j) in enumerate(pairs_of(len(vectors))):
        part = jnp.sum(vectors[i] * vectors[j], axis=0, keepdims=True)
        total = jnp.where(lane == place, jnp.sum(part, axis=1, keepdims=True), total)
    out[...] = jnp.broadcast_to(total, out.shape)


def finish_kernel(parts_ref, *refs):
    directions, out = refs[:-1], refs[-1]
    width = len(directions)
    total = jnp.sum(parts_ref[...], axis=0, keepdims=True)
    lane = lax.broadcasted_iota(jnp.int32, total.shape, 1)
    gram = {}
    for place, pair in enumerate(pairs_of(width + 1)):
        value = jnp.sum(jnp.where(lane == place, total, 0.0), axis=1, keepdims=True)
        gram[pair] = gram[pair[::-1]] = value
    half = [[gram[j + 1, i] + gram[j, i] for i in range(width + 1)] for j in range(width)]
    normal = [[half[j][i + 1] + half[j][i] for i in range(width)] for j in range(width)]
    right = [half[j][0] for j in range(width)]
    for i in range(width):
        inverse = 1.0 / normal[i][i]
        for j in range(i + 1, width):
            factor = normal[j][i] * inverse
            for k in range(i, width):
                normal[j][k] = normal[j][k] - factor * normal[i][k]
            right[j] = right[j] - factor * right[i]
    coeffs = [None] * width
    for i in reversed(range(width)):
        value = right[i]
        for k in range(i + 1, width):
            value = value - normal[i][k] * coeffs[k]
        coeffs[i] = value / normal[i][i]
    step = coeffs[0] * directions[0][...]
    for j in range(1, width):
        step = step + coeffs[j] * directions[j][...]
    out[...] = step


def per_device(newton_residual, diag_block, lower, upper, west, east, pivot_inverse):
    shape = newton_residual.shape
    count, block, rows, across = shape
    wide = rows * across

    def flat(matrix):
        return matrix.reshape(count, block, block, wide)

    diag_block, lower, upper, west, east, pivot = map(
        flat, (diag_block, lower, upper, west, east, pivot_inverse)
    )
    line = lax.axis_size("line")
    devices = line * lax.axis_size("patch")
    basis = [newton_residual.reshape(count, block, wide)]
    directions = []
    last = None
    for j in range(ITERS):
        direction, coupled, below = precondition(basis[j], last, lower, upper, pivot)
        if below is not None:
            basis[j] = basis[j].at[0].add(single_apply(lower[0], below))
        directions.append(direction)
        before, after = rows_beside(direction, across)
        last = direction[-1]
        image = coupled - basis[j] + block_apply(diag_block, direction)
        inner = [single_apply(lower[k], direction[k - 1]) for k in range(1, count)]
        if j == ITERS - 1:
            below = lax.ppermute(last, "line", [(i, i + 1) for i in range(line - 1)])
            inner = [single_apply(lower[0], below)] + inner
        else:
            inner = [jnp.zeros_like(last)] + inner
        image = image + jnp.stack(inner)
        image = image + block_apply(west, before) + block_apply(east, after)
        basis.append(image)
    sums = pl.pallas_call(
        gram_kernel,
        out_shape=jax.ShapeDtypeStruct((devices, 128), jnp.float32),
    )(*[member.reshape(count * block, wide) for member in basis])
    sums = lax.all_to_all(sums, ("line", "patch"), 0, 0, tiled=True)
    step = pl.pallas_call(
        finish_kernel,
        out_shape=jax.ShapeDtypeStruct((count * block, wide), jnp.float32),
    )(sums, *[direction.reshape(count * block, wide) for direction in directions])
    return step.reshape(shape)


def solution(mesh):
    blocks = P("line", None, None, "patch", None)
    field = P("line", None, "patch", None)
    return jax.shard_map(
        per_device, mesh=mesh, in_specs=(field,) + (blocks,) * 6, out_specs=field, check_vma=False
    )
```

```python
import jax
import jax.numpy as jnp
from jax import lax
from jax.experimental import pallas as pl
from jax.experimental.pallas import tpu as pltpu
from jax.sharding import PartitionSpec as P

ITERS = 4


def single_apply(block_mat, vector):
    return jnp.sum(block_mat.astype(jnp.float32) * vector[None], axis=1)


def block_apply(block_mat, vector):
    return jnp.sum(block_mat.astype(jnp.float32) * vector[:, None], axis=2)


def sweep_down(vector, lower, pivot, entry):
    forward = [single_apply(pivot[0], vector[0] + single_apply(lower[0], entry))]
    for k in range(1, vector.shape[0]):
        forward.append(single_apply(pivot[k], vector[k] - single_apply(lower[k], forward[-1])))
    return forward


def sweep_up(forward, upper, pivot, incoming):
    count = len(forward)
    following = incoming
    result = [None] * count
    coupled = [None] * count
    for k in reversed(range(count)):
        coupled[k] = single_apply(upper[k], following)
        following = forward[k] - single_apply(pivot[k], coupled[k])
        result[k] = following
    return result, coupled


def down_entry(message):
    return -message[0] if message.shape[0] == 1 else message[1] - message[0]


def precondition(vector, last, lower, upper, pivot, products=None):
    count = lax.axis_size("line")
    incoming = jnp.zeros((1 if last is None else 2,) + vector.shape[1:], vector.dtype)
    for turn in range(count - 1):
        outgoing = sweep_down(vector, lower, pivot, down_entry(incoming))[-1]
        if products is not None:
            products.down(turn, outgoing)
        message = outgoing[None] if last is None else jnp.stack([outgoing, last])
        incoming = incoming + lax.ppermute(message, "line", [(turn, turn + 1)])
    forward = sweep_down(vector, lower, pivot, down_entry(incoming))
    below = None if last is None else incoming[1]
    incoming = jnp.zeros_like(vector[0])
    for turn in range(count - 1):
        outgoing = sweep_up(forward, upper, pivot, incoming)[0][0]
        if products is not None:
            outgoing = products.up(turn, outgoing)
        pair = (count - 1 - turn, count - 2 - turn)
        incoming = incoming + lax.ppermute(outgoing, "line", [pair])
    result, coupled = sweep_up(forward, upper, pivot, incoming)
    return jnp.stack(result), jnp.stack(coupled), below


def short_precondition(vector, last, lower, upper, pivot, near, far):
    nothing = jnp.zeros_like(last)
    outgoing = sweep_down(vector, lower, pivot, nothing)[-1]
    first = lax.ppermute(jnp.stack([outgoing, last]), "line", [(0, 1), (2, 3)])
    entry = down_entry(first)
    message = jnp.stack([sweep_down(vector, lower, pivot, entry)[-1], last])
    to_last = lax.ppermute(message, "line", [(1, 3)])
    to_next = lax.ppermute(message, "line", [(1, 2)])
    entry = entry + down_entry(to_next) + single_apply(near, down_entry(to_last))
    below = first[1] + to_next[1]
    forward = sweep_down(vector, lower, pivot, entry)
    outgoing = sweep_up(forward, upper, pivot, nothing)[0][0]
    third = lax.ppermute(outgoing, "line", [(3, 0)])
    second = lax.ppermute(outgoing, "line", [(2, 0)])
    beside = lax.ppermute(outgoing, "line", [(3, 2), (1, 0)])
    incoming = beside + single_apply(near, second + single_apply(far, third))
    outgoing = sweep_up(forward, upper, pivot, incoming)[0][0]
    incoming = incoming + lax.ppermute(outgoing, "line", [(2, 1)])
    result, coupled = sweep_up(forward, upper, pivot, incoming)
    return jnp.stack(result), jnp.stack(coupled), below


def multiply_lines(left, right, out):
    block = right.shape[0]
    group = max(g for g in (1, 2, 3, 4) if block % g == 0)
    unroll = max(u for u in (1, 2, 4, 8) if block % u == 0)

    def rows(step, carry):
        start = step * group

        def add(j, totals):
            row = right[j]
            return tuple(
                total + left[start + q, pl.ds(j, 1), :] * row for q, total in enumerate(totals)
            )

        zero = jnp.zeros(right.shape[1:], jnp.float32)
        totals = lax.fori_loop(0, block, add, (zero,) * group, unroll=unroll)
        for q, total in enumerate(totals):
            out[start + q] = total
        return carry

    lax.fori_loop(0, block // group, rows, 0)


def factors_kernel(up_on, down_on, lower, upper, pivot, after, out, held, left, right, made, sem):
    me = lax.axis_index("line")
    up = me == up_on

    def widen(source, target):
        def row(i, carry):
            target[i] = source[i].astype(jnp.float32)
            return carry

        lax.fori_loop(0, target.shape[0], row, 0, unroll=4)

    def run(coupling, order):
        for place, k in enumerate(order):
            copies = [
                pltpu.make_async_copy(pivot.at[k], held.at[0], sem.at[0]),
                pltpu.make_async_copy(coupling.at[k], held.at[1], sem.at[1]),
            ]
            for copy in copies:
                copy.start()
            for copy in copies:
                copy.wait()
            widen(held.at[0], left)
            widen(held.at[1], right)
            multiply_lines(left, right, made)
            copy = pltpu.make_async_copy(made, out.at[place], sem.at[0])
            copy.start()
            copy.wait()

    if up_on is not None:
        pl.when(up)(lambda: run(upper, (0, 1)))
    if down_on is not None:
        pl.when(me == down_on)(lambda: run(lower, (1, 0)))


def factors(up_on, down_on, lower, upper, pivot, after):
    shape = lower.shape[1:]
    anywhere = pl.BlockSpec(memory_space=pl.ANY)
    return pl.pallas_call(
        lambda *refs: factors_kernel(up_on, down_on, *refs),
        out_shape=jax.ShapeDtypeStruct((2,) + shape, jnp.float32),
        in_specs=[anywhere] * 4,
        out_specs=anywhere,
        scratch_shapes=[
            pltpu.VMEM((2,) + shape, lower.dtype),
            pltpu.VMEM(shape, jnp.float32),
            pltpu.VMEM(shape, jnp.float32),
            pltpu.VMEM(shape, jnp.float32),
            pltpu.SemaphoreType.DMA((2,)),
        ],
        compiler_params=pltpu.CompilerParams(vmem_limit_bytes=12 << 20),
    )(lower, upper, pivot, after)


def product_kernel(on, pair, after, out, left, right, made, sem):
    me = lax.axis_index("line")
    here = me == on[0]
    for other in on[1:]:
        here = here | (me == other)

    @pl.when(here)
    def _():
        copies = [
            pltpu.make_async_copy(pair.at[0], left, sem.at[0]),
            pltpu.make_async_copy(pair.at[1], right, sem.at[1]),
        ]
        for copy in copies:
            copy.start()
        for copy in copies:
            copy.wait()
        multiply_lines(left, right, made)
        copy = pltpu.make_async_copy(made, out, sem.at[0])
        copy.start()
        copy.wait()


def product(on, pair, after):
    shape = pair.shape[1:]
    anywhere = pl.BlockSpec(memory_space=pl.ANY)
    return pl.pallas_call(
        lambda *refs: product_kernel(on, *refs),
        out_shape=jax.ShapeDtypeStruct(shape, jnp.float32),
        in_specs=[anywhere] * 2,
        out_specs=anywhere,
        scratch_shapes=[pltpu.VMEM(shape, jnp.float32)] * 3 + [pltpu.SemaphoreType.DMA((2,))],
        compiler_params=pltpu.CompilerParams(vmem_limit_bytes=12 << 20),
    )(pair, after)


class Products:
    def __init__(self, vector, lower, upper, pivot):
        self.blocks = lower, upper, pivot
        self.early = product((2,), factors(2, None, *self.blocks, vector), vector)

    def down(self, turn, outgoing):
        if turn == 1:
            early, _ = lax.optimization_barrier((self.early, outgoing))
            self.far = lax.ppermute(early, "line", [(2, 0)])
        if turn == 2:
            self.pair = factors(1, 2, *self.blocks, outgoing)

    def up(self, turn, outgoing):
        if turn == 0:
            outgoing, self.pair = lax.optimization_barrier((outgoing, self.pair))
        if turn == 1:
            self.made = product((1, 2), self.pair, outgoing)
        if turn == 2:
            outgoing, made = lax.optimization_barrier((outgoing, self.made))
            self.near = lax.ppermute(made, "line", [(1, 0), (2, 3)])
        return outgoing


def rows_beside(field, across):
    count = lax.axis_size("patch")
    even = [(i, i + 1) for i in range(0, count - 1, 2)]
    odd = [(i, i + 1) for i in range(1, count - 1, 2)]
    is_even = lax.axis_index("patch") % 2 == 0
    first, last = field[..., :across], field[..., -across:]
    several = field.shape[-1] > across
    to_far = jnp.where(is_even, first, last) if several else field
    to_near = jnp.where(is_even, last, first) if several else field
    far = lax.ppermute(to_far, "patch", odd + [(b, a) for a, b in odd])
    near = lax.ppermute(to_near, "patch", even + [(b, a) for a, b in even])
    before, after = jnp.where(is_even, far, near), jnp.where(is_even, near, far)
    if several:
        before = jnp.concatenate([before, field[..., :-across]], axis=-1)
        after = jnp.concatenate([field[..., across:], after], axis=-1)
    return before, after


def pairs_of(count):
    return [(i, j) for i in range(count) for j in range(i, count)]


def gram_kernel(*refs):
    ins, out = refs[:-1], refs[-1]
    lane = lax.broadcasted_iota(jnp.int32, (1, 128), 1)
    total = jnp.zeros((1, 128), jnp.float32)
    vectors = [ref[...] for ref in ins]
    for place, (i, j) in enumerate(pairs_of(len(vectors))):
        part = jnp.sum(vectors[i] * vectors[j], axis=0, keepdims=True)
        total = jnp.where(lane == place, jnp.sum(part, axis=1, keepdims=True), total)
    out[...] = jnp.broadcast_to(total, out.shape)


def finish_kernel(parts_ref, *refs):
    directions, out = refs[:-1], refs[-1]
    width = len(directions)
    total = jnp.sum(parts_ref[...], axis=0, keepdims=True)
    lane = lax.broadcasted_iota(jnp.int32, total.shape, 1)
    gram = {}
    for place, pair in enumerate(pairs_of(width + 1)):
        value = jnp.sum(jnp.where(lane == place, total, 0.0), axis=1, keepdims=True)
        gram[pair] = gram[pair[::-1]] = value
    half = [[gram[j + 1, i] + gram[j, i] for i in range(width + 1)] for j in range(width)]
    normal = [[half[j][i + 1] + half[j][i] for i in range(width)] for j in range(width)]
    right = [half[j][0] for j in range(width)]
    for i in range(width):
        inverse = 1.0 / normal[i][i]
        for j in range(i + 1, width):
            factor = normal[j][i] * inverse
            for k in range(i, width):
                normal[j][k] = normal[j][k] - factor * normal[i][k]
            right[j] = right[j] - factor * right[i]
    coeffs = [None] * width
    for i in reversed(range(width)):
        value = right[i]
        for k in range(i + 1, width):
            value = value - normal[i][k] * coeffs[k]
        coeffs[i] = value / normal[i][i]
    step = coeffs[0] * directions[0][...]
    for j in range(1, width):
        step = step + coeffs[j] * directions[j][...]
    out[...] = step


def per_device(newton_residual, diag_block, lower, upper, west, east, pivot_inverse):
    shape = newton_residual.shape
    count, block, rows, across = shape
    wide = rows * across

    def flat(matrix):
        return matrix.reshape(count, block, block, wide)

    diag_block, lower, upper, west, east, pivot = map(
        flat, (diag_block, lower, upper, west, east, pivot_inverse)
    )
    line = lax.axis_size("line")
    devices = line * lax.axis_size("patch")
    basis = [newton_residual.reshape(count, block, wide)]
    directions = []
    last = None
    short = line == 4 and count == 2
    for j in range(ITERS):
        blocks = lower, upper, pivot
        if j == 0 or not short:
            products = Products(basis[0], *blocks) if short else None
            direction, coupled, below = precondition(basis[j], last, *blocks, products)
        else:
            direction, coupled, below = short_precondition(
                basis[j], last, *blocks, products.near, products.far
            )
        if below is not None:
            basis[j] = basis[j].at[0].add(single_apply(lower[0], below))
        directions.append(direction)
        before, after = rows_beside(direction, across)
        last = direction[-1]
        image = coupled - basis[j] + block_apply(diag_block, direction)
        inner = [single_apply(lower[k], direction[k - 1]) for k in range(1, count)]
        if j == ITERS - 1:
            below = lax.ppermute(last, "line", [(i, i + 1) for i in range(line - 1)])
            inner = [single_apply(lower[0], below)] + inner
        else:
            inner = [jnp.zeros_like(last)] + inner
        image = image + jnp.stack(inner)
        image = image + block_apply(west, before) + block_apply(east, after)
        basis.append(image)
    sums = pl.pallas_call(
        gram_kernel,
        out_shape=jax.ShapeDtypeStruct((devices, 128), jnp.float32),
    )(*[member.reshape(count * block, wide) for member in basis])
    sums = lax.all_to_all(sums, ("line", "patch"), 0, 0, tiled=True)
    step = pl.pallas_call(
        finish_kernel,
        out_shape=jax.ShapeDtypeStruct((count * block, wide), jnp.float32),
    )(sums, *[direction.reshape(count * block, wide) for direction in directions])
    return step.reshape(shape)


def solution(mesh):
    blocks = P("line", None, None, "patch", None)
    field = P("line", None, "patch", None)
    return jax.shard_map(
        per_device, mesh=mesh, in_specs=(field,) + (blocks,) * 6, out_specs=field, check_vma=False
    )
```

```python
import functools

import jax
import jax.numpy as jnp
from jax import lax
from jax.experimental import pallas as pl
from jax.experimental.pallas import tpu as pltpu
from jax.sharding import PartitionSpec as P

ITERS = 4


def single_apply(block_mat, vector):
    return jnp.sum(block_mat.astype(jnp.float32) * vector[None], axis=1)


def block_apply(block_mat, vector):
    return jnp.sum(block_mat.astype(jnp.float32) * vector[:, None], axis=2)


def sweep_down(vector, lower, pivot, entry):
    forward = [single_apply(pivot[0], vector[0] + single_apply(lower[0], entry))]
    for k in range(1, vector.shape[0]):
        forward.append(single_apply(pivot[k], vector[k] - single_apply(lower[k], forward[-1])))
    return forward


def sweep_up(forward, upper, pivot, incoming):
    count = len(forward)
    following = incoming
    result = [None] * count
    coupled = [None] * count
    for k in reversed(range(count)):
        coupled[k] = single_apply(upper[k], following)
        following = forward[k] - single_apply(pivot[k], coupled[k])
        result[k] = following
    return result, coupled


def down_entry(message):
    return -message[0] if message.shape[0] == 1 else message[1] - message[0]


def precondition(vector, last, lower, upper, pivot, products, step):
    count = lax.axis_size("line")
    incoming = jnp.zeros((1 if last is None else 2,) + vector.shape[1:], vector.dtype)
    for turn in range(count - 1):
        outgoing = sweep_down(vector, lower, pivot, down_entry(incoming))[-1]
        if products is not None and step == 0:
            outgoing = products.down(turn, outgoing)
        if products is not None and step == 1:
            outgoing = products.send(turn + count - 1, outgoing)
        message = outgoing[None] if last is None else jnp.stack([outgoing, last])
        incoming = incoming + lax.ppermute(message, "line", [(turn, turn + 1)])
    forward = sweep_down(vector, lower, pivot, down_entry(incoming))
    below = None if last is None else incoming[1]
    incoming = jnp.zeros_like(vector[0])
    if products is not None and step > 0:
        near, far = products.received()
        outgoing = sweep_up(forward, upper, pivot, incoming)[0][0]
        two = lax.ppermute(outgoing, "line", [(3, 0), (2, 1)])
        side = lax.ppermute(outgoing, "line", [(2, 0), (3, 1)])
        one = lax.ppermute(outgoing, "line", [(3, 2), (1, 0)])
        passed = single_apply(near, side + single_apply(far, two))
        incoming = one + jnp.where(lax.axis_index("line") == 1, two, 0.0) + passed
    else:
        for turn in range(count - 1):
            outgoing = sweep_up(forward, upper, pivot, incoming)[0][0]
            if products is not None:
                outgoing = products.up(turn, outgoing)
            pair = (count - 1 - turn, count - 2 - turn)
            incoming = incoming + lax.ppermute(outgoing, "line", [pair])
    result, coupled = sweep_up(forward, upper, pivot, incoming)
    return jnp.stack(result), jnp.stack(coupled), below


def multiply_lines(left, right, out):
    block = right.shape[0]
    group = max(g for g in (1, 2, 3, 4) if block % g == 0)
    unroll = max(u for u in (1, 2, 4, 8) if block % u == 0)

    def rows(step, carry):
        start = step * group

        def add(j, totals):
            row = right[j]
            return tuple(
                total + left[start + q, pl.ds(j, 1), :] * row for q, total in enumerate(totals)
            )

        zero = jnp.zeros(right.shape[1:], jnp.float32)
        totals = lax.fori_loop(0, block, add, (zero,) * group, unroll=unroll)
        for q, total in enumerate(totals):
            out[start + q] = total
        return carry

    lax.fori_loop(0, block // group, rows, 0)


def among(devices):
    me = lax.axis_index("line")
    here = me == devices[0]
    for other in devices[1:]:
        here = here | (me == other)
    return here


def fetch(sources, targets, sem):
    copies = [
        pltpu.make_async_copy(source, target, sem.at[place])
        for place, (source, target) in enumerate(zip(sources, targets))
    ]
    for copy in copies:
        copy.start()
    for copy in copies:
        copy.wait()


def widen(source, target):
    def row(i, carry):
        target[i] = source[i].astype(jnp.float32)
        return carry

    lax.fori_loop(0, target.shape[0], row, 0, unroll=4)


def factor(k, upper, pivot, held, left, right, made, sem):
    fetch((pivot.at[k], upper.at[k]), (held.at[0], held.at[1]), sem)
    widen(held.at[0], left)
    widen(held.at[1], right)
    multiply_lines(left, right, made)


def factor_kernel(k, devices, upper, pivot, after, out, held, left, right, made, sem):
    @pl.when(among(devices))
    def _():
        factor(k, upper, pivot, held, left, right, made, sem)
        fetch((made,), (out,), sem)


def product_kernel(made_here, given, upper, pivot, first, second, after, *rest):
    *pieces, held, left, right, made, sem = rest

    def deliver(source):
        start = 0
        copies = []
        for piece in pieces:
            rows = pl.ds(start, piece.shape[0])
            copies.append(pltpu.make_async_copy(source.at[rows], piece, sem.at[0]))
            start += piece.shape[0]
        for copy in copies:
            copy.start()
            copy.wait()

    @pl.when(among((made_here,)))
    def _():
        factor(0, upper, pivot, held, left, right, made, sem)
        fetch((second,), (right,), sem)
        multiply_lines(made, right, left)
        deliver(left)

    @pl.when(among((given,)))
    def _():
        fetch((first, second), (left, right), sem)
        multiply_lines(left, right, made)
        deliver(made)


def lines_call(kernel, pieces, upper, *operands):
    shape = upper.shape[1:]
    bounds = [shape[0] * piece // pieces for piece in range(pieces + 1)]
    anywhere = pl.BlockSpec(memory_space=pl.ANY)
    return pl.pallas_call(
        kernel,
        out_shape=[
            jax.ShapeDtypeStruct((end - start,) + shape[1:], jnp.float32)
            for start, end in zip(bounds, bounds[1:])
        ],
        in_specs=[anywhere] * (1 + len(operands)),
        out_specs=[anywhere] * pieces,
        scratch_shapes=[pltpu.VMEM((2,) + shape, upper.dtype)]
        + [pltpu.VMEM(shape, jnp.float32)] * 3
        + [pltpu.SemaphoreType.DMA((2,))],
        compiler_params=pltpu.CompilerParams(vmem_limit_bytes=12 << 20),
    )(upper, *operands)


class Products:
    pieces = 6

    def __init__(self, upper, pivot):
        self.blocks = upper, pivot
        self.sent = []

    def down(self, turn, outgoing):
        def call(kernel, pieces, *operands):
            return lines_call(kernel, pieces, *self.blocks, *operands, outgoing)

        if turn == 0:
            (self.second,) = call(functools.partial(factor_kernel, 1, (1, 2)), 1)
            outgoing, self.second = lax.optimization_barrier((outgoing, self.second))
        if turn == 1:
            (self.first,) = call(functools.partial(factor_kernel, 0, (2,)), 1)
        if turn == 2:
            outgoing, self.first = lax.optimization_barrier((outgoing, self.first))
            kernel = functools.partial(product_kernel, 1, 2)
            self.made = call(kernel, self.pieces, self.first, self.second)
        return outgoing

    def up(self, turn, outgoing):
        if turn == 0:
            outgoing, *self.made = lax.optimization_barrier((outgoing, *self.made))
            return outgoing
        return self.send(turn - 1, outgoing)

    def send(self, place, value):
        if place >= self.pieces:
            return value
        value, piece = lax.optimization_barrier((value, self.made[place]))
        if place >= 2:
            value, *self.sent[place - 2] = lax.optimization_barrier((value, *self.sent[place - 2]))
        near = lax.ppermute(piece, "line", [(1, 0), (2, 1)])
        far = lax.ppermute(piece, "line", [(2, 0)])
        self.sent.append([near, far])
        return value

    def received(self):
        return [jnp.concatenate(pieces) for pieces in zip(*self.sent)]


def rows_beside(field, across):
    count = lax.axis_size("patch")
    even = [(i, i + 1) for i in range(0, count - 1, 2)]
    odd = [(i, i + 1) for i in range(1, count - 1, 2)]
    is_even = lax.axis_index("patch") % 2 == 0
    first, last = field[..., :across], field[..., -across:]
    several = field.shape[-1] > across
    to_far = jnp.where(is_even, first, last) if several else field
    to_near = jnp.where(is_even, last, first) if several else field
    far = lax.ppermute(to_far, "patch", odd + [(b, a) for a, b in odd])
    near = lax.ppermute(to_near, "patch", even + [(b, a) for a, b in even])
    before, after = jnp.where(is_even, far, near), jnp.where(is_even, near, far)
    if several:
        before = jnp.concatenate([before, field[..., :-across]], axis=-1)
        after = jnp.concatenate([field[..., across:], after], axis=-1)
    return before, after


def pairs_of(count):
    return [(i, j) for i in range(count) for j in range(i, count)]


def gram_kernel(*refs):
    ins, out = refs[:-1], refs[-1]
    lane = lax.broadcasted_iota(jnp.int32, (1, 128), 1)
    total = jnp.zeros((1, 128), jnp.float32)
    vectors = [ref[...] for ref in ins]
    for place, (i, j) in enumerate(pairs_of(len(vectors))):
        part = jnp.sum(vectors[i] * vectors[j], axis=0, keepdims=True)
        total = jnp.where(lane == place, jnp.sum(part, axis=1, keepdims=True), total)
    out[...] = jnp.broadcast_to(total, out.shape)


def finish_kernel(parts_ref, *refs):
    directions, out = refs[:-1], refs[-1]
    width = len(directions)
    total = jnp.sum(parts_ref[...], axis=0, keepdims=True)
    lane = lax.broadcasted_iota(jnp.int32, total.shape, 1)
    gram = {}
    for place, pair in enumerate(pairs_of(width + 1)):
        value = jnp.sum(jnp.where(lane == place, total, 0.0), axis=1, keepdims=True)
        gram[pair] = gram[pair[::-1]] = value
    half = [[gram[j + 1, i] + gram[j, i] for i in range(width + 1)] for j in range(width)]
    normal = [[half[j][i + 1] + half[j][i] for i in range(width)] for j in range(width)]
    right = [half[j][0] for j in range(width)]
    for i in range(width):
        inverse = 1.0 / normal[i][i]
        for j in range(i + 1, width):
            factor = normal[j][i] * inverse
            for k in range(i, width):
                normal[j][k] = normal[j][k] - factor * normal[i][k]
            right[j] = right[j] - factor * right[i]
    coeffs = [None] * width
    for i in reversed(range(width)):
        value = right[i]
        for k in range(i + 1, width):
            value = value - normal[i][k] * coeffs[k]
        coeffs[i] = value / normal[i][i]
    step = coeffs[0] * directions[0][...]
    for j in range(1, width):
        step = step + coeffs[j] * directions[j][...]
    out[...] = step


def per_device(newton_residual, diag_block, lower, upper, west, east, pivot_inverse):
    shape = newton_residual.shape
    count, block, rows, across = shape
    wide = rows * across

    def flat(matrix):
        return matrix.reshape(count, block, block, wide)

    diag_block, lower, upper, west, east, pivot = map(
        flat, (diag_block, lower, upper, west, east, pivot_inverse)
    )
    line = lax.axis_size("line")
    devices = line * lax.axis_size("patch")
    basis = [newton_residual.reshape(count, block, wide)]
    directions = []
    last = None
    products = Products(upper, pivot) if line == 4 and count == 2 else None
    for j in range(ITERS):
        direction, coupled, below = precondition(
            basis[j], last, lower, upper, pivot, products, j
        )
        if products is not None and j == 0:
            direction = products.send(2, direction)
        if below is not None:
            basis[j] = basis[j].at[0].add(single_apply(lower[0], below))
        directions.append(direction)
        before, after = rows_beside(direction, across)
        last = direction[-1]
        image = coupled - basis[j] + block_apply(diag_block, direction)
        inner = [single_apply(lower[k], direction[k - 1]) for k in range(1, count)]
        if j == ITERS - 1:
            below = lax.ppermute(last, "line", [(i, i + 1) for i in range(line - 1)])
            inner = [single_apply(lower[0], below)] + inner
        else:
            inner = [jnp.zeros_like(last)] + inner
        image = image + jnp.stack(inner)
        image = image + block_apply(west, before) + block_apply(east, after)
        basis.append(image)
    sums = pl.pallas_call(
        gram_kernel,
        out_shape=jax.ShapeDtypeStruct((devices, 128), jnp.float32),
    )(*[member.reshape(count * block, wide) for member in basis])
    sums = lax.all_to_all(sums, ("line", "patch"), 0, 0, tiled=True)
    step = pl.pallas_call(
        finish_kernel,
        out_shape=jax.ShapeDtypeStruct((count * block, wide), jnp.float32),
    )(sums, *[direction.reshape(count * block, wide) for direction in directions])
    return step.reshape(shape)


def solution(mesh):
    blocks = P("line", None, None, "patch", None)
    field = P("line", None, "patch", None)
    return jax.shard_map(
        per_device, mesh=mesh, in_specs=(field,) + (blocks,) * 6, out_specs=field, check_vma=False
    )
```

```python
import functools

import jax
import jax.numpy as jnp
from jax import lax
from jax.experimental import pallas as pl
from jax.experimental.pallas import tpu as pltpu
from jax.sharding import PartitionSpec as P

ITERS = 4


def single_apply(block_mat, vector):
    return jnp.sum(block_mat.astype(jnp.float32) * vector[None], axis=1)


def block_apply(block_mat, vector):
    return jnp.sum(block_mat.astype(jnp.float32) * vector[:, None], axis=2)


def sweep_down(vector, lower, pivot, entry):
    forward = [single_apply(pivot[0], vector[0] + single_apply(lower[0], entry))]
    for k in range(1, vector.shape[0]):
        forward.append(single_apply(pivot[k], vector[k] - single_apply(lower[k], forward[-1])))
    return forward


def sweep_up(forward, upper, pivot, incoming):
    count = len(forward)
    following = incoming
    result = [None] * count
    coupled = [None] * count
    for k in reversed(range(count)):
        coupled[k] = single_apply(upper[k], following)
        following = forward[k] - single_apply(pivot[k], coupled[k])
        result[k] = following
    return result, coupled


def down_entry(message):
    return -message[0] if message.shape[0] == 1 else message[1] - message[0]


def carry_down(vector, last, lower, pivot, products=None):
    count = lax.axis_size("line")
    incoming = jnp.zeros((1 if last is None else 2,) + vector.shape[1:], vector.dtype)
    for turn in range(count - 1):
        outgoing = sweep_down(vector, lower, pivot, down_entry(incoming))[-1]
        if products is not None:
            outgoing = products.down(turn, outgoing)
        message = outgoing[None] if last is None else jnp.stack([outgoing, last])
        incoming = incoming + lax.ppermute(message, "line", [(turn, turn + 1)])
    return incoming


def carry_up(forward, upper, pivot, products=None):
    count = lax.axis_size("line")
    incoming = jnp.zeros_like(forward[0])
    for turn in range(count - 1):
        outgoing = sweep_up(forward, upper, pivot, incoming)[0][0]
        if products is not None:
            outgoing = products.up(turn, outgoing)
        pair = (count - 1 - turn, count - 2 - turn)
        incoming = incoming + lax.ppermute(outgoing, "line", [pair])
    return incoming


def carry_up_at_once(forward, upper, pivot, near, far):
    outgoing = sweep_up(forward, upper, pivot, jnp.zeros_like(forward[0]))[0][0]
    two = lax.ppermute(outgoing, "line", [(3, 0), (2, 1)])
    side = lax.ppermute(outgoing, "line", [(2, 0), (3, 1)])
    one = lax.ppermute(outgoing, "line", [(3, 2), (1, 0)])
    passed = single_apply(near, side + single_apply(far, two))
    return one + jnp.where(lax.axis_index("line") == 1, two, 0.0) + passed


def precondition(vector, last, lower, upper, pivot, products, step):
    if products is not None and step == 1:
        shape = (2,) + vector.shape[1:]
        incoming = lax.cond(
            lax.axis_index("patch") < lax.axis_size("patch"),
            carry_down,
            lambda *_: jnp.zeros(shape, vector.dtype),
            *(vector, last, lower, pivot),
        )
    else:
        incoming = carry_down(vector, last, lower, pivot, products if step == 0 else None)
    forward = sweep_down(vector, lower, pivot, down_entry(incoming))
    below = None if last is None else incoming[1]
    if products is not None and step > 0:
        incoming = carry_up_at_once(forward, upper, pivot, products.near, products.far)
    else:
        incoming = carry_up(forward, upper, pivot, products)
    result, coupled = sweep_up(forward, upper, pivot, incoming)
    return jnp.stack(result), jnp.stack(coupled), below


def multiply_lines(left, right, out):
    block = right.shape[0]
    group = max(g for g in (1, 2, 3, 4) if block % g == 0)
    unroll = max(u for u in (1, 2, 4, 8) if block % u == 0)

    def rows(step, carry):
        start = step * group

        def add(j, totals):
            row = right[j]
            return tuple(
                total + left[start + q, pl.ds(j, 1), :] * row for q, total in enumerate(totals)
            )

        zero = jnp.zeros(right.shape[1:], jnp.float32)
        totals = lax.fori_loop(0, block, add, (zero,) * group, unroll=unroll)
        for q, total in enumerate(totals):
            out[start + q] = total
        return carry

    lax.fori_loop(0, block // group, rows, 0)


def among(devices):
    me = lax.axis_index("line")
    here = me == devices[0]
    for other in devices[1:]:
        here = here | (me == other)
    return here


def fetch(sources, targets, sem):
    copies = [
        pltpu.make_async_copy(source, target, sem.at[place])
        for place, (source, target) in enumerate(zip(sources, targets))
    ]
    for copy in copies:
        copy.start()
    for copy in copies:
        copy.wait()


def widen(source, target):
    def row(i, carry):
        target[i] = source[i].astype(jnp.float32)
        return carry

    lax.fori_loop(0, target.shape[0], row, 0, unroll=4)


def factor(k, upper, pivot, held, left, right, made, sem):
    fetch((pivot.at[k], upper.at[k]), (held.at[0], held.at[1]), sem)
    widen(held.at[0], left)
    widen(held.at[1], right)
    multiply_lines(left, right, made)


def factor_kernel(k, devices, upper, pivot, after, out, held, left, right, made, sem):
    @pl.when(among(devices))
    def _():
        factor(k, upper, pivot, held, left, right, made, sem)
        fetch((made,), (out,), sem)


def whole_kernel(devices, upper, pivot, after, out, held, left, right, made, sem):
    @pl.when(among(devices))
    def _():
        factor(1, upper, pivot, held, left, right, made, sem)
        fetch((made,), (out,), sem)
        factor(0, upper, pivot, held, left, right, made, sem)
        fetch((out,), (right,), sem)
        multiply_lines(made, right, left)
        fetch((left,), (out,), sem)


def product_kernel(devices, upper, first, second, after, other, out, held, left, right, made, sem):
    @pl.when(among(devices))
    def _():
        fetch((first, second), (left, right), sem)
        multiply_lines(left, right, made)
        fetch((made,), (out,), sem)


def lines_call(kernel, upper, *operands, alias=None):
    shape = upper.shape[1:]
    anywhere = pl.BlockSpec(memory_space=pl.ANY)
    return pl.pallas_call(
        kernel,
        out_shape=jax.ShapeDtypeStruct(shape, jnp.float32),
        in_specs=[anywhere] * (1 + len(operands)),
        out_specs=anywhere,
        scratch_shapes=[pltpu.VMEM((2,) + shape, upper.dtype)]
        + [pltpu.VMEM(shape, jnp.float32)] * 3
        + [pltpu.SemaphoreType.DMA((2,))],
        input_output_aliases={} if alias is None else {alias: 0},
        compiler_params=pltpu.CompilerParams(vmem_limit_bytes=12 << 20),
    )(upper, *operands)


class Products:
    def __init__(self, upper, pivot):
        self.upper, self.pivot = upper, pivot

    def down(self, turn, outgoing):
        def call(kernel, *leading):
            return lines_call(
                functools.partial(kernel, *leading), self.upper, self.pivot, outgoing
            )

        if turn == 0:
            self.second = call(factor_kernel, 1, (2,))
            outgoing, self.second = lax.optimization_barrier((outgoing, self.second))
        if turn == 1:
            self.first = call(factor_kernel, 0, (2,))
        if turn == 2:
            outgoing, self.first = lax.optimization_barrier((outgoing, self.first))
            self.made = call(whole_kernel, (1,))
        return outgoing

    def up(self, turn, outgoing):
        if turn == 0:
            outgoing, self.made = lax.optimization_barrier((outgoing, self.made))
        if turn == 1:
            kernel = functools.partial(product_kernel, (2,))
            self.made = lines_call(
                kernel, self.upper, self.first, self.second, outgoing, self.made, alias=4
            )
        if turn == 2:
            outgoing, self.made = lax.optimization_barrier((outgoing, self.made))
        return outgoing

    def send(self, direction):
        direction, made = lax.optimization_barrier((direction, self.made))
        self.near = lax.ppermute(made, "line", [(1, 0), (2, 1)])
        self.far = lax.ppermute(made, "line", [(2, 0)])
        return direction


def rows_beside(field, across):
    count = lax.axis_size("patch")
    even = [(i, i + 1) for i in range(0, count - 1, 2)]
    odd = [(i, i + 1) for i in range(1, count - 1, 2)]
    is_even = lax.axis_index("patch") % 2 == 0
    first, last = field[..., :across], field[..., -across:]
    several = field.shape[-1] > across
    to_far = jnp.where(is_even, first, last) if several else field
    to_near = jnp.where(is_even, last, first) if several else field
    far = lax.ppermute(to_far, "patch", odd + [(b, a) for a, b in odd])
    near = lax.ppermute(to_near, "patch", even + [(b, a) for a, b in even])
    before, after = jnp.where(is_even, far, near), jnp.where(is_even, near, far)
    if several:
        before = jnp.concatenate([before, field[..., :-across]], axis=-1)
        after = jnp.concatenate([field[..., across:], after], axis=-1)
    return before, after


def pairs_of(count):
    return [(i, j) for i in range(count) for j in range(i, count)]


def gram_kernel(*refs):
    ins, out = refs[:-1], refs[-1]
    lane = lax.broadcasted_iota(jnp.int32, (1, 128), 1)
    total = jnp.zeros((1, 128), jnp.float32)
    vectors = [ref[...] for ref in ins]
    for place, (i, j) in enumerate(pairs_of(len(vectors))):
        part = jnp.sum(vectors[i] * vectors[j], axis=0, keepdims=True)
        total = jnp.where(lane == place, jnp.sum(part, axis=1, keepdims=True), total)
    out[...] = jnp.broadcast_to(total, out.shape)


def finish_kernel(parts_ref, *refs):
    directions, out = refs[:-1], refs[-1]
    width = len(directions)
    total = jnp.sum(parts_ref[...], axis=0, keepdims=True)
    lane = lax.broadcasted_iota(jnp.int32, total.shape, 1)
    gram = {}
    for place, pair in enumerate(pairs_of(width + 1)):
        value = jnp.sum(jnp.where(lane == place, total, 0.0), axis=1, keepdims=True)
        gram[pair] = gram[pair[::-1]] = value
    half = [[gram[j + 1, i] + gram[j, i] for i in range(width + 1)] for j in range(width)]
    normal = [[half[j][i + 1] + half[j][i] for i in range(width)] for j in range(width)]
    right = [half[j][0] for j in range(width)]
    for i in range(width):
        inverse = 1.0 / normal[i][i]
        for j in range(i + 1, width):
            factor = normal[j][i] * inverse
            for k in range(i, width):
                normal[j][k] = normal[j][k] - factor * normal[i][k]
            right[j] = right[j] - factor * right[i]
    coeffs = [None] * width
    for i in reversed(range(width)):
        value = right[i]
        for k in range(i + 1, width):
            value = value - normal[i][k] * coeffs[k]
        coeffs[i] = value / normal[i][i]
    step = coeffs[0] * directions[0][...]
    for j in range(1, width):
        step = step + coeffs[j] * directions[j][...]
    out[...] = step


def per_device(newton_residual, diag_block, lower, upper, west, east, pivot_inverse):
    shape = newton_residual.shape
    count, block, rows, across = shape
    wide = rows * across

    def flat(matrix):
        return matrix.reshape(count, block, block, wide)

    diag_block, lower, upper, west, east, pivot = map(
        flat, (diag_block, lower, upper, west, east, pivot_inverse)
    )
    line = lax.axis_size("line")
    devices = line * lax.axis_size("patch")
    basis = [newton_residual.reshape(count, block, wide)]
    directions = []
    last = None
    products = Products(upper, pivot) if line == 4 and count == 2 else None
    for j in range(ITERS):
        direction, coupled, below = precondition(
            basis[j], last, lower, upper, pivot, products, j
        )
        if products is not None and j == 0:
            direction = products.send(direction)
        if below is not None:
            basis[j] = basis[j].at[0].add(single_apply(lower[0], below))
        directions.append(direction)
        before, after = rows_beside(direction, across)
        last = direction[-1]
        image = coupled - basis[j] + block_apply(diag_block, direction)
        inner = [single_apply(lower[k], direction[k - 1]) for k in range(1, count)]
        if j == ITERS - 1:
            below = lax.ppermute(last, "line", [(i, i + 1) for i in range(line - 1)])
            inner = [single_apply(lower[0], below)] + inner
        else:
            inner = [jnp.zeros_like(last)] + inner
        image = image + jnp.stack(inner)
        image = image + block_apply(west, before) + block_apply(east, after)
        basis.append(image)
    sums = pl.pallas_call(
        gram_kernel,
        out_shape=jax.ShapeDtypeStruct((devices, 128), jnp.float32),
    )(*[member.reshape(count * block, wide) for member in basis])
    sums = lax.all_to_all(sums, ("line", "patch"), 0, 0, tiled=True)
    step = pl.pallas_call(
        finish_kernel,
        out_shape=jax.ShapeDtypeStruct((count * block, wide), jnp.float32),
    )(sums, *[direction.reshape(count * block, wide) for direction in directions])
    return step.reshape(shape)


def solution(mesh):
    blocks = P("line", None, None, "patch", None)
    field = P("line", None, "patch", None)
    return jax.shard_map(
        per_device, mesh=mesh, in_specs=(field,) + (blocks,) * 6, out_specs=field, check_vma=False
    )
```

```python
import functools

import jax
import jax.numpy as jnp
from jax import lax
from jax.experimental import pallas as pl
from jax.experimental.pallas import tpu as pltpu
from jax.sharding import PartitionSpec as P

ITERS = 4


def single_apply(block_mat, vector):
    return jnp.sum(block_mat.astype(jnp.float32) * vector[None], axis=1)


def block_apply(block_mat, vector):
    return jnp.sum(block_mat.astype(jnp.float32) * vector[:, None], axis=2)


def sweep_down(vector, lower, pivot, entry):
    forward = [single_apply(pivot[0], vector[0] + single_apply(lower[0], entry))]
    for k in range(1, vector.shape[0]):
        forward.append(single_apply(pivot[k], vector[k] - single_apply(lower[k], forward[-1])))
    return forward


def sweep_up(forward, upper, pivot, incoming):
    count = len(forward)
    following = incoming
    result = [None] * count
    coupled = [None] * count
    for k in reversed(range(count)):
        coupled[k] = single_apply(upper[k], following)
        following = forward[k] - single_apply(pivot[k], coupled[k])
        result[k] = following
    return result, coupled


def down_entry(message):
    return -message[0] if message.shape[0] == 1 else message[1] - message[0]


def precondition(vector, last, lower, upper, pivot, turning):
    count = lax.axis_size("line")
    incoming = jnp.zeros((1 if last is None else 2,) + vector.shape[1:], vector.dtype)
    for turn in range(count - 1):
        outgoing = sweep_down(vector, lower, pivot, down_entry(incoming))[-1]
        if turning is not None:
            outgoing = turning.down(turn, outgoing)
        message = outgoing[None] if last is None else jnp.stack([outgoing, last])
        incoming = incoming + lax.ppermute(message, "line", [(turn, turn + 1)])
    forward = sweep_down(vector, lower, pivot, down_entry(incoming))
    below = None if last is None else incoming[1]
    incoming = jnp.zeros_like(vector[0])
    for turn in range(count - 1):
        outgoing = sweep_up(forward, upper, pivot, incoming)[0][0]
        if turning is not None:
            outgoing = turning.up(turn, outgoing)
        pair = (count - 1 - turn, count - 2 - turn)
        incoming = incoming + lax.ppermute(outgoing, "line", [pair])
    result, coupled = sweep_up(forward, upper, pivot, incoming)
    return jnp.stack(result), jnp.stack(coupled), below


def short_precondition(vector, last, lower, upper, pivot, turning):
    count = lax.axis_size("line")
    nothing = jnp.zeros_like(last)
    incoming = jnp.zeros((2,) + vector.shape[1:], vector.dtype)
    turned = nothing
    for turn in range(count - 2):
        forward = sweep_down(vector, lower, pivot, down_entry(incoming))
        outgoing = forward[-1]
        if turn == 0:
            outgoing = turning.settle(outgoing)
        message = jnp.stack([outgoing, last])
        incoming = incoming + lax.ppermute(message, "line", [(turn, turn + 1)])
        if turn == 0:
            alone = sweep_up(forward, upper, pivot, nothing)[0][0]
            turned = lax.ppermute(alone, "line", [(count - 1, count - 2)])
    forward = sweep_down(vector, lower, pivot, down_entry(incoming))
    message = jnp.stack([forward[-1], last])
    turned = turned + single_apply(turning.held, down_entry(message))
    upward = turned
    for turn in range(1, count - 1):
        outgoing = sweep_up(forward, upper, pivot, upward)[0][0]
        if turn == 1:
            outgoing, message = lax.optimization_barrier((outgoing, message))
        pair = (count - 1 - turn, count - 2 - turn)
        upward = upward + lax.ppermute(outgoing, "line", [pair])
        if turn == 1:
            incoming = incoming + lax.ppermute(message, "line", [(count - 2, count - 1)])
    forward = sweep_down(vector, lower, pivot, down_entry(incoming))
    result, coupled = sweep_up(forward, upper, pivot, upward)
    return jnp.stack(result), jnp.stack(coupled), incoming[1]


def multiply_lines(left, right, out):
    block = right.shape[0]
    group = max(g for g in (1, 2, 3, 4) if block % g == 0)
    unroll = max(u for u in (1, 2, 4, 8) if block % u == 0)

    def rows(step, carry):
        start = step * group

        def add(j, totals):
            row = right[j]
            return tuple(
                total + left[start + q, pl.ds(j, 1), :] * row for q, total in enumerate(totals)
            )

        zero = jnp.zeros(right.shape[1:], jnp.float32)
        totals = lax.fori_loop(0, block, add, (zero,) * group, unroll=unroll)
        for q, total in enumerate(totals):
            out[start + q] = total
        return carry

    lax.fori_loop(0, block // group, rows, 0)


def fetch(sources, targets, sem):
    copies = [
        pltpu.make_async_copy(source, target, sem.at[place])
        for place, (source, target) in enumerate(zip(sources, targets))
    ]
    for copy in copies:
        copy.start()
    for copy in copies:
        copy.wait()


def widen(source, target):
    def row(i, carry):
        target[i] = source[i].astype(jnp.float32)
        return carry

    lax.fori_loop(0, target.shape[0], row, 0, unroll=4)


def on_last(body):
    pl.when(lax.axis_index("line") == lax.axis_size("line") - 1)(body)


def first_kernel(lower, pivot, after, factor, out, held, left, right, made, sem):
    def body():
        fetch((pivot.at[0], lower.at[0]), (held.at[0], held.at[1]), sem)
        widen(held.at[0], left)
        widen(held.at[1], right)
        multiply_lines(left, right, made)
        fetch((made, lower.at[1]), (factor, held.at[0]), sem)
        widen(held.at[0], left)
        multiply_lines(left, made, right)
        fetch((right,), (out,), sem)

    on_last(body)


def second_kernel(pivot, given, after, out, held, left, right, made, sem):
    def body():
        fetch((pivot.at[1], given), (held.at[0], right), sem)
        widen(held.at[0], left)
        multiply_lines(left, right, made)
        fetch((made,), (out,), sem)

    on_last(body)


def third_kernel(upper, pivot, given, factor, after, out, held, left, right, made, sem):
    def body():
        fetch((upper.at[0], given), (held.at[0], right), sem)
        fetch((pivot.at[0],), (held.at[1],), sem)
        widen(held.at[0], left)
        multiply_lines(left, right, made)
        widen(held.at[1], left)
        multiply_lines(left, made, right)
        fetch((factor,), (made,), sem)

        def row(i, carry):
            right[i] = right[i] + made[i]
            return carry

        lax.fori_loop(0, right.shape[0], row, 0, unroll=4)
        fetch((right,), (out,), sem)

    on_last(body)


def lines_call(kernel, results, block, *operands):
    shape = block.shape[1:]
    anywhere = pl.BlockSpec(memory_space=pl.ANY)
    return pl.pallas_call(
        kernel,
        out_shape=[jax.ShapeDtypeStruct(shape, jnp.float32)] * results,
        in_specs=[anywhere] * (1 + len(operands)),
        out_specs=[anywhere] * results,
        scratch_shapes=[pltpu.VMEM((2,) + shape, block.dtype)]
        + [pltpu.VMEM(shape, jnp.float32)] * 3
        + [pltpu.SemaphoreType.DMA((2,))],
        compiler_params=pltpu.CompilerParams(vmem_limit_bytes=12 << 20),
    )(block, *operands)


class Turning:
    def __init__(self, lower, upper, pivot):
        self.lower, self.upper, self.pivot = lower, upper, pivot

    def down(self, turn, outgoing):
        end = lax.axis_size("line") - 2
        if turn == 0:
            self.factor, self.made = lines_call(first_kernel, 2, self.lower, self.pivot, outgoing)
        if turn == min(1, end):
            outgoing, self.made = lax.optimization_barrier((outgoing, self.made))
        if turn == end:
            (self.made,) = lines_call(second_kernel, 1, self.pivot, self.made, outgoing)
        return outgoing

    def up(self, turn, outgoing):
        end = lax.axis_size("line") - 2
        if turn == 0:
            outgoing, self.made = lax.optimization_barrier((outgoing, self.made))
            (self.made,) = lines_call(
                third_kernel, 1, self.upper, self.pivot, self.made, self.factor, outgoing
            )
        if turn == end:
            outgoing, self.made = lax.optimization_barrier((outgoing, self.made))
        return outgoing

    def send(self, direction):
        direction, made = lax.optimization_barrier((direction, self.made))
        end = lax.axis_size("line") - 1
        self.held = lax.ppermute(made, "line", [(end, end - 1)])
        return direction

    def settle(self, outgoing):
        if not hasattr(self, "settled"):
            outgoing, self.held = lax.optimization_barrier((outgoing, self.held))
            self.settled = True
        return outgoing


def rows_beside(field, across):
    count = lax.axis_size("patch")
    even = [(i, i + 1) for i in range(0, count - 1, 2)]
    odd = [(i, i + 1) for i in range(1, count - 1, 2)]
    is_even = lax.axis_index("patch") % 2 == 0
    first, last = field[..., :across], field[..., -across:]
    several = field.shape[-1] > across
    to_far = jnp.where(is_even, first, last) if several else field
    to_near = jnp.where(is_even, last, first) if several else field
    far = lax.ppermute(to_far, "patch", odd + [(b, a) for a, b in odd])
    near = lax.ppermute(to_near, "patch", even + [(b, a) for a, b in even])
    before, after = jnp.where(is_even, far, near), jnp.where(is_even, near, far)
    if several:
        before = jnp.concatenate([before, field[..., :-across]], axis=-1)
        after = jnp.concatenate([field[..., across:], after], axis=-1)
    return before, after


def pairs_of(count):
    return [(i, j) for i in range(count) for j in range(i, count)]


def gram_kernel(*refs):
    ins, out = refs[:-1], refs[-1]
    lane = lax.broadcasted_iota(jnp.int32, (1, 128), 1)
    total = jnp.zeros((1, 128), jnp.float32)
    vectors = [ref[...] for ref in ins]
    for place, (i, j) in enumerate(pairs_of(len(vectors))):
        part = jnp.sum(vectors[i] * vectors[j], axis=0, keepdims=True)
        total = jnp.where(lane == place, jnp.sum(part, axis=1, keepdims=True), total)
    out[...] = jnp.broadcast_to(total, out.shape)


def finish_kernel(parts_ref, *refs):
    directions, out = refs[:-1], refs[-1]
    width = len(directions)
    total = jnp.sum(parts_ref[...], axis=0, keepdims=True)
    lane = lax.broadcasted_iota(jnp.int32, total.shape, 1)
    gram = {}
    for place, pair in enumerate(pairs_of(width + 1)):
        value = jnp.sum(jnp.where(lane == place, total, 0.0), axis=1, keepdims=True)
        gram[pair] = gram[pair[::-1]] = value
    half = [[gram[j + 1, i] + gram[j, i] for i in range(width + 1)] for j in range(width)]
    normal = [[half[j][i + 1] + half[j][i] for i in range(width)] for j in range(width)]
    right = [half[j][0] for j in range(width)]
    for i in range(width):
        inverse = 1.0 / normal[i][i]
        for j in range(i + 1, width):
            factor = normal[j][i] * inverse
            for k in range(i, width):
                normal[j][k] = normal[j][k] - factor * normal[i][k]
            right[j] = right[j] - factor * right[i]
    coeffs = [None] * width
    for i in reversed(range(width)):
        value = right[i]
        for k in range(i + 1, width):
            value = value - normal[i][k] * coeffs[k]
        coeffs[i] = value / normal[i][i]
    step = coeffs[0] * directions[0][...]
    for j in range(1, width):
        step = step + coeffs[j] * directions[j][...]
    out[...] = step


def per_device(newton_residual, diag_block, lower, upper, west, east, pivot_inverse):
    shape = newton_residual.shape
    count, block, rows, across = shape
    wide = rows * across

    def flat(matrix):
        return matrix.reshape(count, block, block, wide)

    diag_block, lower, upper, west, east, pivot = map(
        flat, (diag_block, lower, upper, west, east, pivot_inverse)
    )
    line = lax.axis_size("line")
    devices = line * lax.axis_size("patch")
    basis = [newton_residual.reshape(count, block, wide)]
    directions = []
    last = None
    turning = Turning(lower, upper, pivot) if line > 2 and count == 2 else None
    for j in range(ITERS):
        blocks = lower, upper, pivot
        if j == 0 or turning is None:
            direction, coupled, below = precondition(basis[j], last, *blocks, turning)
        else:
            direction, coupled, below = short_precondition(basis[j], last, *blocks, turning)
        if turning is not None and j == 0:
            direction = turning.send(direction)
        if below is not None:
            basis[j] = basis[j].at[0].add(single_apply(lower[0], below))
        directions.append(direction)
        before, after = rows_beside(direction, across)
        last = direction[-1]
        image = coupled - basis[j] + block_apply(diag_block, direction)
        inner = [single_apply(lower[k], direction[k - 1]) for k in range(1, count)]
        if j == ITERS - 1:
            below = lax.ppermute(last, "line", [(i, i + 1) for i in range(line - 1)])
            inner = [single_apply(lower[0], below)] + inner
        else:
            inner = [jnp.zeros_like(last)] + inner
        image = image + jnp.stack(inner)
        image = image + block_apply(west, before) + block_apply(east, after)
        basis.append(image)
    sums = pl.pallas_call(
        gram_kernel,
        out_shape=jax.ShapeDtypeStruct((devices, 128), jnp.float32),
    )(*[member.reshape(count * block, wide) for member in basis])
    sums = lax.all_to_all(sums, ("line", "patch"), 0, 0, tiled=True)
    step = pl.pallas_call(
        finish_kernel,
        out_shape=jax.ShapeDtypeStruct((count * block, wide), jnp.float32),
    )(sums, *[direction.reshape(count * block, wide) for direction in directions])
    return step.reshape(shape)


def solution(mesh):
    blocks = P("line", None, None, "patch", None)
    field = P("line", None, "patch", None)
    return jax.shard_map(
        per_device, mesh=mesh, in_specs=(field,) + (blocks,) * 6, out_specs=field, check_vma=False
    )
```

```python
import functools

import jax
import jax.numpy as jnp
from jax import lax
from jax.experimental import pallas as pl
from jax.experimental.pallas import tpu as pltpu
from jax.sharding import PartitionSpec as P

ITERS = 4


def single_apply(block_mat, vector):
    return jnp.sum(block_mat.astype(jnp.float32) * vector[None], axis=1)


def block_apply(block_mat, vector):
    return jnp.sum(block_mat.astype(jnp.float32) * vector[:, None], axis=2)


def sweep_down(vector, lower, pivot, entry):
    forward = [single_apply(pivot[0], vector[0] + single_apply(lower[0], entry))]
    for k in range(1, vector.shape[0]):
        forward.append(single_apply(pivot[k], vector[k] - single_apply(lower[k], forward[-1])))
    return forward


def sweep_up(forward, upper, pivot, incoming):
    count = len(forward)
    following = incoming
    result = [None] * count
    coupled = [None] * count
    for k in reversed(range(count)):
        coupled[k] = single_apply(upper[k], following)
        following = forward[k] - single_apply(pivot[k], coupled[k])
        result[k] = following
    return result, coupled


def down_entry(message):
    return -message[0] if message.shape[0] == 1 else message[1] - message[0]


def precondition(vector, last, lower, upper, pivot, turning, step):
    count = lax.axis_size("line")
    incoming = jnp.zeros((1 if last is None else 2,) + vector.shape[1:], vector.dtype)
    for turn in range(count - 1):
        outgoing = sweep_down(vector, lower, pivot, down_entry(incoming))[-1]
        if turning is not None:
            outgoing = turning.down(step, turn, outgoing)
        message = outgoing[None] if last is None else jnp.stack([outgoing, last])
        incoming = incoming + lax.ppermute(message, "line", [(turn, turn + 1)])
    forward = sweep_down(vector, lower, pivot, down_entry(incoming))
    below = None if last is None else incoming[1]
    incoming = jnp.zeros_like(vector[0])
    for turn in range(count - 1):
        outgoing = sweep_up(forward, upper, pivot, incoming)[0][0]
        if turning is not None:
            outgoing = turning.up(step, turn, outgoing)
        pair = (count - 1 - turn, count - 2 - turn)
        incoming = incoming + lax.ppermute(outgoing, "line", [pair])
    result, coupled = sweep_up(forward, upper, pivot, incoming)
    return jnp.stack(result), jnp.stack(coupled), below


def short_precondition(vector, last, lower, upper, pivot, turning):
    count = lax.axis_size("line")
    nothing = jnp.zeros_like(last)
    incoming = jnp.zeros((2,) + vector.shape[1:], vector.dtype)
    turned = nothing
    for turn in range(count - 2):
        forward = sweep_down(vector, lower, pivot, down_entry(incoming))
        outgoing = forward[-1]
        message = jnp.stack([outgoing, last])
        incoming = incoming + lax.ppermute(message, "line", [(turn, turn + 1)])
        if turn == 0:
            alone = sweep_up(forward, upper, pivot, nothing)[0][0]
            turned = lax.ppermute(alone, "line", [(count - 1, count - 2)])
    forward = sweep_down(vector, lower, pivot, down_entry(incoming))
    message = jnp.stack([forward[-1], last])
    turned = turned + single_apply(turning.held, down_entry(message))
    upward = turned
    for turn in range(1, count - 1):
        outgoing = sweep_up(forward, upper, pivot, upward)[0][0]
        if turn == 1:
            outgoing, message = lax.optimization_barrier((outgoing, message))
        pair = (count - 1 - turn, count - 2 - turn)
        upward = upward + lax.ppermute(outgoing, "line", [pair])
        if turn == 1:
            incoming = incoming + lax.ppermute(message, "line", [(count - 2, count - 1)])
    forward = sweep_down(vector, lower, pivot, down_entry(incoming))
    result, coupled = sweep_up(forward, upper, pivot, upward)
    return jnp.stack(result), jnp.stack(coupled), incoming[1]


def multiply_lines(left, right, out):
    block = right.shape[0]
    group = max(g for g in (1, 2, 3, 4) if block % g == 0)
    unroll = max(u for u in (1, 2, 4, 8) if block % u == 0)

    def rows(step, carry):
        start = step * group

        def add(j, totals):
            row = right[j]
            return tuple(
                total + left[start + q, pl.ds(j, 1), :] * row for q, total in enumerate(totals)
            )

        zero = jnp.zeros(right.shape[1:], jnp.float32)
        totals = lax.fori_loop(0, block, add, (zero,) * group, unroll=unroll)
        for q, total in enumerate(totals):
            out[start + q] = total
        return carry

    lax.fori_loop(0, block // group, rows, 0)


def fetch(sources, targets, sem):
    copies = [
        pltpu.make_async_copy(source, target, sem.at[place])
        for place, (source, target) in enumerate(zip(sources, targets))
    ]
    for copy in copies:
        copy.start()
    for copy in copies:
        copy.wait()


def widen(source, target):
    def row(i, carry):
        target[i] = source[i].astype(jnp.float32)
        return carry

    lax.fori_loop(0, target.shape[0], row, 0, unroll=4)


def on_last(body):
    pl.when(lax.axis_index("line") == lax.axis_size("line") - 1)(body)


def factor_kernel(lower, pivot, after, out, held, left, right, made, sem):
    def body():
        fetch((pivot.at[0], lower.at[0]), (held.at[0], held.at[1]), sem)
        widen(held.at[0], left)
        widen(held.at[1], right)
        multiply_lines(left, right, made)
        fetch((made,), (out,), sem)

    on_last(body)


def product_kernel(places, *refs):
    *blocks, given, after, out, held, left, right, made, sem = refs

    def body():
        fetch((given,), (right,), sem)
        source, target = right, made
        for block, place in zip(blocks, places):
            fetch((block.at[place],), (held.at[0],), sem)
            widen(held.at[0], left)
            multiply_lines(left, source, target)
            source, target = target, source
        fetch((source,), (out,), sem)

    on_last(body)


def sum_kernel(place, block, given, added, after, out, held, left, right, made, sem):
    def body():
        fetch((block.at[place], given), (held.at[0], right), sem)
        widen(held.at[0], left)
        multiply_lines(left, right, made)
        fetch((added,), (right,), sem)

        def row(i, carry):
            made[i] = made[i] + right[i]
            return carry

        lax.fori_loop(0, made.shape[0], row, 0, unroll=4)
        fetch((made,), (out,), sem)

    on_last(body)


def lines_call(kernel, block, *operands):
    shape = block.shape[1:]
    anywhere = pl.BlockSpec(memory_space=pl.ANY)
    return pl.pallas_call(
        kernel,
        out_shape=jax.ShapeDtypeStruct(shape, jnp.float32),
        in_specs=[anywhere] * (1 + len(operands)),
        out_specs=anywhere,
        scratch_shapes=[pltpu.VMEM((2,) + shape, block.dtype)]
        + [pltpu.VMEM(shape, jnp.float32)] * 3
        + [pltpu.SemaphoreType.DMA((2,))],
        compiler_params=pltpu.CompilerParams(vmem_limit_bytes=12 << 20),
    )(block, *operands)


def in_order(first, second):
    return lax.optimization_barrier((first, second))


class Turning:
    def __init__(self, lower, upper, pivot):
        self.lower, self.upper, self.pivot = lower, upper, pivot

    def down(self, step, turn, outgoing):
        end = lax.axis_size("line") - 2
        if step == 0 and turn == 0:
            self.factor = lines_call(factor_kernel, self.lower, self.pivot, outgoing)
        if step == 0 and turn == end:
            outgoing, self.factor = in_order(outgoing, self.factor)
            kernel = functools.partial(product_kernel, (1,))
            self.made = lines_call(kernel, self.lower, self.factor, outgoing)
        if step == 1 and turn == 0:
            outgoing, self.made = in_order(outgoing, self.made)
            kernel = functools.partial(sum_kernel, 0)
            self.made = lines_call(kernel, self.pivot, self.made, self.factor, outgoing)
        if step == 1 and turn == end:
            outgoing, self.made = in_order(outgoing, self.made)
        return outgoing

    def up(self, step, turn, outgoing):
        if step == 0 and turn == 0:
            outgoing, self.made = in_order(outgoing, self.made)
            kernel = functools.partial(product_kernel, (1, 0))
            self.made = lines_call(kernel, self.pivot, self.upper, self.made, outgoing)
        if step == 1 and turn == 1:
            outgoing, made = in_order(outgoing, self.made)
            end = lax.axis_size("line") - 1
            self.held = lax.ppermute(made, "line", [(end, end - 1)])
        return outgoing

    def settle(self, value):
        value, self.held = in_order(value, self.held)
        return value


def rows_beside(field, across):
    count = lax.axis_size("patch")
    even = [(i, i + 1) for i in range(0, count - 1, 2)]
    odd = [(i, i + 1) for i in range(1, count - 1, 2)]
    is_even = lax.axis_index("patch") % 2 == 0
    first, last = field[..., :across], field[..., -across:]
    several = field.shape[-1] > across
    to_far = jnp.where(is_even, first, last) if several else field
    to_near = jnp.where(is_even, last, first) if several else field
    far = lax.ppermute(to_far, "patch", odd + [(b, a) for a, b in odd])
    near = lax.ppermute(to_near, "patch", even + [(b, a) for a, b in even])
    before, after = jnp.where(is_even, far, near), jnp.where(is_even, near, far)
    if several:
        before = jnp.concatenate([before, field[..., :-across]], axis=-1)
        after = jnp.concatenate([field[..., across:], after], axis=-1)
    return before, after


def pairs_of(count):
    return [(i, j) for i in range(count) for j in range(i, count)]


def gram_kernel(*refs):
    ins, out = refs[:-1], refs[-1]
    lane = lax.broadcasted_iota(jnp.int32, (1, 128), 1)
    total = jnp.zeros((1, 128), jnp.float32)
    vectors = [ref[...] for ref in ins]
    for place, (i, j) in enumerate(pairs_of(len(vectors))):
        part = jnp.sum(vectors[i] * vectors[j], axis=0, keepdims=True)
        total = jnp.where(lane == place, jnp.sum(part, axis=1, keepdims=True), total)
    out[...] = jnp.broadcast_to(total, out.shape)


def finish_kernel(parts_ref, *refs):
    directions, out = refs[:-1], refs[-1]
    width = len(directions)
    total = jnp.sum(parts_ref[...], axis=0, keepdims=True)
    lane = lax.broadcasted_iota(jnp.int32, total.shape, 1)
    gram = {}
    for place, pair in enumerate(pairs_of(width + 1)):
        value = jnp.sum(jnp.where(lane == place, total, 0.0), axis=1, keepdims=True)
        gram[pair] = gram[pair[::-1]] = value
    half = [[gram[j + 1, i] + gram[j, i] for i in range(width + 1)] for j in range(width)]
    normal = [[half[j][i + 1] + half[j][i] for i in range(width)] for j in range(width)]
    right = [half[j][0] for j in range(width)]
    for i in range(width):
        inverse = 1.0 / normal[i][i]
        for j in range(i + 1, width):
            factor = normal[j][i] * inverse
            for k in range(i, width):
                normal[j][k] = normal[j][k] - factor * normal[i][k]
            right[j] = right[j] - factor * right[i]
    coeffs = [None] * width
    for i in reversed(range(width)):
        value = right[i]
        for k in range(i + 1, width):
            value = value - normal[i][k] * coeffs[k]
        coeffs[i] = value / normal[i][i]
    step = coeffs[0] * directions[0][...]
    for j in range(1, width):
        step = step + coeffs[j] * directions[j][...]
    out[...] = step


def per_device(newton_residual, diag_block, lower, upper, west, east, pivot_inverse):
    shape = newton_residual.shape
    count, block, rows, across = shape
    wide = rows * across

    def flat(matrix):
        return matrix.reshape(count, block, block, wide)

    diag_block, lower, upper, west, east, pivot = map(
        flat, (diag_block, lower, upper, west, east, pivot_inverse)
    )
    line = lax.axis_size("line")
    devices = line * lax.axis_size("patch")
    basis = [newton_residual.reshape(count, block, wide)]
    directions = []
    last = None
    turning = Turning(lower, upper, pivot) if line > 2 and count == 2 else None
    for j in range(ITERS):
        blocks = lower, upper, pivot
        if j < 2 or turning is None:
            direction, coupled, below = precondition(basis[j], last, *blocks, turning, j)
        else:
            direction, coupled, below = short_precondition(basis[j], last, *blocks, turning)
        if below is not None:
            basis[j] = basis[j].at[0].add(single_apply(lower[0], below))
        directions.append(direction)
        before, after = rows_beside(direction, across)
        if turning is not None and j == 1:
            before = turning.settle(before)
        last = direction[-1]
        image = coupled - basis[j] + block_apply(diag_block, direction)
        inner = [single_apply(lower[k], direction[k - 1]) for k in range(1, count)]
        if j == ITERS - 1:
            below = lax.ppermute(last, "line", [(i, i + 1) for i in range(line - 1)])
            inner = [single_apply(lower[0], below)] + inner
        else:
            inner = [jnp.zeros_like(last)] + inner
        image = image + jnp.stack(inner)
        image = image + block_apply(west, before) + block_apply(east, after)
        basis.append(image)
    sums = pl.pallas_call(
        gram_kernel,
        out_shape=jax.ShapeDtypeStruct((devices, 128), jnp.float32),
    )(*[member.reshape(count * block, wide) for member in basis])
    sums = lax.all_to_all(sums, ("line", "patch"), 0, 0, tiled=True)
    step = pl.pallas_call(
        finish_kernel,
        out_shape=jax.ShapeDtypeStruct((count * block, wide), jnp.float32),
    )(sums, *[direction.reshape(count * block, wide) for direction in directions])
    return step.reshape(shape)


def solution(mesh):
    blocks = P("line", None, None, "patch", None)
    field = P("line", None, "patch", None)
    return jax.shard_map(
        per_device, mesh=mesh, in_specs=(field,) + (blocks,) * 6, out_specs=field, check_vma=False
    )
```

```python
import functools

import jax
import jax.numpy as jnp
from jax import lax
from jax.experimental import pallas as pl
from jax.experimental.pallas import tpu as pltpu
from jax.sharding import PartitionSpec as P

ITERS = 4
SUMS = 16


def single_apply(block_mat, vector):
    return jnp.sum(block_mat.astype(jnp.float32) * vector[None], axis=1)


def block_apply(block_mat, vector):
    return jnp.sum(block_mat.astype(jnp.float32) * vector[:, None], axis=2)


def sweep_down(vector, lower, pivot, entry):
    forward = [single_apply(pivot[0], vector[0] + single_apply(lower[0], entry))]
    for k in range(1, vector.shape[0]):
        forward.append(single_apply(pivot[k], vector[k] - single_apply(lower[k], forward[-1])))
    return forward


def sweep_up(forward, upper, pivot, incoming):
    count = len(forward)
    following = incoming
    result = [None] * count
    coupled = [None] * count
    for k in reversed(range(count)):
        coupled[k] = single_apply(upper[k], following)
        following = forward[k] - single_apply(pivot[k], coupled[k])
        result[k] = following
    return result, coupled


def first_kernel(vector, lower, pivot, out, field, held, middle, sems):
    count, block = vector.shape[:2]
    blocks = [pivot.at[0]]
    for k in range(1, count):
        blocks += [lower.at[k], pivot.at[k]]
    copies = [pltpu.make_async_copy(vector, field, sems.at[0])]
    for place, source in enumerate(blocks):
        copies.append(pltpu.make_async_copy(source, held.at[place], sems.at[1 + place]))
    for copy in copies:
        copy.start()
    rows = 16 if block % 16 == 0 else block

    def apply(place, value, target):
        for start in range(0, block, rows):
            part = held[place, start : start + rows].astype(jnp.float32)
            target[start : start + rows] = jnp.sum(part * value[None], axis=1)

    copies[0].wait()
    copies[1].wait()
    apply(0, field[0], middle)
    for k in range(1, count):
        copies[2 * k].wait()
        apply(2 * k - 1, middle[...], out)
        value = field[k] - out[...]
        copies[2 * k + 1].wait()
        apply(2 * k, value, out)
        if k < count - 1:
            middle[...] = out[...]
    if count == 1:
        out[...] = middle[...]


def first_carry(vector, lower, pivot):
    count, block, wide = vector.shape
    blocks = 2 * count - 1
    return pl.pallas_call(
        first_kernel,
        out_shape=jax.ShapeDtypeStruct((block, wide), jnp.float32),
        in_specs=[pl.BlockSpec(memory_space=pl.ANY)] * 3,
        scratch_shapes=[
            pltpu.VMEM(vector.shape, jnp.float32),
            pltpu.VMEM((blocks,) + lower.shape[1:], lower.dtype),
            pltpu.VMEM((block, wide), jnp.float32),
            pltpu.SemaphoreType.DMA((1 + blocks,)),
        ],
        compiler_params=pltpu.CompilerParams(vmem_limit_bytes=8 << 20),
    )(vector, lower, pivot)


def precondition(vector, last, lower, upper, pivot):
    count = lax.axis_size("line")
    incoming = jnp.zeros((1 if last is None else 2,) + vector.shape[1:], vector.dtype)

    def entry():
        return -incoming[0] if last is None else incoming[1] - incoming[0]

    for turn in range(count - 1):
        if last is None and turn == 0:
            outgoing = first_carry(vector, lower, pivot)
        else:
            outgoing = sweep_down(vector, lower, pivot, entry())[-1]
        message = outgoing[None] if last is None else jnp.stack([outgoing, last])
        incoming = incoming + lax.ppermute(message, "line", [(turn, turn + 1)])
    forward = sweep_down(vector, lower, pivot, entry())
    below = None if last is None else incoming[1]
    incoming = jnp.zeros_like(vector[0])
    for turn in reversed(range(count - 1)):
        outgoing = sweep_up(forward, upper, pivot, incoming)[0][0]
        incoming = incoming + lax.ppermute(outgoing, "line", [(turn + 1, turn)])
    result, coupled = sweep_up(forward, upper, pivot, incoming)
    return jnp.stack(result), jnp.stack(coupled), below


def rows_beside(field, across):
    count = lax.axis_size("patch")
    even = [(i, i + 1) for i in range(0, count - 1, 2)]
    odd = [(i, i + 1) for i in range(1, count - 1, 2)]
    is_even = lax.axis_index("patch") % 2 == 0
    first, last = field[..., :across], field[..., -across:]
    several = field.shape[-1] > across
    to_far = jnp.where(is_even, first, last) if several else field
    to_near = jnp.where(is_even, last, first) if several else field
    far = lax.ppermute(to_far, "patch", odd + [(b, a) for a, b in odd])
    near = lax.ppermute(to_near, "patch", even + [(b, a) for a, b in even])
    if several:
        up = [jnp.concatenate([field[..., across:], row], axis=-1) for row in (near, far)]
        down = [jnp.concatenate([row, field[..., :-across]], axis=-1) for row in (near, far)]
        near = jnp.where(is_even, up[0], down[0])
        far = jnp.where(is_even, down[1], up[1])
    return near, far


def place_of(pair):
    low, high = sorted(pair)
    return high * (high + 1) // 2 + low


def gram_kernel(pairs, *refs):
    *ins, given, out = refs
    row = lax.broadcasted_iota(jnp.int32, given.shape, 0)
    sums = given[...]
    for i, j in pairs:
        part = jnp.sum(ins[i][...] * ins[j][...], axis=0, keepdims=True)
        sums = jnp.where(row == place_of((i, j)), part, sums)
    if out.shape != sums.shape:
        lane = lax.broadcasted_iota(jnp.int32, sums.shape, 1)
        whole = jnp.sum(sums, axis=1, keepdims=True)
        sums = jnp.sum(jnp.where(lane == row, whole, 0.0), axis=0, keepdims=True)
    out[...] = jnp.broadcast_to(sums, out.shape)


def gram_sums(basis, pairs, given, rows):
    return pl.pallas_call(
        functools.partial(gram_kernel, pairs),
        out_shape=jax.ShapeDtypeStruct((rows, given.shape[1]), jnp.float32),
    )(*basis, given)


def finish_kernel(parts_ref, *refs):
    directions, out = refs[:-1], refs[-1]
    width = len(directions)
    total = jnp.sum(parts_ref[...], axis=0, keepdims=True)
    shape = (SUMS, total.shape[1])
    row = lax.broadcasted_iota(jnp.int32, shape, 0)
    lane = lax.broadcasted_iota(jnp.int32, shape, 1)
    sums = jnp.sum(jnp.where(lane == row, total, 0.0), axis=1, keepdims=True)
    sums = jnp.broadcast_to(sums, shape)
    gram = {}
    for i in range(width + 1):
        for j in range(width + 1):
            place = place_of((i, j))
            gram[i, j] = sums[place : place + 1]
    half = [[gram[j + 1, i] + gram[j, i] for i in range(width + 1)] for j in range(width)]
    normal = [[half[j][i + 1] + half[j][i] for i in range(width)] for j in range(width)]
    right = [half[j][0] for j in range(width)]
    for i in range(width):
        inverse = 1.0 / normal[i][i]
        for j in range(i + 1, width):
            factor = normal[j][i] * inverse
            for k in range(i, width):
                normal[j][k] = normal[j][k] - factor * normal[i][k]
            right[j] = right[j] - factor * right[i]
    coeffs = [None] * width
    for i in reversed(range(width)):
        value = right[i]
        for k in range(i + 1, width):
            value = value - normal[i][k] * coeffs[k]
        coeffs[i] = value / normal[i][i]
    step = coeffs[0] * directions[0][...]
    for j in range(1, width):
        step = step + coeffs[j] * directions[j][...]
    out[...] = step


def per_device(newton_residual, diag_block, lower, upper, west, east, pivot_inverse):
    shape = newton_residual.shape
    count, block, rows, across = shape
    wide = rows * across

    def flat(matrix):
        return matrix.reshape(count, block, block, wide)

    diag_block, lower, upper, west, east, pivot = map(
        flat, (diag_block, lower, upper, west, east, pivot_inverse)
    )
    line = lax.axis_size("line")
    devices = line * lax.axis_size("patch")
    basis = [newton_residual.reshape(count, block, wide)]
    is_even = lax.axis_index("patch") % 2 == 0
    near_block = jnp.where(is_even, east, west)
    far_block = jnp.where(is_even, west, east)
    directions = []
    last = None
    for j in range(ITERS):
        direction, coupled, below = precondition(basis[j], last, lower, upper, pivot)
        if below is not None:
            basis[j] = basis[j].at[0].add(single_apply(lower[0], below))
        directions.append(direction)
        near, far = rows_beside(direction, across)
        last = direction[-1]
        image = coupled - basis[j] + block_apply(diag_block, direction)
        inner = [single_apply(lower[k], direction[k - 1]) for k in range(1, count)]
        if j == ITERS - 1:
            below = lax.ppermute(last, "line", [(i, i + 1) for i in range(line - 1)])
            inner = [single_apply(lower[0], below)] + inner
        else:
            inner = [jnp.zeros_like(last)] + inner
        image = image + jnp.stack(inner)
        image = (image + block_apply(near_block, near)) + block_apply(far_block, far)
        basis.append(image)
    flat_basis = [member.reshape(count * block, wide) for member in basis]
    pairs = [(i, j) for i in range(ITERS) for j in range(i, ITERS)]
    sums = gram_sums(flat_basis[:-1], pairs, jnp.zeros((SUMS, wide), jnp.float32), SUMS)
    sums = gram_sums(flat_basis, [(i, ITERS) for i in range(ITERS + 1)], sums, devices)
    sums = lax.all_to_all(sums, ("line", "patch"), 0, 0, tiled=True)
    step = pl.pallas_call(
        finish_kernel,
        out_shape=jax.ShapeDtypeStruct((count * block, wide), jnp.float32),
    )(sums, *[direction.reshape(count * block, wide) for direction in directions])
    return step.reshape(shape)


def solution(mesh):
    blocks = P("line", None, None, "patch", None)
    field = P("line", None, "patch", None)
    return jax.shard_map(
        per_device, mesh=mesh, in_specs=(field,) + (blocks,) * 6, out_specs=field, check_vma=False
    )
```

```python
import functools

import jax
import jax.numpy as jnp
from jax import lax
from jax.experimental import pallas as pl
from jax.experimental.pallas import tpu as pltpu
from jax.sharding import PartitionSpec as P

ITERS = 4
SUMS = 16


def single_apply(block_mat, vector):
    return jnp.sum(block_mat.astype(jnp.float32) * vector[None], axis=1)


def block_apply(block_mat, vector):
    return jnp.sum(block_mat.astype(jnp.float32) * vector[:, None], axis=2)


def sweep_down(vector, lower, pivot, entry):
    forward = [single_apply(pivot[0], vector[0] + single_apply(lower[0], entry))]
    for k in range(1, vector.shape[0]):
        forward.append(single_apply(pivot[k], vector[k] - single_apply(lower[k], forward[-1])))
    return forward


def sweep_up(forward, upper, pivot, incoming):
    count = len(forward)
    following = incoming
    result = [None] * count
    coupled = [None] * count
    for k in reversed(range(count)):
        coupled[k] = single_apply(upper[k], following)
        following = forward[k] - single_apply(pivot[k], coupled[k])
        result[k] = following
    return result, coupled


ROOM = 56 << 20


def start_all(pairs, sems):
    copies = [
        pltpu.make_async_copy(source, target, sems.at[place])
        for place, (source, target) in enumerate(pairs)
    ]
    for copy in copies:
        copy.start()
    return copies


def apply_into(block_mat, value, target):
    block = target.shape[0]
    rows = 16 if block % 16 == 0 else block
    for start in range(0, block, rows):
        part = block_mat[start : start + rows].astype(jnp.float32)
        target[start : start + rows] = jnp.sum(part * value[None], axis=1)


def first_kernel(vector, lower, pivot, lower_held, pivot_held, out, field, middle, sems):
    count = vector.shape[0]
    pairs = [(vector, field), (pivot.at[0], pivot_held.at[0])]
    for k in range(1, count):
        pairs += [(lower.at[k], lower_held.at[k]), (pivot.at[k], pivot_held.at[k])]
    pairs.append((lower.at[0], lower_held.at[0]))
    copies = start_all(pairs, sems)
    copies[0].wait()
    copies[1].wait()
    apply_into(pivot_held.at[0], field[0], out)
    for k in range(1, count):
        copies[2 * k].wait()
        apply_into(lower_held.at[k], out[...], middle)
        copies[2 * k + 1].wait()
        apply_into(pivot_held.at[k], field[k] - middle[...], out)
    copies[-1].wait()


def first_carry(vector, lower, pivot):
    count, block, wide = vector.shape
    vmem = pl.BlockSpec(memory_space=pltpu.VMEM)
    return pl.pallas_call(
        first_kernel,
        out_shape=[
            pltpu.VMEM(lower.shape, lower.dtype),
            pltpu.VMEM(pivot.shape, pivot.dtype),
            pltpu.VMEM((block, wide), jnp.float32),
        ],
        in_specs=[pl.BlockSpec(memory_space=pltpu.HBM)] * 3,
        out_specs=[vmem] * 3,
        scratch_shapes=[
            pltpu.VMEM(vector.shape, jnp.float32),
            pltpu.VMEM((block, wide), jnp.float32),
            pltpu.SemaphoreType.DMA((1 + 2 * count,)),
        ],
        compiler_params=pltpu.CompilerParams(vmem_limit_bytes=ROOM),
    )(vector, lower, pivot)


def hold_kernel(upper, diag_block, west, east, after, upper_held, diag_held, near, far, sems):
    even = lax.axis_index("patch") % 2 == 0

    def run(first, second):
        pairs = [(upper, upper_held), (diag_block, diag_held), (first, near), (second, far)]
        for copy in start_all(pairs, sems):
            copy.wait()

    pl.when(even)(lambda: run(east, west))
    pl.when(jnp.logical_not(even))(lambda: run(west, east))


def hold(upper, diag_block, west, east, after):
    return pl.pallas_call(
        hold_kernel,
        out_shape=[pltpu.VMEM(upper.shape, upper.dtype)] * 4,
        in_specs=[pl.BlockSpec(memory_space=pltpu.HBM)] * 4 + [pl.BlockSpec(memory_space=pl.ANY)],
        out_specs=[pl.BlockSpec(memory_space=pltpu.VMEM)] * 4,
        scratch_shapes=[pltpu.SemaphoreType.DMA((4,))],
        compiler_params=pltpu.CompilerParams(vmem_limit_bytes=ROOM),
    )(upper, diag_block, west, east, after)


def precondition(vector, last, lower, upper, pivot, carry=None):
    count = lax.axis_size("line")
    incoming = jnp.zeros((1 if last is None else 2,) + vector.shape[1:], vector.dtype)

    def entry():
        return -incoming[0] if last is None else incoming[1] - incoming[0]

    for turn in range(count - 1):
        if carry is not None and turn == 0:
            outgoing = carry
        else:
            outgoing = sweep_down(vector, lower, pivot, entry())[-1]
        message = outgoing[None] if last is None else jnp.stack([outgoing, last])
        incoming = incoming + lax.ppermute(message, "line", [(turn, turn + 1)])
    forward = sweep_down(vector, lower, pivot, entry())
    below = None if last is None else incoming[1]
    incoming = jnp.zeros_like(vector[0])
    for turn in reversed(range(count - 1)):
        outgoing = sweep_up(forward, upper, pivot, incoming)[0][0]
        incoming = incoming + lax.ppermute(outgoing, "line", [(turn + 1, turn)])
    result, coupled = sweep_up(forward, upper, pivot, incoming)
    return jnp.stack(result), jnp.stack(coupled), below


def rows_beside(field, across):
    count = lax.axis_size("patch")
    even = [(i, i + 1) for i in range(0, count - 1, 2)]
    odd = [(i, i + 1) for i in range(1, count - 1, 2)]
    is_even = lax.axis_index("patch") % 2 == 0
    first, last = field[..., :across], field[..., -across:]
    several = field.shape[-1] > across
    to_far = jnp.where(is_even, first, last) if several else field
    to_near = jnp.where(is_even, last, first) if several else field
    far = lax.ppermute(to_far, "patch", odd + [(b, a) for a, b in odd])
    near = lax.ppermute(to_near, "patch", even + [(b, a) for a, b in even])
    if several:
        up = [jnp.concatenate([field[..., across:], row], axis=-1) for row in (near, far)]
        down = [jnp.concatenate([row, field[..., :-across]], axis=-1) for row in (near, far)]
        near = jnp.where(is_even, up[0], down[0])
        far = jnp.where(is_even, down[1], up[1])
    return near, far


def place_of(pair):
    low, high = sorted(pair)
    return high * (high + 1) // 2 + low


def gram_kernel(pairs, *refs):
    *ins, given, out = refs
    row = lax.broadcasted_iota(jnp.int32, given.shape, 0)
    sums = given[...]
    for i, j in pairs:
        part = jnp.sum(ins[i][...] * ins[j][...], axis=0, keepdims=True)
        sums = jnp.where(row == place_of((i, j)), part, sums)
    if out.shape != sums.shape:
        lane = lax.broadcasted_iota(jnp.int32, sums.shape, 1)
        whole = jnp.sum(sums, axis=1, keepdims=True)
        sums = jnp.sum(jnp.where(lane == row, whole, 0.0), axis=0, keepdims=True)
    out[...] = jnp.broadcast_to(sums, out.shape)


def gram_sums(basis, pairs, given, rows):
    return pl.pallas_call(
        functools.partial(gram_kernel, pairs),
        out_shape=jax.ShapeDtypeStruct((rows, given.shape[1]), jnp.float32),
    )(*basis, given)


def finish_kernel(parts_ref, *refs):
    directions, out = refs[:-1], refs[-1]
    width = len(directions)
    total = jnp.sum(parts_ref[...], axis=0, keepdims=True)
    shape = (SUMS, total.shape[1])
    row = lax.broadcasted_iota(jnp.int32, shape, 0)
    lane = lax.broadcasted_iota(jnp.int32, shape, 1)
    sums = jnp.sum(jnp.where(lane == row, total, 0.0), axis=1, keepdims=True)
    sums = jnp.broadcast_to(sums, shape)
    gram = {}
    for i in range(width + 1):
        for j in range(width + 1):
            place = place_of((i, j))
            gram[i, j] = sums[place : place + 1]
    half = [[gram[j + 1, i] + gram[j, i] for i in range(width + 1)] for j in range(width)]
    normal = [[half[j][i + 1] + half[j][i] for i in range(width)] for j in range(width)]
    right = [half[j][0] for j in range(width)]
    for i in range(width):
        inverse = 1.0 / normal[i][i]
        for j in range(i + 1, width):
            factor = normal[j][i] * inverse
            for k in range(i, width):
                normal[j][k] = normal[j][k] - factor * normal[i][k]
            right[j] = right[j] - factor * right[i]
    coeffs = [None] * width
    for i in reversed(range(width)):
        value = right[i]
        for k in range(i + 1, width):
            value = value - normal[i][k] * coeffs[k]
        coeffs[i] = value / normal[i][i]
    step = coeffs[0] * directions[0][...]
    for j in range(1, width):
        step = step + coeffs[j] * directions[j][...]
    out[...] = step


def per_device(newton_residual, diag_block, lower, upper, west, east, pivot_inverse):
    shape = newton_residual.shape
    count, block, rows, across = shape
    wide = rows * across

    def flat(matrix):
        return matrix.reshape(count, block, block, wide)

    diag_block, lower, upper, west, east, pivot = map(
        flat, (diag_block, lower, upper, west, east, pivot_inverse)
    )
    line = lax.axis_size("line")
    devices = line * lax.axis_size("patch")
    basis = [newton_residual.reshape(count, block, wide)]
    lower, pivot, carry = first_carry(basis[0], lower, pivot)
    upper, diag_block, near_block, far_block = hold(upper, diag_block, west, east, carry)
    directions = []
    last = None
    for j in range(ITERS):
        direction, coupled, below = precondition(
            basis[j], last, lower, upper, pivot, carry if j == 0 else None
        )
        if below is not None:
            basis[j] = basis[j].at[0].add(single_apply(lower[0], below))
        directions.append(direction)
        near, far = rows_beside(direction, across)
        last = direction[-1]
        image = coupled - basis[j] + block_apply(diag_block, direction)
        inner = [single_apply(lower[k], direction[k - 1]) for k in range(1, count)]
        if j == ITERS - 1:
            below = lax.ppermute(last, "line", [(i, i + 1) for i in range(line - 1)])
            inner = [single_apply(lower[0], below)] + inner
        else:
            inner = [jnp.zeros_like(last)] + inner
        image = image + jnp.stack(inner)
        image = (image + block_apply(near_block, near)) + block_apply(far_block, far)
        basis.append(image)
    flat_basis = [member.reshape(count * block, wide) for member in basis]
    pairs = [(i, j) for i in range(ITERS) for j in range(i, ITERS)]
    sums = gram_sums(flat_basis[:-1], pairs, jnp.zeros((SUMS, wide), jnp.float32), SUMS)
    sums = gram_sums(flat_basis, [(i, ITERS) for i in range(ITERS + 1)], sums, devices)
    sums = lax.all_to_all(sums, ("line", "patch"), 0, 0, tiled=True)
    step = pl.pallas_call(
        finish_kernel,
        out_shape=jax.ShapeDtypeStruct((count * block, wide), jnp.float32),
    )(sums, *[direction.reshape(count * block, wide) for direction in directions])
    return step.reshape(shape)


def solution(mesh):
    blocks = P("line", None, None, "patch", None)
    field = P("line", None, "patch", None)
    return jax.shard_map(
        per_device, mesh=mesh, in_specs=(field,) + (blocks,) * 6, out_specs=field, check_vma=False
    )
```

```python
import functools

import jax
import jax.numpy as jnp
from jax import lax
from jax.experimental import pallas as pl
from jax.experimental.pallas import tpu as pltpu
from jax.sharding import PartitionSpec as P

ITERS = 4
SUMS = 16
FETCH_ROOM = 56 << 20
LOAD_ROOM = 40 << 20
STAGE_ROOM = 16 << 20


def start_all(pairs, sems):
    copies = [
        pltpu.make_async_copy(source, target, sems.at[place])
        for place, (source, target) in enumerate(pairs)
    ]
    for copy in copies:
        copy.start()
    return copies


def turn_over(source, target):
    block = source.shape[0]
    high = 16 if block % 16 == 0 else block
    wide = 8 if block % 8 == 0 else block
    for i in range(0, block, wide):
        for j in range(0, block, high):
            part = source[i : i + wide, j : j + high].astype(jnp.float32)
            target[j : j + high, i : i + wide] = jnp.swapaxes(part, 0, 1)


def apply_plain(block_mat, value, target):
    block = target.shape[0]
    rows = 16 if block % 16 == 0 else block
    for start in range(0, block, rows):
        part = block_mat[start : start + rows].astype(jnp.float32)
        target[start : start + rows] = jnp.sum(part * value[None], axis=1)


def apply_turned(block_mat, vector):
    totals = [None, None]
    for j in range(block_mat.shape[0]):
        term = block_mat[j] * vector[j : j + 1]
        totals[j % 2] = term if totals[j % 2] is None else totals[j % 2] + term
    return totals[0] + totals[1]


def first_kernel(vector, lower, pivot, lower_held, pivot_held, out, field, middle, sems):
    count = vector.shape[0]
    pairs = [(vector, field), (pivot.at[0], pivot_held.at[0])]
    for k in range(1, count):
        pairs += [(lower.at[k], lower_held.at[k]), (pivot.at[k], pivot_held.at[k])]
    pairs.append((lower.at[0], lower_held.at[0]))
    copies = start_all(pairs, sems)
    copies[0].wait()
    copies[1].wait()
    apply_plain(pivot_held.at[0], field[0], out.at[0])
    for k in range(1, count):
        copies[2 * k].wait()
        apply_plain(lower_held.at[k], out[0], middle)
        copies[2 * k + 1].wait()
        apply_plain(pivot_held.at[k], field[k] - middle[...], out.at[0])
    copies[-1].wait()


def first_carry(vector, lower, pivot):
    count, block, wide = vector.shape
    return pl.pallas_call(
        first_kernel,
        out_shape=[
            pltpu.VMEM(lower.shape, lower.dtype),
            pltpu.VMEM(pivot.shape, pivot.dtype),
            jax.ShapeDtypeStruct((1, block, wide), jnp.float32),
        ],
        in_specs=[pl.BlockSpec(memory_space=pl.ANY)] * 3,
        out_specs=[pl.BlockSpec(memory_space=pltpu.VMEM)] * 3,
        scratch_shapes=[
            pltpu.VMEM(vector.shape, jnp.float32),
            pltpu.VMEM((block, wide), jnp.float32),
            pltpu.SemaphoreType.DMA((1 + 2 * count,)),
        ],
        compiler_params=pltpu.CompilerParams(vmem_limit_bytes=FETCH_ROOM),
    )(vector, lower, pivot)


def turn_held_kernel(*refs):
    half = len(refs) // 2
    for source, target in zip(refs[:half], refs[half:]):
        for k in range(source.shape[0]):
            turn_over(source.at[k], target.at[k])


def turn_held(*blocks):
    vmem = pl.BlockSpec(memory_space=pltpu.VMEM)
    return pl.pallas_call(
        turn_held_kernel,
        out_shape=[pltpu.VMEM(block.shape, jnp.float32) for block in blocks],
        in_specs=[vmem] * len(blocks),
        out_specs=[vmem] * len(blocks),
        compiler_params=pltpu.CompilerParams(vmem_limit_bytes=STAGE_ROOM),
    )(*blocks)


def load_kernel(choose, *refs):
    *refs, held, sems = refs
    size = (len(refs) - 1) // 2
    sources, targets = refs[:size], refs[size + 1 :]

    def run(sources):
        copies = start_all([(s, held.at[place]) for place, s in enumerate(sources)], sems)
        for place, target in enumerate(targets):
            copies[place].wait()
            for k in range(target.shape[0]):
                turn_over(held.at[place, k], target.at[k])

    if choose:
        even = lax.axis_index("patch") % 2 == 0
        pl.when(even)(lambda: run(sources))
        pl.when(jnp.logical_not(even))(lambda: run((*sources[:-2], sources[-1], sources[-2])))
    else:
        run(sources)


def load(blocks, after, choose=False):
    shape = blocks[0].shape
    return pl.pallas_call(
        functools.partial(load_kernel, choose),
        out_shape=[pltpu.VMEM(shape, jnp.float32) for block in blocks],
        in_specs=[pl.BlockSpec(memory_space=pl.ANY)] * (len(blocks) + 1),
        out_specs=[pl.BlockSpec(memory_space=pltpu.VMEM)] * len(blocks),
        scratch_shapes=[
            pltpu.VMEM((len(blocks),) + shape, blocks[0].dtype),
            pltpu.SemaphoreType.DMA((len(blocks),)),
        ],
        compiler_params=pltpu.CompilerParams(vmem_limit_bytes=LOAD_ROOM),
    )(*blocks, after)


def stage(kernel, out_shapes, operands, scratch=()):
    vmem = pl.BlockSpec(memory_space=pltpu.VMEM)
    return pl.pallas_call(
        kernel,
        out_shape=[jax.ShapeDtypeStruct(shape, jnp.float32) for shape in out_shapes],
        in_specs=[vmem] * len(operands),
        out_specs=[vmem] * len(out_shapes),
        scratch_shapes=[pltpu.VMEM(shape, jnp.float32) for shape in scratch],
        compiler_params=pltpu.CompilerParams(vmem_limit_bytes=STAGE_ROOM),
    )(*operands)


def run_down(vector, lower, pivot, entry, forward, work):
    for k in range(vector.shape[0]):
        if k > 0:
            work[...] = vector[k] - apply_turned(lower.at[k], forward.at[k - 1])
        elif entry is not None:
            work[...] = vector[k] + apply_turned(lower.at[k], entry)
        else:
            work[...] = vector[k]
        forward[k] = apply_turned(pivot.at[k], work)


def run_up(forward, upper, pivot, incoming, result, coupled):
    count = forward.shape[0]
    for k in reversed(range(count)):
        following = result.at[k + 1] if k < count - 1 else incoming
        if following is None:
            result[k] = forward[k]
        else:
            coupled[k] = apply_turned(upper.at[k], following)
            result[k] = forward[k] - apply_turned(pivot.at[k], coupled.at[k])


def add_up(parts, target):
    total = parts[0][...]
    for part in parts[1:]:
        total = total + part[...]
    target[...] = total


def set_entry(carried, entry):
    both = carried.shape[0] == 2
    entry[...] = carried[1] - carried[0] if both else -carried[0]


def hop_down_kernel(parts, has_last, vector, lower, pivot, *refs):
    carried_in, refs = refs[:parts], refs[parts:]
    if has_last:
        last, *refs = refs
    carried, message, entry, forward, work = refs
    add_up(carried_in, carried)
    set_entry(carried, entry)
    run_down(vector, lower, pivot, entry, forward, work)
    message[0] = forward[forward.shape[0] - 1]
    if has_last:
        message[1] = last[...]


def turn_kernel(parts, vector, lower, pivot, upper, *refs):
    carried_in = refs[:parts]
    carried, forward, outgoing, entry, work, result, coupled = refs[parts:]
    add_up(carried_in, carried)
    set_entry(carried, entry)
    run_down(vector, lower, pivot, entry, forward, work)
    run_up(forward, upper, pivot, None, result, coupled)
    outgoing[...] = result[0]


def hop_up_kernel(parts, forward, upper, pivot, *refs):
    carried_in = refs[:parts]
    carried, outgoing, result, coupled = refs[parts:]
    add_up(carried_in, carried)
    run_up(forward, upper, pivot, carried, result, coupled)
    outgoing[...] = result[0]


def end_kernel(parts, forward, upper, pivot, *refs):
    carried_in = refs[:parts]
    result, coupled, last, carried = refs[parts:]
    add_up(carried_in, carried)
    run_up(forward, upper, pivot, carried, result, coupled)
    last[...] = result[result.shape[0] - 1]


def own_kernel(vector, carried, lower, diag_block, direction, coupled, whole, image):
    for k in range(vector.shape[0]):
        value = vector[k]
        if k == 0 and carried.shape[0] == 2:
            value = value + apply_turned(lower.at[0], carried.at[1])
        whole[k] = value
        value = coupled[k] - value + apply_turned(diag_block.at[k], direction.at[k])
        if k > 0:
            value = value + apply_turned(lower.at[k], direction.at[k - 1])
        image[k] = value


def near_kernel(image, near_block, near, out):
    for k in range(image.shape[0]):
        out[k] = image[k] + apply_turned(near_block.at[k], near.at[k])


def next_kernel(image, far_block, far, lower, pivot, last, out, message, forward, work):
    for k in range(image.shape[0]):
        out[k] = image[k] + apply_turned(far_block.at[k], far.at[k])
    run_down(out, lower, pivot, None, forward, work)
    message[0] = forward[forward.shape[0] - 1]
    message[1] = last[...]


def place_of(pair):
    low, high = sorted(pair)
    return high * (high + 1) // 2 + low


def pair_sum(left, right):
    total = left[0] * right[0]
    for k in range(1, left.shape[0]):
        total = total + left[k] * right[k]
    return jnp.sum(total, axis=0, keepdims=True)


def sums_kernel(*refs):
    *basis, out = refs
    row = lax.broadcasted_iota(jnp.int32, out.shape, 0)
    sums = jnp.zeros(out.shape, jnp.float32)
    for i in range(len(basis)):
        for j in range(i, len(basis)):
            sums = jnp.where(row == place_of((i, j)), pair_sum(basis[i], basis[j]), sums)
    out[...] = sums


def last_kernel(image, far_block, far, lower, below, sums_in, *refs):
    *basis, out, newest = refs
    for k in range(image.shape[0]):
        value = image[k] + apply_turned(far_block.at[k], far.at[k])
        if k == 0:
            value = value + apply_turned(lower.at[0], below)
        newest[k] = value
    sums = sums_in[...]
    row = lax.broadcasted_iota(jnp.int32, sums.shape, 0)
    lane = lax.broadcasted_iota(jnp.int32, sums.shape, 1)
    high = len(basis)
    for i, member in enumerate((*basis, newest)):
        sums = jnp.where(row == place_of((i, high)), pair_sum(member, newest), sums)
    whole = jnp.sum(sums, axis=1, keepdims=True)
    sums = jnp.sum(jnp.where(lane == row, whole, 0.0), axis=0, keepdims=True)
    out[...] = jnp.broadcast_to(sums, out.shape)


def finish_kernel(parts_ref, *refs):
    directions, out = refs[:-1], refs[-1]
    width = len(directions)
    total = jnp.sum(parts_ref[...], axis=0, keepdims=True)
    shape = (SUMS, total.shape[1])
    row = lax.broadcasted_iota(jnp.int32, shape, 0)
    lane = lax.broadcasted_iota(jnp.int32, shape, 1)
    sums = jnp.sum(jnp.where(lane == row, total, 0.0), axis=1, keepdims=True)
    sums = jnp.broadcast_to(sums, shape)
    gram = {}
    for i in range(width + 1):
        for j in range(width + 1):
            place = place_of((i, j))
            gram[i, j] = sums[place : place + 1]
    half = [[gram[j + 1, i] + gram[j, i] for i in range(width + 1)] for j in range(width)]
    normal = [[half[j][i + 1] + half[j][i] for i in range(width)] for j in range(width)]
    right = [half[j][0] for j in range(width)]
    for i in range(width):
        inverse = 1.0 / normal[i][i]
        for j in range(i + 1, width):
            factor = normal[j][i] * inverse
            for k in range(i, width):
                normal[j][k] = normal[j][k] - factor * normal[i][k]
            right[j] = right[j] - factor * right[i]
    coeffs = [None] * width
    for i in reversed(range(width)):
        value = right[i]
        for k in range(i + 1, width):
            value = value - normal[i][k] * coeffs[k]
        coeffs[i] = value / normal[i][i]
    for k in range(out.shape[0]):
        step = coeffs[0] * directions[0][k]
        for j in range(1, width):
            step = step + coeffs[j] * directions[j][k]
        out[k] = step


def rows_beside(field, across):
    count = lax.axis_size("patch")
    even = [(i, i + 1) for i in range(0, count - 1, 2)]
    odd = [(i, i + 1) for i in range(1, count - 1, 2)]
    is_even = lax.axis_index("patch") % 2 == 0
    first, last = field[..., :across], field[..., -across:]
    several = field.shape[-1] > across
    to_far = jnp.where(is_even, first, last) if several else field
    to_near = jnp.where(is_even, last, first) if several else field
    far = lax.ppermute(to_far, "patch", odd + [(b, a) for a, b in odd])
    near = lax.ppermute(to_near, "patch", even + [(b, a) for a, b in even])
    if several:
        up = [jnp.concatenate([field[..., across:], row], axis=-1) for row in (near, far)]
        down = [jnp.concatenate([row, field[..., :-across]], axis=-1) for row in (near, far)]
        near = jnp.where(is_even, up[0], down[0])
        far = jnp.where(is_even, down[1], up[1])
    return near, far


def per_device(newton_residual, diag_block, lower, upper, west, east, pivot_inverse):
    shape = newton_residual.shape
    count, block, rows, across = shape
    wide = rows * across

    def flat(matrix):
        return matrix.reshape(count, block, block, wide)

    diag_block, lower, upper, west, east, pivot = map(
        flat, (diag_block, lower, upper, west, east, pivot_inverse)
    )
    line = lax.axis_size("line")
    devices = line * lax.axis_size("patch")
    one, field = (block, wide), (count, block, wide)
    vector = newton_residual.reshape(field)
    lower, pivot, message = first_carry(vector, lower, pivot)
    lower, pivot = turn_held(lower, pivot)
    basis = []
    directions = []
    last = None
    for j in range(ITERS):
        parts = []
        for turn in range(line - 1):
            parts.append(lax.ppermute(message, "line", [(turn, turn + 1)]))
            if j == 0 and turn == 0:
                (upper,) = load((upper,), message)
            if turn < line - 2:
                lasts = [] if last is None else [last]
                carried, message = stage(
                    functools.partial(hop_down_kernel, len(parts), bool(lasts)),
                    [message.shape, message.shape],
                    [vector, lower, pivot, *parts, *lasts],
                    [one, field, one],
                )
                parts = [carried]
        parts = parts or [jnp.zeros_like(message)]
        carried_down, forward, outgoing = stage(
            functools.partial(turn_kernel, len(parts)),
            [message.shape, field, one],
            [vector, lower, pivot, upper, *parts],
            [one, one, field, field],
        )
        parts = []
        for turn in reversed(range(line - 1)):
            parts.append(lax.ppermute(outgoing, "line", [(turn + 1, turn)]))
            if j == 0 and turn == line - 2:
                diag_block, near_block, far_block = load((diag_block, east, west), outgoing, True)
            if turn > 0:
                carried, outgoing = stage(
                    functools.partial(hop_up_kernel, len(parts)),
                    [one, one],
                    [forward, upper, pivot, *parts],
                    [field, field],
                )
                parts = [carried]
        parts = parts or [jnp.zeros_like(outgoing)]
        direction, coupled, last = stage(
            functools.partial(end_kernel, len(parts)),
            [field, field, one],
            [forward, upper, pivot, *parts],
            [one],
        )
        directions.append(direction)
        near, far = rows_beside(direction, across)
        whole, image = stage(
            own_kernel,
            [field, field],
            [vector, carried_down, lower, diag_block, direction, coupled],
        )
        basis.append(whole)
        (image,) = stage(near_kernel, [field], [image, near_block, near])
        if j < ITERS - 1:
            vector, message = stage(
                next_kernel,
                [field, (2,) + one],
                [image, far_block, far, lower, pivot, last],
                [field, one],
            )
        else:
            below = lax.ppermute(last, "line", [(i, i + 1) for i in range(line - 1)])
            (sums,) = stage(sums_kernel, [(SUMS, wide)], basis)
            (sums,) = stage(
                last_kernel,
                [(devices, wide)],
                [image, far_block, far, lower, below, sums, *basis],
                [field],
            )
    sums = lax.all_to_all(sums, ("line", "patch"), 0, 0, tiled=True)
    (step,) = stage(finish_kernel, [field], [sums, *directions])
    return step.reshape(shape)


def solution(mesh):
    blocks = P("line", None, None, "patch", None)
    field = P("line", None, "patch", None)
    return jax.shard_map(
        per_device, mesh=mesh, in_specs=(field,) + (blocks,) * 6, out_specs=field, check_vma=False
    )
```

```python
import functools

import jax
import jax.numpy as jnp
from jax import lax
from jax.experimental import pallas as pl
from jax.experimental.pallas import tpu as pltpu
from jax.sharding import PartitionSpec as P

ITERS = 4
SUMS = 16
FETCH_ROOM = 56 << 20
LOAD_ROOM = 40 << 20
STAGE_ROOM = 16 << 20


def start_all(pairs, sems):
    copies = [
        pltpu.make_async_copy(source, target, sems.at[place])
        for place, (source, target) in enumerate(pairs)
    ]
    for copy in copies:
        copy.start()
    return copies


def turn_over(source, target):
    block = source.shape[0]
    high = 16 if block % 16 == 0 else block
    wide = 8 if block % 8 == 0 else block
    for i in range(0, block, wide):
        for j in range(0, block, high):
            part = source[i : i + wide, j : j + high].astype(jnp.float32)
            target[j : j + high, i : i + wide] = jnp.swapaxes(part, 0, 1)


def apply_plain(block_mat, value, target):
    block = target.shape[0]
    rows = 16 if block % 16 == 0 else block
    for start in range(0, block, rows):
        part = block_mat[start : start + rows].astype(jnp.float32)
        target[start : start + rows] = jnp.sum(part * value[None], axis=1)


def apply_turned(block_mat, vector):
    totals = [None, None]
    for j in range(block_mat.shape[0]):
        term = block_mat[j] * vector[j : j + 1]
        totals[j % 2] = term if totals[j % 2] is None else totals[j % 2] + term
    return totals[0] + totals[1]


def first_kernel(vector, lower, pivot, lower_held, pivot_held, out, field, middle, sems):
    count = vector.shape[0]
    pairs = [(vector, field), (pivot.at[0], pivot_held.at[0])]
    for k in range(1, count):
        pairs += [(lower.at[k], lower_held.at[k]), (pivot.at[k], pivot_held.at[k])]
    pairs.append((lower.at[0], lower_held.at[0]))
    copies = start_all(pairs, sems)
    copies[0].wait()
    copies[1].wait()
    apply_plain(pivot_held.at[0], field[0], out.at[0])
    for k in range(1, count):
        copies[2 * k].wait()
        apply_plain(lower_held.at[k], out[0], middle)
        copies[2 * k + 1].wait()
        apply_plain(pivot_held.at[k], field[k] - middle[...], out.at[0])
    copies[-1].wait()


def first_carry(vector, lower, pivot):
    count, block, wide = vector.shape
    return pl.pallas_call(
        first_kernel,
        out_shape=[
            pltpu.VMEM(lower.shape, lower.dtype),
            pltpu.VMEM(pivot.shape, pivot.dtype),
            jax.ShapeDtypeStruct((1, block, wide), jnp.float32),
        ],
        in_specs=[pl.BlockSpec(memory_space=pl.ANY)] * 3,
        out_specs=[pl.BlockSpec(memory_space=pltpu.VMEM)] * 3,
        scratch_shapes=[
            pltpu.VMEM(vector.shape, jnp.float32),
            pltpu.VMEM((block, wide), jnp.float32),
            pltpu.SemaphoreType.DMA((1 + 2 * count,)),
        ],
        compiler_params=pltpu.CompilerParams(vmem_limit_bytes=FETCH_ROOM),
    )(vector, lower, pivot)


def turn_held_kernel(*refs):
    half = len(refs) // 2
    for source, target in zip(refs[:half], refs[half:]):
        for k in range(source.shape[0]):
            turn_over(source.at[k], target.at[k])


def turn_held(*blocks):
    vmem = pl.BlockSpec(memory_space=pltpu.VMEM)
    return pl.pallas_call(
        turn_held_kernel,
        out_shape=[pltpu.VMEM(block.shape, jnp.float32) for block in blocks],
        in_specs=[vmem] * len(blocks),
        out_specs=[vmem] * len(blocks),
        compiler_params=pltpu.CompilerParams(vmem_limit_bytes=STAGE_ROOM),
    )(*blocks)


def load_kernel(choose, *refs):
    *refs, held, sems = refs
    size = (len(refs) - 1) // 2
    sources, targets = refs[:size], refs[size + 1 :]

    def run(sources):
        copies = start_all([(s, held.at[place]) for place, s in enumerate(sources)], sems)
        for place, target in enumerate(targets):
            copies[place].wait()
            for k in range(target.shape[0]):
                turn_over(held.at[place, k], target.at[k])

    if choose:
        even = lax.axis_index("patch") % 2 == 0
        pl.when(even)(lambda: run(sources))
        pl.when(jnp.logical_not(even))(lambda: run((*sources[:-2], sources[-1], sources[-2])))
    else:
        run(sources)


def load(blocks, after, choose=False):
    shape = blocks[0].shape
    return pl.pallas_call(
        functools.partial(load_kernel, choose),
        out_shape=[pltpu.VMEM(shape, jnp.float32) for block in blocks],
        in_specs=[pl.BlockSpec(memory_space=pl.ANY)] * (len(blocks) + 1),
        out_specs=[pl.BlockSpec(memory_space=pltpu.VMEM)] * len(blocks),
        scratch_shapes=[
            pltpu.VMEM((len(blocks),) + shape, blocks[0].dtype),
            pltpu.SemaphoreType.DMA((len(blocks),)),
        ],
        compiler_params=pltpu.CompilerParams(vmem_limit_bytes=LOAD_ROOM),
    )(*blocks, after)


def stage(kernel, out_shapes, operands, scratch=()):
    vmem = pl.BlockSpec(memory_space=pltpu.VMEM)
    return pl.pallas_call(
        kernel,
        out_shape=[jax.ShapeDtypeStruct(shape, jnp.float32) for shape in out_shapes],
        in_specs=[vmem] * len(operands),
        out_specs=[vmem] * len(out_shapes),
        scratch_shapes=[pltpu.VMEM(shape, jnp.float32) for shape in scratch],
        compiler_params=pltpu.CompilerParams(vmem_limit_bytes=STAGE_ROOM),
    )(*operands)


def run_down(vector, lower, pivot, entry, forward, work):
    for k in range(vector.shape[0]):
        if k > 0:
            work[...] = vector[k] - apply_turned(lower.at[k], forward.at[k - 1])
        elif entry is not None:
            work[...] = vector[k] + apply_turned(lower.at[k], entry)
        else:
            work[...] = vector[k]
        forward[k] = apply_turned(pivot.at[k], work)


def run_up(forward, upper, pivot, incoming, result, coupled):
    count = forward.shape[0]
    for k in reversed(range(count)):
        following = result.at[k + 1] if k < count - 1 else incoming
        if following is None:
            result[k] = forward[k]
        else:
            coupled[k] = apply_turned(upper.at[k], following)
            result[k] = forward[k] - apply_turned(pivot.at[k], coupled.at[k])


def add_up(parts, target):
    total = parts[0][...]
    for part in parts[1:]:
        total = total + part[...]
    target[...] = total


def set_entry(carried, entry):
    both = carried.shape[0] == 2
    entry[...] = carried[1] - carried[0] if both else -carried[0]


def hop_down_kernel(parts, has_last, vector, lower, pivot, *refs):
    carried_in, refs = refs[:parts], refs[parts:]
    if has_last:
        last, *refs = refs
    carried, message, entry, forward, work = refs
    add_up(carried_in, carried)
    set_entry(carried, entry)
    run_down(vector, lower, pivot, entry, forward, work)
    message[0] = forward[forward.shape[0] - 1]
    if has_last:
        message[1] = last[...]


def turn_kernel(parts, vector, lower, pivot, upper, *refs):
    carried_in = refs[:parts]
    carried, forward, outgoing, entry, work, result, coupled = refs[parts:]
    add_up(carried_in, carried)
    set_entry(carried, entry)
    run_down(vector, lower, pivot, entry, forward, work)
    run_up(forward, upper, pivot, None, result, coupled)
    outgoing[...] = result[0]


def hop_up_kernel(parts, forward, upper, pivot, *refs):
    carried_in = refs[:parts]
    carried, outgoing, result, coupled = refs[parts:]
    add_up(carried_in, carried)
    run_up(forward, upper, pivot, carried, result, coupled)
    outgoing[...] = result[0]


def end_kernel(parts, forward, upper, pivot, *refs):
    carried_in = refs[:parts]
    result, coupled, last, carried = refs[parts:]
    add_up(carried_in, carried)
    run_up(forward, upper, pivot, carried, result, coupled)
    last[...] = result[result.shape[0] - 1]


def multiply_lines(left, right, out):
    block = right.shape[0]
    group = max(g for g in (1, 2, 3, 4) if block % g == 0)
    unroll = max(u for u in (1, 2, 4, 8) if block % u == 0)

    def rows(step, carry):
        start = step * group

        def add(j, totals):
            row = right[j]
            return tuple(
                total + left[start + q, pl.ds(j, 1), :] * row for q, total in enumerate(totals)
            )

        zero = jnp.zeros(right.shape[1:], jnp.float32)
        totals = lax.fori_loop(0, block, add, (zero,) * group, unroll=unroll)
        for q, total in enumerate(totals):
            out[start + q] = total
        return carry

    lax.fori_loop(0, block // group, rows, 0)


def on_last(body):
    pl.when(lax.axis_index("line") == lax.axis_size("line") - 1)(body)


def factor_kernel(lower, pivot, after, factor, out):
    def body():
        multiply_lines(lower.at[0], pivot.at[0], factor)
        multiply_lines(factor, lower.at[1], out)

    on_last(body)


def response_kernel(factor, given, upper, pivot, after, out, work):
    def body():
        multiply_lines(given, pivot.at[1], out)
        multiply_lines(out, upper.at[0], work)
        multiply_lines(work, pivot.at[0], out)

        def row(i, carry):
            out[i] = out[i] + factor[i]
            return carry

        lax.fori_loop(0, out.shape[0], row, 0, unroll=4)

    on_last(body)


def alone_kernel(forward, upper, pivot, outgoing, result, coupled):
    run_up(forward, upper, pivot, None, result, coupled)
    outgoing[...] = result[0]


def short_turn_kernel(parts, vector, lower, pivot, upper, response, alone, last, *refs):
    carried_in = refs[:parts]
    carried, message, upward, outgoing, forward, entry, work, result, coupled = refs[parts:]
    add_up(carried_in, carried)
    set_entry(carried, entry)
    run_down(vector, lower, pivot, entry, forward, work)
    message[0] = forward[forward.shape[0] - 1]
    message[1] = last[...]
    entry[...] = message[1] - message[0]
    upward[...] = alone[...] + apply_turned(response, entry)
    run_up(forward, upper, pivot, upward, result, coupled)
    outgoing[...] = result[0]


def forward_kernel(parts, vector, lower, pivot, *refs):
    carried_in = refs[:parts]
    carried, forward, entry, work = refs[parts:]
    add_up(carried_in, carried)
    set_entry(carried, entry)
    run_down(vector, lower, pivot, entry, forward, work)


def own_kernel(vector, carried, lower, diag_block, direction, coupled, whole, image):
    for k in range(vector.shape[0]):
        value = vector[k]
        if k == 0 and carried.shape[0] == 2:
            value = value + apply_turned(lower.at[0], carried.at[1])
        whole[k] = value
        value = coupled[k] - value + apply_turned(diag_block.at[k], direction.at[k])
        if k > 0:
            value = value + apply_turned(lower.at[k], direction.at[k - 1])
        image[k] = value


def near_kernel(image, near_block, near, *refs):
    *below, out = refs
    for k in range(image.shape[0]):
        out[k] = image[k] + apply_turned(near_block.at[k], near.at[k])
    if below:
        out[0] = out[0] + apply_turned(below[0].at[0], below[1])


def next_kernel(image, far_block, far, lower, pivot, last, out, message, forward, work):
    for k in range(image.shape[0]):
        out[k] = image[k] + apply_turned(far_block.at[k], far.at[k])
    run_down(out, lower, pivot, None, forward, work)
    message[0] = forward[forward.shape[0] - 1]
    message[1] = last[...]


def place_of(pair):
    low, high = sorted(pair)
    return high * (high + 1) // 2 + low


def pair_sum(left, right):
    total = left[0] * right[0]
    for k in range(1, left.shape[0]):
        total = total + left[k] * right[k]
    return jnp.sum(total, axis=0, keepdims=True)


def sums_kernel(*refs):
    *basis, out = refs
    row = lax.broadcasted_iota(jnp.int32, out.shape, 0)
    sums = jnp.zeros(out.shape, jnp.float32)
    for i in range(len(basis)):
        for j in range(i, len(basis)):
            sums = jnp.where(row == place_of((i, j)), pair_sum(basis[i], basis[j]), sums)
    out[...] = sums


def last_kernel(image, far_block, far, sums_in, *refs):
    *basis, out, newest = refs
    for k in range(image.shape[0]):
        newest[k] = image[k] + apply_turned(far_block.at[k], far.at[k])
    sums = sums_in[...]
    row = lax.broadcasted_iota(jnp.int32, sums.shape, 0)
    lane = lax.broadcasted_iota(jnp.int32, sums.shape, 1)
    high = len(basis)
    for i, member in enumerate((*basis, newest)):
        sums = jnp.where(row == place_of((i, high)), pair_sum(member, newest), sums)
    whole = jnp.sum(sums, axis=1, keepdims=True)
    sums = jnp.sum(jnp.where(lane == row, whole, 0.0), axis=0, keepdims=True)
    out[...] = jnp.broadcast_to(sums, out.shape)


def finish_kernel(parts_ref, *refs):
    directions, out = refs[:-1], refs[-1]
    width = len(directions)
    total = jnp.sum(parts_ref[...], axis=0, keepdims=True)
    shape = (SUMS, total.shape[1])
    row = lax.broadcasted_iota(jnp.int32, shape, 0)
    lane = lax.broadcasted_iota(jnp.int32, shape, 1)
    sums = jnp.sum(jnp.where(lane == row, total, 0.0), axis=1, keepdims=True)
    sums = jnp.broadcast_to(sums, shape)
    gram = {}
    for i in range(width + 1):
        for j in range(width + 1):
            place = place_of((i, j))
            gram[i, j] = sums[place : place + 1]
    half = [[gram[j + 1, i] + gram[j, i] for i in range(width + 1)] for j in range(width)]
    normal = [[half[j][i + 1] + half[j][i] for i in range(width)] for j in range(width)]
    right = [half[j][0] for j in range(width)]
    for i in range(width):
        inverse = 1.0 / normal[i][i]
        for j in range(i + 1, width):
            factor = normal[j][i] * inverse
            for k in range(i, width):
                normal[j][k] = normal[j][k] - factor * normal[i][k]
            right[j] = right[j] - factor * right[i]
    coeffs = [None] * width
    for i in reversed(range(width)):
        value = right[i]
        for k in range(i + 1, width):
            value = value - normal[i][k] * coeffs[k]
        coeffs[i] = value / normal[i][i]
    for k in range(out.shape[0]):
        step = coeffs[0] * directions[0][k]
        for j in range(1, width):
            step = step + coeffs[j] * directions[j][k]
        out[k] = step


def rows_beside(field, across):
    count = lax.axis_size("patch")
    even = [(i, i + 1) for i in range(0, count - 1, 2)]
    odd = [(i, i + 1) for i in range(1, count - 1, 2)]
    is_even = lax.axis_index("patch") % 2 == 0
    first, last = field[..., :across], field[..., -across:]
    several = field.shape[-1] > across
    to_far = jnp.where(is_even, first, last) if several else field
    to_near = jnp.where(is_even, last, first) if several else field
    far = lax.ppermute(to_far, "patch", odd + [(b, a) for a, b in odd])
    near = lax.ppermute(to_near, "patch", even + [(b, a) for a, b in even])
    if several:
        up = [jnp.concatenate([field[..., across:], row], axis=-1) for row in (near, far)]
        down = [jnp.concatenate([row, field[..., :-across]], axis=-1) for row in (near, far)]
        near = jnp.where(is_even, up[0], down[0])
        far = jnp.where(is_even, down[1], up[1])
    return near, far


def sweep_short(vector, message, alone_forward, last, lower, pivot, upper, response):
    line = lax.axis_size("line")
    field, one = vector.shape, last.shape
    parts = []
    for turn in range(line - 2):
        parts.append(lax.ppermute(message, "line", [(turn, turn + 1)]))
        if turn == 0:
            (alone,) = stage(
                alone_kernel, [one], [alone_forward, upper, pivot], [field, field]
            )
            alone = lax.ppermute(alone, "line", [(line - 1, line - 2)])
        if turn < line - 3:
            carried, message = stage(
                functools.partial(hop_down_kernel, len(parts), True),
                [message.shape, message.shape],
                [vector, lower, pivot, *parts, last],
                [one, field, one],
            )
            parts = [carried]
    carried_down, message, upward, outgoing, forward = stage(
        functools.partial(short_turn_kernel, len(parts)),
        [message.shape, message.shape, one, one, field],
        [vector, lower, pivot, upper, response, alone, last, *parts],
        [one, one, field, field],
    )
    parts = [upward]
    for turn in reversed(range(line - 2)):
        if turn == 0:
            outgoing, message = lax.optimization_barrier((outgoing, message))
        parts.append(lax.ppermute(outgoing, "line", [(turn + 1, turn)]))
        if turn == 0:
            onward = lax.ppermute(message, "line", [(line - 2, line - 1)])
            carried_down, whole_forward = stage(
                functools.partial(forward_kernel, 2),
                [message.shape, field],
                [vector, lower, pivot, carried_down, onward],
                [one, one],
            )
        if turn > 0:
            carried, outgoing = stage(
                functools.partial(hop_up_kernel, len(parts)),
                [one, one],
                [forward, upper, pivot, *parts],
                [field, field],
            )
            parts = [carried]
    return carried_down, whole_forward, parts


def per_device(newton_residual, diag_block, lower, upper, west, east, pivot_inverse):
    shape = newton_residual.shape
    count, block, rows, across = shape
    wide = rows * across

    def flat(matrix):
        return matrix.reshape(count, block, block, wide)

    diag_block, lower, upper, west, east, pivot = map(
        flat, (diag_block, lower, upper, west, east, pivot_inverse)
    )
    line = lax.axis_size("line")
    devices = line * lax.axis_size("patch")
    one, field = (block, wide), (count, block, wide)
    vector = newton_residual.reshape(field)
    lower, pivot, message = first_carry(vector, lower, pivot)
    lower, pivot = turn_held(lower, pivot)
    basis = []
    directions = []
    last = None
    short = line > 2 and count == 2
    for j in range(ITERS):
        if j >= 2 and short:
            carried_down, forward, parts = sweep_short(
                vector, message, alone_forward, last, lower, pivot, upper, response
            )
        else:
            parts = []
            for turn in range(line - 1):
                parts.append(lax.ppermute(message, "line", [(turn, turn + 1)]))
                if j == 0 and turn == 0:
                    (upper,) = load((upper,), message)
                if j == 0 and turn == line - 2 and short:
                    factor, response = stage(
                        factor_kernel, [(block,) + one] * 2, [lower, pivot, message]
                    )
                if turn < line - 2:
                    lasts = [] if last is None else [last]
                    carried, message = stage(
                        functools.partial(hop_down_kernel, len(parts), bool(lasts)),
                        [message.shape, message.shape],
                        [vector, lower, pivot, *parts, *lasts],
                        [one, field, one],
                    )
                    parts = [carried]
            parts = parts or [jnp.zeros_like(message)]
            carried_down, forward, outgoing = stage(
                functools.partial(turn_kernel, len(parts)),
                [message.shape, field, one],
                [vector, lower, pivot, upper, *parts],
                [one, one, field, field],
            )
            if j == 0 and short:
                outgoing, response = lax.optimization_barrier((outgoing, response))
            parts = []
            for turn in reversed(range(line - 1)):
                if j == 1 and turn == line - 3 and short:
                    outgoing, ready = lax.optimization_barrier((outgoing, response))
                    response = lax.ppermute(ready, "line", [(line - 1, line - 2)])
                parts.append(lax.ppermute(outgoing, "line", [(turn + 1, turn)]))
                if j == 0 and turn == line - 2:
                    diag_block, near_block, far_block = load(
                        (diag_block, east, west), outgoing, True
                    )
                if j == 0 and turn == line - 3 and short:
                    (response,) = stage(
                        response_kernel,
                        [(block,) + one],
                        [factor, response, upper, pivot, outgoing],
                        [(block,) + one],
                    )
                if turn > 0:
                    carried, outgoing = stage(
                        functools.partial(hop_up_kernel, len(parts)),
                        [one, one],
                        [forward, upper, pivot, *parts],
                        [field, field],
                    )
                    parts = [carried]
            parts = parts or [jnp.zeros_like(outgoing)]
        direction, coupled, last = stage(
            functools.partial(end_kernel, len(parts)),
            [field, field, one],
            [forward, upper, pivot, *parts],
            [one],
        )
        directions.append(direction)
        near, far = rows_beside(direction, across)
        if j == 1 and short:
            near, response = lax.optimization_barrier((near, response))
        whole, image = stage(
            own_kernel,
            [field, field],
            [vector, carried_down, lower, diag_block, direction, coupled],
        )
        basis.append(whole)
        beneath = []
        if j == ITERS - 1:
            (sums,) = stage(sums_kernel, [(SUMS, wide)], basis)
            below = lax.ppermute(last, "line", [(i, i + 1) for i in range(line - 1)])
            beneath = [lower, below]
        (image,) = stage(near_kernel, [field], [image, near_block, near, *beneath])
        if j < ITERS - 1:
            vector, message, alone_forward = stage(
                next_kernel,
                [field, (2,) + one, field],
                [image, far_block, far, lower, pivot, last],
                [one],
            )
            if j == 0 and short:
                message, response = lax.optimization_barrier((message, response))
        else:
            (sums,) = stage(
                last_kernel,
                [(devices, wide)],
                [image, far_block, far, sums, *basis],
                [field],
            )
    sums = lax.all_to_all(sums, ("line", "patch"), 0, 0, tiled=True)
    (step,) = stage(finish_kernel, [field], [sums, *directions])
    return step.reshape(shape)


def solution(mesh):
    blocks = P("line", None, None, "patch", None)
    field = P("line", None, "patch", None)
    return jax.shard_map(
        per_device, mesh=mesh, in_specs=(field,) + (blocks,) * 6, out_specs=field, check_vma=False
    )
```

```python
import functools

import jax
import jax.numpy as jnp
from jax import lax
from jax.experimental import pallas as pl
from jax.experimental.pallas import tpu as pltpu
from jax.sharding import PartitionSpec as P

ITERS = 4
SUMS = 16
FETCH_ROOM = 56 << 20
LOAD_ROOM = 40 << 20
STAGE_ROOM = 16 << 20


def start_all(pairs, sems):
    copies = [
        pltpu.make_async_copy(source, target, sems.at[place])
        for place, (source, target) in enumerate(pairs)
    ]
    for copy in copies:
        copy.start()
    return copies


def turn_over(source, target):
    block = source.shape[0]
    high = 16 if block % 16 == 0 else block
    wide = 8 if block % 8 == 0 else block
    for i in range(0, block, wide):
        for j in range(0, block, high):
            part = source[i : i + wide, j : j + high].astype(jnp.float32)
            target[j : j + high, i : i + wide] = jnp.swapaxes(part, 0, 1)


def apply_plain(block_mat, value, target):
    block = target.shape[0]
    rows = 16 if block % 16 == 0 else block
    for start in range(0, block, rows):
        part = block_mat[start : start + rows].astype(jnp.float32)
        target[start : start + rows] = jnp.sum(part * value[None], axis=1)


def apply_turned(block_mat, vector):
    totals = [None, None]
    for j in range(block_mat.shape[0]):
        term = block_mat[j] * vector[j : j + 1]
        totals[j % 2] = term if totals[j % 2] is None else totals[j % 2] + term
    return totals[0] + totals[1]


def first_kernel(vector, lower, pivot, lower_held, pivot_held, out, field, middle, sems):
    count = vector.shape[0]
    pairs = [(vector, field), (pivot.at[0], pivot_held.at[0])]
    for k in range(1, count):
        pairs += [(lower.at[k], lower_held.at[k]), (pivot.at[k], pivot_held.at[k])]
    pairs.append((lower.at[0], lower_held.at[0]))
    copies = start_all(pairs, sems)
    copies[0].wait()
    copies[1].wait()
    apply_plain(pivot_held.at[0], field[0], out.at[0])
    for k in range(1, count):
        copies[2 * k].wait()
        apply_plain(lower_held.at[k], out[0], middle)
        copies[2 * k + 1].wait()
        apply_plain(pivot_held.at[k], field[k] - middle[...], out.at[0])
    copies[-1].wait()


def first_carry(vector, lower, pivot):
    count, block, wide = vector.shape
    return pl.pallas_call(
        first_kernel,
        out_shape=[
            pltpu.VMEM(lower.shape, lower.dtype),
            pltpu.VMEM(pivot.shape, pivot.dtype),
            jax.ShapeDtypeStruct((1, block, wide), jnp.float32),
        ],
        in_specs=[pl.BlockSpec(memory_space=pl.ANY)] * 3,
        out_specs=[pl.BlockSpec(memory_space=pltpu.VMEM)] * 3,
        scratch_shapes=[
            pltpu.VMEM(vector.shape, jnp.float32),
            pltpu.VMEM((block, wide), jnp.float32),
            pltpu.SemaphoreType.DMA((1 + 2 * count,)),
        ],
        compiler_params=pltpu.CompilerParams(vmem_limit_bytes=FETCH_ROOM),
    )(vector, lower, pivot)


def turn_held_kernel(*refs):
    half = len(refs) // 2
    for source, target in zip(refs[:half], refs[half:]):
        for k in range(source.shape[0]):
            turn_over(source.at[k], target.at[k])


def turn_held(*blocks):
    vmem = pl.BlockSpec(memory_space=pltpu.VMEM)
    return pl.pallas_call(
        turn_held_kernel,
        out_shape=[pltpu.VMEM(block.shape, jnp.float32) for block in blocks],
        in_specs=[vmem] * len(blocks),
        out_specs=[vmem] * len(blocks),
        compiler_params=pltpu.CompilerParams(vmem_limit_bytes=STAGE_ROOM),
    )(*blocks)


def load_kernel(choose, *refs):
    *refs, held, sems = refs
    size = (len(refs) - 1) // 2
    sources, targets = refs[:size], refs[size + 1 :]

    def run(sources):
        copies = start_all([(s, held.at[place]) for place, s in enumerate(sources)], sems)
        for place, target in enumerate(targets):
            copies[place].wait()
            for k in range(target.shape[0]):
                turn_over(held.at[place, k], target.at[k])

    if choose:
        even = lax.axis_index("patch") % 2 == 0
        pl.when(even)(lambda: run(sources))
        pl.when(jnp.logical_not(even))(lambda: run((*sources[:-2], sources[-1], sources[-2])))
    else:
        run(sources)


def load(blocks, after, choose=False):
    shape = blocks[0].shape
    return pl.pallas_call(
        functools.partial(load_kernel, choose),
        out_shape=[pltpu.VMEM(shape, jnp.float32) for block in blocks],
        in_specs=[pl.BlockSpec(memory_space=pl.ANY)] * (len(blocks) + 1),
        out_specs=[pl.BlockSpec(memory_space=pltpu.VMEM)] * len(blocks),
        scratch_shapes=[
            pltpu.VMEM((len(blocks),) + shape, blocks[0].dtype),
            pltpu.SemaphoreType.DMA((len(blocks),)),
        ],
        compiler_params=pltpu.CompilerParams(vmem_limit_bytes=LOAD_ROOM),
    )(*blocks, after)


def stage(kernel, out_shapes, operands, scratch=()):
    vmem = pl.BlockSpec(memory_space=pltpu.VMEM)
    return pl.pallas_call(
        kernel,
        out_shape=[jax.ShapeDtypeStruct(shape, jnp.float32) for shape in out_shapes],
        in_specs=[vmem] * len(operands),
        out_specs=[vmem] * len(out_shapes),
        scratch_shapes=[pltpu.VMEM(shape, jnp.float32) for shape in scratch],
        compiler_params=pltpu.CompilerParams(vmem_limit_bytes=STAGE_ROOM),
    )(*operands)


def run_down(vector, lower, pivot, entry, forward, work):
    for k in range(vector.shape[0]):
        if k > 0:
            work[...] = vector[k] - apply_turned(lower.at[k], forward.at[k - 1])
        elif entry is not None:
            work[...] = vector[k] + apply_turned(lower.at[k], entry)
        else:
            work[...] = vector[k]
        forward[k] = apply_turned(pivot.at[k], work)


def run_up(forward, upper, pivot, incoming, result, coupled):
    count = forward.shape[0]
    for k in reversed(range(count)):
        following = result.at[k + 1] if k < count - 1 else incoming
        if following is None:
            result[k] = forward[k]
        else:
            coupled[k] = apply_turned(upper.at[k], following)
            result[k] = forward[k] - apply_turned(pivot.at[k], coupled.at[k])


def add_up(parts, target):
    total = parts[0][...]
    for part in parts[1:]:
        total = total + part[...]
    target[...] = total


def set_entry(carried, entry):
    both = carried.shape[0] == 2
    entry[...] = carried[1] - carried[0] if both else -carried[0]


def hop_down_kernel(parts, has_last, vector, lower, pivot, *refs):
    carried_in, refs = refs[:parts], refs[parts:]
    if has_last:
        last, *refs = refs
    carried, message, entry, forward, work = refs
    add_up(carried_in, carried)
    set_entry(carried, entry)
    run_down(vector, lower, pivot, entry, forward, work)
    message[0] = forward[forward.shape[0] - 1]
    if has_last:
        message[1] = last[...]


def turn_kernel(parts, vector, lower, pivot, upper, *refs):
    carried_in = refs[:parts]
    carried, forward, outgoing, entry, work, result, coupled = refs[parts:]
    add_up(carried_in, carried)
    set_entry(carried, entry)
    run_down(vector, lower, pivot, entry, forward, work)
    run_up(forward, upper, pivot, None, result, coupled)
    outgoing[...] = result[0]


def hop_up_kernel(parts, forward, upper, pivot, *refs):
    carried_in = refs[:parts]
    carried, outgoing, result, coupled = refs[parts:]
    add_up(carried_in, carried)
    run_up(forward, upper, pivot, carried, result, coupled)
    outgoing[...] = result[0]


def end_kernel(parts, forward, upper, pivot, *refs):
    carried_in = refs[:parts]
    result, coupled, last, carried = refs[parts:]
    add_up(carried_in, carried)
    run_up(forward, upper, pivot, carried, result, coupled)
    last[...] = result[result.shape[0] - 1]


def multiply_lines(left, right, out):
    block = right.shape[0]
    group = max(g for g in (1, 2, 3, 4) if block % g == 0)
    unroll = max(u for u in (1, 2, 4, 8) if block % u == 0)

    def rows(step, carry):
        start = step * group

        def add(j, totals):
            row = right[j]
            return tuple(
                total + left[start + q, pl.ds(j, 1), :] * row for q, total in enumerate(totals)
            )

        zero = jnp.zeros(right.shape[1:], jnp.float32)
        totals = lax.fori_loop(0, block, add, (zero,) * group, unroll=unroll)
        for q, total in enumerate(totals):
            out[start + q] = total
        return carry

    lax.fori_loop(0, block // group, rows, 0)


def on_last(body):
    pl.when(lax.axis_index("line") == lax.axis_size("line") - 1)(body)


def factor_kernel(lower, pivot, after, factor, out):
    def body():
        multiply_lines(lower.at[0], pivot.at[0], factor)
        multiply_lines(factor, lower.at[1], out)

    on_last(body)


def response_kernel(factor, given, upper, pivot, after, out, work):
    def body():
        multiply_lines(given, pivot.at[1], out)
        multiply_lines(out, upper.at[0], work)
        multiply_lines(work, pivot.at[0], out)

        def row(i, carry):
            out[i] = out[i] + factor[i]
            return carry

        lax.fori_loop(0, out.shape[0], row, 0, unroll=4)

    on_last(body)


def alone_kernel(forward, upper, pivot, outgoing, result, coupled):
    run_up(forward, upper, pivot, None, result, coupled)
    outgoing[...] = result[0]


def short_turn_kernel(parts, vector, lower, pivot, upper, response, alone, last, *refs):
    carried_in = refs[:parts]
    carried, message, upward, outgoing, forward, entry, work, result, coupled = refs[parts:]
    add_up(carried_in, carried)
    set_entry(carried, entry)
    run_down(vector, lower, pivot, entry, forward, work)
    message[0] = forward[forward.shape[0] - 1]
    message[1] = last[...]
    entry[...] = message[1] - message[0]
    upward[...] = alone[...] + apply_turned(response, entry)
    run_up(forward, upper, pivot, upward, result, coupled)
    outgoing[...] = result[0]


def forward_kernel(parts, vector, lower, pivot, *refs):
    carried_in = refs[:parts]
    carried, forward, entry, work = refs[parts:]
    add_up(carried_in, carried)
    set_entry(carried, entry)
    run_down(vector, lower, pivot, entry, forward, work)


def own_kernel(vector, carried, lower, diag_block, direction, coupled, whole, image):
    for k in range(vector.shape[0]):
        value = vector[k]
        if k == 0 and carried.shape[0] == 2:
            value = value + apply_turned(lower.at[0], carried.at[1])
        whole[k] = value
        value = coupled[k] - value + apply_turned(diag_block.at[k], direction.at[k])
        if k > 0:
            value = value + apply_turned(lower.at[k], direction.at[k - 1])
        image[k] = value


def near_kernel(image, near_block, near, *refs):
    *below, out = refs
    for k in range(image.shape[0]):
        out[k] = image[k] + apply_turned(near_block.at[k], near.at[k])
    if below:
        out[0] = out[0] + apply_turned(below[0].at[0], below[1])


def next_kernel(image, far_block, far, lower, pivot, last, out, message, forward, work):
    for k in range(image.shape[0]):
        out[k] = image[k] + apply_turned(far_block.at[k], far.at[k])
    run_down(out, lower, pivot, None, forward, work)
    message[0] = forward[forward.shape[0] - 1]
    message[1] = last[...]


def place_of(pair):
    low, high = sorted(pair)
    return high * (high + 1) // 2 + low


def pair_sum(left, right):
    total = left[0] * right[0]
    for k in range(1, left.shape[0]):
        total = total + left[k] * right[k]
    return jnp.sum(total, axis=0, keepdims=True)


def sums_kernel(*refs):
    *basis, out = refs
    row = lax.broadcasted_iota(jnp.int32, out.shape, 0)
    sums = jnp.zeros(out.shape, jnp.float32)
    for i in range(len(basis)):
        for j in range(i, len(basis)):
            sums = jnp.where(row == place_of((i, j)), pair_sum(basis[i], basis[j]), sums)
    out[...] = sums


def last_kernel(image, far_block, far, sums_in, *refs):
    *basis, out, newest = refs
    for k in range(image.shape[0]):
        newest[k] = image[k] + apply_turned(far_block.at[k], far.at[k])
    sums = sums_in[...]
    row = lax.broadcasted_iota(jnp.int32, sums.shape, 0)
    lane = lax.broadcasted_iota(jnp.int32, sums.shape, 1)
    high = len(basis)
    for i, member in enumerate((*basis, newest)):
        sums = jnp.where(row == place_of((i, high)), pair_sum(member, newest), sums)
    whole = jnp.sum(sums, axis=1, keepdims=True)
    sums = jnp.sum(jnp.where(lane == row, whole, 0.0), axis=0, keepdims=True)
    out[...] = jnp.broadcast_to(sums, out.shape)


def finish_kernel(parts_ref, *refs):
    directions, out = refs[:-1], refs[-1]
    width = len(directions)
    total = jnp.sum(parts_ref[...], axis=0, keepdims=True)
    shape = (SUMS, total.shape[1])
    row = lax.broadcasted_iota(jnp.int32, shape, 0)
    lane = lax.broadcasted_iota(jnp.int32, shape, 1)
    sums = jnp.sum(jnp.where(lane == row, total, 0.0), axis=1, keepdims=True)
    sums = jnp.broadcast_to(sums, shape)
    gram = {}
    for i in range(width + 1):
        for j in range(width + 1):
            place = place_of((i, j))
            gram[i, j] = sums[place : place + 1]
    half = [[gram[j + 1, i] + gram[j, i] for i in range(width + 1)] for j in range(width)]
    normal = [[half[j][i + 1] + half[j][i] for i in range(width)] for j in range(width)]
    right = [half[j][0] for j in range(width)]
    for i in range(width):
        inverse = 1.0 / normal[i][i]
        for j in range(i + 1, width):
            factor = normal[j][i] * inverse
            for k in range(i, width):
                normal[j][k] = normal[j][k] - factor * normal[i][k]
            right[j] = right[j] - factor * right[i]
    coeffs = [None] * width
    for i in reversed(range(width)):
        value = right[i]
        for k in range(i + 1, width):
            value = value - normal[i][k] * coeffs[k]
        coeffs[i] = value / normal[i][i]
    for k in range(out.shape[0]):
        step = coeffs[0] * directions[0][k]
        for j in range(1, width):
            step = step + coeffs[j] * directions[j][k]
        out[k] = step


def rows_beside(field, across):
    count = lax.axis_size("patch")
    even = [(i, i + 1) for i in range(0, count - 1, 2)]
    odd = [(i, i + 1) for i in range(1, count - 1, 2)]
    is_even = lax.axis_index("patch") % 2 == 0
    first, last = field[..., :across], field[..., -across:]
    several = field.shape[-1] > across
    to_far = jnp.where(is_even, first, last) if several else field
    to_near = jnp.where(is_even, last, first) if several else field
    far = lax.ppermute(to_far, "patch", odd + [(b, a) for a, b in odd])
    near = lax.ppermute(to_near, "patch", even + [(b, a) for a, b in even])
    if several:
        up = [jnp.concatenate([field[..., across:], row], axis=-1) for row in (near, far)]
        down = [jnp.concatenate([row, field[..., :-across]], axis=-1) for row in (near, far)]
        near = jnp.where(is_even, up[0], down[0])
        far = jnp.where(is_even, down[1], up[1])
    return near, far


def sweep_short(vector, message, alone_forward, last, lower, pivot, upper, response):
    line = lax.axis_size("line")
    field, one = vector.shape, last.shape
    parts = []
    for turn in range(line - 2):
        parts.append(lax.ppermute(message, "line", [(turn, turn + 1)]))
        if turn == 0:
            (alone,) = stage(
                alone_kernel, [one], [alone_forward, upper, pivot], [field, field]
            )
            alone = lax.ppermute(alone, "line", [(line - 1, line - 2)])
        if turn < line - 3:
            carried, message = stage(
                functools.partial(hop_down_kernel, len(parts), True),
                [message.shape, message.shape],
                [vector, lower, pivot, *parts, last],
                [one, field, one],
            )
            parts = [carried]
    carried_down, message, upward, outgoing, forward = stage(
        functools.partial(short_turn_kernel, len(parts)),
        [message.shape, message.shape, one, one, field],
        [vector, lower, pivot, upper, response, alone, last, *parts],
        [one, one, field, field],
    )
    parts = [upward]
    for turn in reversed(range(line - 2)):
        if turn == 0:
            outgoing, message = lax.optimization_barrier((outgoing, message))
        parts.append(lax.ppermute(outgoing, "line", [(turn + 1, turn)]))
        if turn == 0:
            onward = lax.ppermute(message, "line", [(line - 2, line - 1)])
            carried_down, whole_forward = stage(
                functools.partial(forward_kernel, 2),
                [message.shape, field],
                [vector, lower, pivot, carried_down, onward],
                [one, one],
            )
        if turn > 0:
            carried, outgoing = stage(
                functools.partial(hop_up_kernel, len(parts)),
                [one, one],
                [forward, upper, pivot, *parts],
                [field, field],
            )
            parts = [carried]
    return carried_down, whole_forward, parts


def per_device(newton_residual, diag_block, lower, upper, west, east, pivot_inverse):
    shape = newton_residual.shape
    count, block, rows, across = shape
    wide = rows * across

    def flat(matrix):
        return matrix.reshape(count, block, block, wide)

    diag_block, lower, upper, west, east, pivot = map(
        flat, (diag_block, lower, upper, west, east, pivot_inverse)
    )
    line = lax.axis_size("line")
    devices = line * lax.axis_size("patch")
    one, field = (block, wide), (count, block, wide)
    vector = newton_residual.reshape(field)
    lower, pivot, message = first_carry(vector, lower, pivot)
    lower, pivot = turn_held(lower, pivot)
    basis = []
    directions = []
    last = None
    short = line > 2 and count == 2
    for j in range(ITERS):
        if j >= 2 and short:
            carried_down, forward, parts = sweep_short(
                vector, message, alone_forward, last, lower, pivot, upper, response
            )
        else:
            parts = []
            for turn in range(line - 1):
                parts.append(lax.ppermute(message, "line", [(turn, turn + 1)]))
                if j == 0 and turn == 0:
                    (upper,) = load((upper,), message)
                if j == 0 and turn == line - 2 and short:
                    factor, response = stage(
                        factor_kernel, [(block,) + one] * 2, [lower, pivot, message]
                    )
                if turn < line - 2:
                    lasts = [] if last is None else [last]
                    carried, message = stage(
                        functools.partial(hop_down_kernel, len(parts), bool(lasts)),
                        [message.shape, message.shape],
                        [vector, lower, pivot, *parts, *lasts],
                        [one, field, one],
                    )
                    parts = [carried]
            parts = parts or [jnp.zeros_like(message)]
            carried_down, forward, outgoing = stage(
                functools.partial(turn_kernel, len(parts)),
                [message.shape, field, one],
                [vector, lower, pivot, upper, *parts],
                [one, one, field, field],
            )
            if j == 0 and short:
                outgoing, response = lax.optimization_barrier((outgoing, response))
            parts = []
            for turn in reversed(range(line - 1)):
                if j == 1 and turn == line - 3 and short:
                    outgoing, ready = lax.optimization_barrier((outgoing, response))
                    response = lax.ppermute(ready, "line", [(line - 1, line - 2)])
                parts.append(lax.ppermute(outgoing, "line", [(turn + 1, turn)]))
                if j == 0 and turn == line - 2:
                    diag_block, near_block, far_block = load(
                        (diag_block, east, west), outgoing, True
                    )
                if j == 0 and turn == line - 3 and short:
                    (response,) = stage(
                        response_kernel,
                        [(block,) + one],
                        [factor, response, upper, pivot, outgoing],
                        [(block,) + one],
                    )
                if turn > 0:
                    carried, outgoing = stage(
                        functools.partial(hop_up_kernel, len(parts)),
                        [one, one],
                        [forward, upper, pivot, *parts],
                        [field, field],
                    )
                    parts = [carried]
            parts = parts or [jnp.zeros_like(outgoing)]
        direction, coupled, last = stage(
            functools.partial(end_kernel, len(parts)),
            [field, field, one],
            [forward, upper, pivot, *parts],
            [one],
        )
        directions.append(direction)
        near, far = rows_beside(direction, across)
        whole, image = stage(
            own_kernel,
            [field, field],
            [vector, carried_down, lower, diag_block, direction, coupled],
        )
        basis.append(whole)
        beneath = []
        if j == ITERS - 1:
            (sums,) = stage(sums_kernel, [(SUMS, wide)], basis)
            below = lax.ppermute(last, "line", [(i, i + 1) for i in range(line - 1)])
            beneath = [lower, below]
        (image,) = stage(near_kernel, [field], [image, near_block, near, *beneath])
        if j < ITERS - 1:
            vector, message, alone_forward = stage(
                next_kernel,
                [field, (2,) + one, field],
                [image, far_block, far, lower, pivot, last],
                [one],
            )
            if j == 0 and short:
                message, response = lax.optimization_barrier((message, response))
        else:
            (sums,) = stage(
                last_kernel,
                [(devices, wide)],
                [image, far_block, far, sums, *basis],
                [field],
            )
    sums = lax.all_to_all(sums, ("line", "patch"), 0, 0, tiled=True)
    (step,) = stage(finish_kernel, [field], [sums, *directions])
    return step.reshape(shape)


def solution(mesh):
    blocks = P("line", None, None, "patch", None)
    field = P("line", None, "patch", None)
    return jax.shard_map(
        per_device, mesh=mesh, in_specs=(field,) + (blocks,) * 6, out_specs=field, check_vma=False
    )
```

```python
import functools

import jax
import jax.numpy as jnp
from jax import lax
from jax.experimental import pallas as pl
from jax.experimental.pallas import tpu as pltpu
from jax.sharding import PartitionSpec as P

ITERS = 4
SUMS = 16
FETCH_ROOM = 56 << 20
LOAD_ROOM = 40 << 20
STAGE_ROOM = 16 << 20


def start_all(pairs, sems):
    copies = [
        pltpu.make_async_copy(source, target, sems.at[place])
        for place, (source, target) in enumerate(pairs)
    ]
    for copy in copies:
        copy.start()
    return copies


def turn_over(source, target):
    block = source.shape[0]
    high = 16 if block % 16 == 0 else block
    wide = 8 if block % 8 == 0 else block
    for i in range(0, block, wide):
        for j in range(0, block, high):
            part = source[i : i + wide, j : j + high].astype(jnp.float32)
            target[j : j + high, i : i + wide] = jnp.swapaxes(part, 0, 1)


def apply_plain(block_mat, value, target):
    block = target.shape[0]
    rows = 16 if block % 16 == 0 else block
    for start in range(0, block, rows):
        part = block_mat[start : start + rows].astype(jnp.float32)
        target[start : start + rows] = jnp.sum(part * value[None], axis=1)


def apply_turned(block_mat, vector):
    totals = [None, None]
    for j in range(block_mat.shape[0]):
        term = block_mat[j] * vector[j : j + 1]
        totals[j % 2] = term if totals[j % 2] is None else totals[j % 2] + term
    return totals[0] + totals[1]


def first_kernel(vector, lower, pivot, lower_held, pivot_held, out, field, middle, sems):
    count = vector.shape[0]
    pairs = [(vector, field), (pivot.at[0], pivot_held.at[0])]
    for k in range(1, count):
        pairs += [(lower.at[k], lower_held.at[k]), (pivot.at[k], pivot_held.at[k])]
    pairs.append((lower.at[0], lower_held.at[0]))
    copies = start_all(pairs, sems)
    copies[0].wait()
    copies[1].wait()
    apply_plain(pivot_held.at[0], field[0], out.at[0])
    for k in range(1, count):
        copies[2 * k].wait()
        apply_plain(lower_held.at[k], out[0], middle)
        copies[2 * k + 1].wait()
        apply_plain(pivot_held.at[k], field[k] - middle[...], out.at[0])
    copies[-1].wait()


def first_carry(vector, lower, pivot):
    count, block, wide = vector.shape
    return pl.pallas_call(
        first_kernel,
        out_shape=[
            pltpu.VMEM(lower.shape, lower.dtype),
            pltpu.VMEM(pivot.shape, pivot.dtype),
            pltpu.VMEM((1, block, wide), jnp.float32),
        ],
        in_specs=[pl.BlockSpec(memory_space=pl.ANY)] * 3,
        out_specs=[pl.BlockSpec(memory_space=pltpu.VMEM)] * 3,
        scratch_shapes=[
            pltpu.VMEM(vector.shape, jnp.float32),
            pltpu.VMEM((block, wide), jnp.float32),
            pltpu.SemaphoreType.DMA((1 + 2 * count,)),
        ],
        compiler_params=pltpu.CompilerParams(vmem_limit_bytes=FETCH_ROOM),
    )(vector, lower, pivot)


def turn_held_kernel(*refs):
    half = len(refs) // 2
    for source, target in zip(refs[:half], refs[half:]):
        for k in range(source.shape[0]):
            turn_over(source.at[k], target.at[k])


def turn_held(*blocks):
    vmem = pl.BlockSpec(memory_space=pltpu.VMEM)
    return pl.pallas_call(
        turn_held_kernel,
        out_shape=[pltpu.VMEM(block.shape, jnp.float32) for block in blocks],
        in_specs=[vmem] * len(blocks),
        out_specs=[vmem] * len(blocks),
        compiler_params=pltpu.CompilerParams(vmem_limit_bytes=STAGE_ROOM),
    )(*blocks)


def load_kernel(choose, *refs):
    *refs, held, sems = refs
    size = (len(refs) - 1) // 2
    sources, targets = refs[:size], refs[size + 1 :]

    def run(sources):
        copies = start_all([(s, held.at[place]) for place, s in enumerate(sources)], sems)
        for place, target in enumerate(targets):
            copies[place].wait()
            for k in range(target.shape[0]):
                turn_over(held.at[place, k], target.at[k])

    if choose:
        even = lax.axis_index("patch") % 2 == 0
        pl.when(even)(lambda: run(sources))
        pl.when(jnp.logical_not(even))(lambda: run((*sources[:-2], sources[-1], sources[-2])))
    else:
        run(sources)


def load(blocks, after, choose=False):
    shape = blocks[0].shape
    return pl.pallas_call(
        functools.partial(load_kernel, choose),
        out_shape=[pltpu.VMEM(shape, jnp.float32) for block in blocks],
        in_specs=[pl.BlockSpec(memory_space=pl.ANY)] * (len(blocks) + 1),
        out_specs=[pl.BlockSpec(memory_space=pltpu.VMEM)] * len(blocks),
        scratch_shapes=[
            pltpu.VMEM((len(blocks),) + shape, blocks[0].dtype),
            pltpu.SemaphoreType.DMA((len(blocks),)),
        ],
        compiler_params=pltpu.CompilerParams(vmem_limit_bytes=LOAD_ROOM),
    )(*blocks, after)


def stage(kernel, out_shapes, operands, scratch=()):
    vmem = pl.BlockSpec(memory_space=pltpu.VMEM)
    return pl.pallas_call(
        kernel,
        out_shape=[pltpu.VMEM(shape, jnp.float32) for shape in out_shapes],
        in_specs=[vmem] * len(operands),
        out_specs=[vmem] * len(out_shapes),
        scratch_shapes=[pltpu.VMEM(shape, jnp.float32) for shape in scratch],
        compiler_params=pltpu.CompilerParams(vmem_limit_bytes=STAGE_ROOM),
    )(*operands)


def run_down(vector, lower, pivot, entry, forward, work):
    for k in range(vector.shape[0]):
        if k > 0:
            work[...] = vector[k] - apply_turned(lower.at[k], forward.at[k - 1])
        elif entry is not None:
            work[...] = vector[k] + apply_turned(lower.at[k], entry)
        else:
            work[...] = vector[k]
        forward[k] = apply_turned(pivot.at[k], work)


def run_up(forward, upper, pivot, incoming, result, coupled):
    count = forward.shape[0]
    for k in reversed(range(count)):
        following = result.at[k + 1] if k < count - 1 else incoming
        if following is None:
            result[k] = forward[k]
        else:
            coupled[k] = apply_turned(upper.at[k], following)
            result[k] = forward[k] - apply_turned(pivot.at[k], coupled.at[k])


def add_up(parts, target):
    total = parts[0][...]
    for part in parts[1:]:
        total = total + part[...]
    target[...] = total


def set_entry(carried, entry):
    both = carried.shape[0] == 2
    entry[...] = carried[1] - carried[0] if both else -carried[0]


def hop_down_kernel(parts, has_last, vector, lower, pivot, *refs):
    carried_in, refs = refs[:parts], refs[parts:]
    if has_last:
        last, *refs = refs
    carried, message, forward, entry, work = refs
    add_up(carried_in, carried)
    set_entry(carried, entry)
    run_down(vector, lower, pivot, entry, forward, work)
    message[0] = forward[forward.shape[0] - 1]
    if has_last:
        message[1] = last[...]


def turn_kernel(parts, vector, lower, pivot, upper, *refs):
    carried_in = refs[:parts]
    carried, forward, outgoing, entry, work, result, coupled = refs[parts:]
    add_up(carried_in, carried)
    set_entry(carried, entry)
    run_down(vector, lower, pivot, entry, forward, work)
    run_up(forward, upper, pivot, None, result, coupled)
    outgoing[...] = result[0]


def hop_up_kernel(parts, forward, upper, pivot, *refs):
    carried_in = refs[:parts]
    carried, outgoing, result, coupled = refs[parts:]
    add_up(carried_in, carried)
    run_up(forward, upper, pivot, carried, result, coupled)
    outgoing[...] = result[0]


def end_kernel(parts, forward, upper, pivot, *refs):
    carried_in = refs[:parts]
    result, coupled, last, carried = refs[parts:]
    add_up(carried_in, carried)
    run_up(forward, upper, pivot, carried, result, coupled)
    last[...] = result[result.shape[0] - 1]


def multiply_lines(left, right, out):
    block = right.shape[0]
    group = max(g for g in (1, 2, 3, 4) if block % g == 0)
    unroll = max(u for u in (1, 2, 4, 8) if block % u == 0)

    def rows(step, carry):
        start = step * group

        def add(j, totals):
            row = right[j]
            return tuple(
                total + left[start + q, pl.ds(j, 1), :] * row for q, total in enumerate(totals)
            )

        zero = jnp.zeros(right.shape[1:], jnp.float32)
        totals = lax.fori_loop(0, block, add, (zero,) * group, unroll=unroll)
        for q, total in enumerate(totals):
            out[start + q] = total
        return carry

    lax.fori_loop(0, block // group, rows, 0)


def on_last(body):
    pl.when(lax.axis_index("line") == lax.axis_size("line") - 1)(body)


def on_second(body):
    pl.when(lax.axis_index("line") == 1)(body)


def up_factor_kernel(upper, pivot, after, out):
    on_second(lambda: multiply_lines(upper.at[1], pivot.at[1], out))


def up_product_kernel(given, upper, pivot, after, first, second, work, made):
    def body():
        multiply_lines(given, upper.at[0], work)
        multiply_lines(work, pivot.at[0], made)
        size = first.shape[0]
        first[...] = made[:size]
        second[...] = made[size:]

    on_second(body)


def factor_kernel(lower, pivot, after, factor, out):
    def body():
        multiply_lines(lower.at[0], pivot.at[0], factor)
        multiply_lines(factor, lower.at[1], out)

    on_last(body)


def response_kernel(factor, given, upper, pivot, after, out, work):
    def body():
        multiply_lines(given, pivot.at[1], out)
        multiply_lines(out, upper.at[0], work)
        multiply_lines(work, pivot.at[0], out)

        def row(i, carry):
            out[i] = out[i] + factor[i]
            return carry

        lax.fori_loop(0, out.shape[0], row, 0, unroll=4)

    on_last(body)


def alone_kernel(forward, upper, pivot, outgoing, result, coupled):
    run_up(forward, upper, pivot, None, result, coupled)
    outgoing[...] = result[0]


def short_turn_kernel(
    vector, lower, pivot, upper, response, alone, message, carried_in, received,
    carried, passed, upward, to_second, to_first, forward, entry, work, result, coupled,
):
    carried[...] = carried_in[...] + received[...]
    set_entry(carried, entry)
    run_down(vector, lower, pivot, entry, forward, work)
    passed[...] = forward[forward.shape[0] - 1]
    entry[...] = message[0] - passed[...]
    upward[...] = alone[...] + apply_turned(response, entry)
    run_up(forward, upper, pivot, upward, result, coupled)
    to_second[...] = result[0]
    to_first[...] = result[0]


def short_end_kernel(
    beside, beyond, onward, vector, lower, pivot, upper, forward_in, carried, first, second, upward,
    result, coupled, last, forward, entry, work,
):
    forward[...] = forward_in[...]

    def again():
        entry[...] = carried[1] - onward[...]
        run_down(vector, lower, pivot, entry, forward, work)

    on_last(again)
    size = first.shape[0]
    through = apply_turned(first, beyond.at[:size]) + apply_turned(second, beyond.at[size:])
    entry[...] = upward[...] + beside[...] + through
    run_up(forward, upper, pivot, entry, result, coupled)
    last[...] = result[result.shape[0] - 1]


def own_kernel(vector, carried, lower, diag_block, direction, coupled, whole, image):
    for k in range(vector.shape[0]):
        value = vector[k]
        if k == 0 and carried.shape[0] == 2:
            value = value + apply_turned(lower.at[0], carried.at[1])
        whole[k] = value
        value = coupled[k] - value + apply_turned(diag_block.at[k], direction.at[k])
        if k > 0:
            value = value + apply_turned(lower.at[k], direction.at[k - 1])
        image[k] = value


def near_kernel(image, near_block, near, *refs):
    *below, out = refs
    for k in range(image.shape[0]):
        out[k] = image[k] + apply_turned(near_block.at[k], near.at[k])
    if below:
        out[0] = out[0] + apply_turned(below[0].at[0], below[1])


def next_kernel(image, far_block, far, lower, pivot, last, out, message, forward, work):
    for k in range(image.shape[0]):
        out[k] = image[k] + apply_turned(far_block.at[k], far.at[k])
    run_down(out, lower, pivot, None, forward, work)
    message[0] = forward[forward.shape[0] - 1]
    message[1] = last[...]


def place_of(pair):
    low, high = sorted(pair)
    return high * (high + 1) // 2 + low


def pair_sum(left, right):
    total = left[0] * right[0]
    for k in range(1, left.shape[0]):
        total = total + left[k] * right[k]
    return jnp.sum(total, axis=0, keepdims=True)


def sums_kernel(*refs):
    *basis, out = refs
    row = lax.broadcasted_iota(jnp.int32, out.shape, 0)
    sums = jnp.zeros(out.shape, jnp.float32)
    for i in range(len(basis)):
        for j in range(i, len(basis)):
            sums = jnp.where(row == place_of((i, j)), pair_sum(basis[i], basis[j]), sums)
    out[...] = sums


def last_kernel(image, far_block, far, sums_in, *refs):
    *basis, out, newest = refs
    for k in range(image.shape[0]):
        newest[k] = image[k] + apply_turned(far_block.at[k], far.at[k])
    sums = sums_in[...]
    row = lax.broadcasted_iota(jnp.int32, sums.shape, 0)
    lane = lax.broadcasted_iota(jnp.int32, sums.shape, 1)
    high = len(basis)
    for i, member in enumerate((*basis, newest)):
        sums = jnp.where(row == place_of((i, high)), pair_sum(member, newest), sums)
    whole = jnp.sum(sums, axis=1, keepdims=True)
    sums = jnp.sum(jnp.where(lane == row, whole, 0.0), axis=0, keepdims=True)
    out[...] = jnp.broadcast_to(sums, out.shape)


def finish_kernel(parts_ref, *refs):
    directions, out = refs[:-1], refs[-1]
    width = len(directions)
    total = jnp.sum(parts_ref[...], axis=0, keepdims=True)
    shape = (SUMS, total.shape[1])
    row = lax.broadcasted_iota(jnp.int32, shape, 0)
    lane = lax.broadcasted_iota(jnp.int32, shape, 1)
    sums = jnp.sum(jnp.where(lane == row, total, 0.0), axis=1, keepdims=True)
    sums = jnp.broadcast_to(sums, shape)
    gram = {}
    for i in range(width + 1):
        for j in range(width + 1):
            place = place_of((i, j))
            gram[i, j] = sums[place : place + 1]
    half = [[gram[j + 1, i] + gram[j, i] for i in range(width + 1)] for j in range(width)]
    normal = [[half[j][i + 1] + half[j][i] for i in range(width)] for j in range(width)]
    right = [half[j][0] for j in range(width)]
    for i in range(width):
        inverse = 1.0 / normal[i][i]
        for j in range(i + 1, width):
            factor = normal[j][i] * inverse
            for k in range(i, width):
                normal[j][k] = normal[j][k] - factor * normal[i][k]
            right[j] = right[j] - factor * right[i]
    coeffs = [None] * width
    for i in reversed(range(width)):
        value = right[i]
        for k in range(i + 1, width):
            value = value - normal[i][k] * coeffs[k]
        coeffs[i] = value / normal[i][i]
    for k in range(out.shape[0]):
        step = coeffs[0] * directions[0][k]
        for j in range(1, width):
            step = step + coeffs[j] * directions[j][k]
        out[k] = step


def rows_beside(field, across):
    count = lax.axis_size("patch")
    even = [(i, i + 1) for i in range(0, count - 1, 2)]
    odd = [(i, i + 1) for i in range(1, count - 1, 2)]
    is_even = lax.axis_index("patch") % 2 == 0
    first, last = field[..., :across], field[..., -across:]
    several = field.shape[-1] > across
    to_far = jnp.where(is_even, first, last) if several else field
    to_near = jnp.where(is_even, last, first) if several else field
    far = lax.ppermute(to_far, "patch", odd + [(b, a) for a, b in odd])
    near = lax.ppermute(to_near, "patch", even + [(b, a) for a, b in even])
    if several:
        up = [jnp.concatenate([field[..., across:], row], axis=-1) for row in (near, far)]
        down = [jnp.concatenate([row, field[..., :-across]], axis=-1) for row in (near, far)]
        near = jnp.where(is_even, up[0], down[0])
        far = jnp.where(is_even, down[1], up[1])
    return near, far


def sweep_short(vector, message, last, lower, pivot, upper, response, product):
    field, one = vector.shape, last.shape
    received = lax.ppermute(message, "line", [(0, 1), (2, 3)])
    carried, onto, forward = stage(
        functools.partial(hop_down_kernel, 1, True),
        [message.shape, message.shape, field],
        [vector, lower, pivot, received, last],
        [one, one],
    )
    received = lax.ppermute(onto, "line", [(1, 2)])
    (alone,) = stage(alone_kernel, [one], [forward, upper, pivot], [field, field])
    alone = lax.ppermute(alone, "line", [(3, 2), (1, 0)])
    carried, passed, upward, to_second, to_first, forward = stage(
        short_turn_kernel,
        [message.shape, one, one, one, one, field],
        [vector, lower, pivot, upper, response, alone, message, carried, received],
        [one, one, field, field],
    )
    beside = lax.ppermute(to_second, "line", [(2, 1)])
    beyond = lax.ppermute(to_first, "line", [(2, 0)])
    onward = lax.ppermute(passed, "line", [(2, 3)])
    direction, coupled, last = stage(
        short_end_kernel,
        [field, field, one],
        [beside, beyond, onward, vector, lower, pivot, upper, forward, carried, *product, upward],
        [field, one, one],
    )
    return direction, coupled, last, carried


def per_device(newton_residual, diag_block, lower, upper, west, east, pivot_inverse):
    shape = newton_residual.shape
    count, block, rows, across = shape
    wide = rows * across

    def flat(matrix):
        return matrix.reshape(count, block, block, wide)

    diag_block, lower, upper, west, east, pivot = map(
        flat, (diag_block, lower, upper, west, east, pivot_inverse)
    )
    line = lax.axis_size("line")
    devices = line * lax.axis_size("patch")
    one, field = (block, wide), (count, block, wide)
    vector = newton_residual.reshape(field)
    lower, pivot, message = first_carry(vector, lower, pivot)
    lower, pivot = turn_held(lower, pivot)
    basis = []
    directions = []
    last = None
    short = line == 4 and count == 2
    third = block // 3
    for j in range(ITERS):
        if j >= 2 and short:
            direction, coupled, last, carried_down = sweep_short(
                vector, message, last, lower, pivot, upper, response, up_product
            )
        else:
            parts = []
            for turn in range(line - 1):
                if j == 1 and turn == 2 and short:
                    message, rest = lax.optimization_barrier((message, up_product[1]))
                    up_product[1] = lax.ppermute(rest, "line", [(1, 0)])
                parts.append(lax.ppermute(message, "line", [(turn, turn + 1)]))
                if j == 0 and turn == 0:
                    (upper,) = load((upper,), message)
                if j == 0 and turn == line - 2 and short:
                    factor, response = stage(
                        factor_kernel, [(block,) + one] * 2, [lower, pivot, message]
                    )
                    (up_factor,) = stage(
                        up_factor_kernel, [(block,) + one], [upper, pivot, message]
                    )
                if turn < line - 2:
                    lasts = [] if last is None else [last]
                    carried, message, _ = stage(
                        functools.partial(hop_down_kernel, len(parts), bool(lasts)),
                        [message.shape, message.shape, field],
                        [vector, lower, pivot, *parts, *lasts],
                        [one, one],
                    )
                    parts = [carried]
            parts = parts or [jnp.zeros_like(message)]
            carried_down, forward, outgoing = stage(
                functools.partial(turn_kernel, len(parts)),
                [message.shape, field, one],
                [vector, lower, pivot, upper, *parts],
                [one, one, field, field],
            )
            if j == 0 and short:
                outgoing, response, up_factor = lax.optimization_barrier(
                    (outgoing, response, up_factor)
                )
            parts = []
            for turn in reversed(range(line - 1)):
                if j == 1 and turn == line - 3 and short:
                    outgoing, ready = lax.optimization_barrier((outgoing, response))
                    response = lax.ppermute(ready, "line", [(line - 1, line - 2)])
                if j == 1 and turn == 0 and short:
                    outgoing, up_product[1] = lax.optimization_barrier(
                        (outgoing, up_product[1])
                    )
                parts.append(lax.ppermute(outgoing, "line", [(turn + 1, turn)]))
                if j == 0 and turn == line - 2:
                    diag_block, near_block, far_block = load(
                        (diag_block, east, west), outgoing, True
                    )
                if j == 0 and turn == line - 3 and short:
                    up_product = stage(
                        up_product_kernel,
                        [(third,) + one, (block - third,) + one],
                        [up_factor, upper, pivot, outgoing],
                        [(block,) + one] * 2,
                    )
                    (response,) = stage(
                        response_kernel,
                        [(block,) + one],
                        [factor, response, upper, pivot, outgoing],
                        [(block,) + one],
                    )
                if turn > 0:
                    carried, outgoing = stage(
                        functools.partial(hop_up_kernel, len(parts)),
                        [one, one],
                        [forward, upper, pivot, *parts],
                        [field, field],
                    )
                    parts = [carried]
                    if j == 0 and turn == line - 3 and short:
                        outgoing, *up_product = lax.optimization_barrier(
                            (outgoing, *up_product)
                        )
            parts = parts or [jnp.zeros_like(outgoing)]
            direction, coupled, last = stage(
                functools.partial(end_kernel, len(parts)),
                [field, field, one],
                [forward, upper, pivot, *parts],
                [one],
            )
        directions.append(direction)
        if j == 1 and short:
            direction, part = lax.optimization_barrier((direction, up_product[0]))
            up_product[0] = lax.ppermute(part, "line", [(1, 0)])
        near, far = rows_beside(direction, across)
        whole, image = stage(
            own_kernel,
            [field, field],
            [vector, carried_down, lower, diag_block, direction, coupled],
        )
        basis.append(whole)
        beneath = []
        if j == ITERS - 1:
            (sums,) = stage(sums_kernel, [(SUMS, wide)], basis)
            below = lax.ppermute(last, "line", [(i, i + 1) for i in range(line - 1)])
            beneath = [lower, below]
        (image,) = stage(near_kernel, [field], [image, near_block, near, *beneath])
        if j < ITERS - 1:
            vector, message = stage(
                next_kernel,
                [field, (2,) + one],
                [image, far_block, far, lower, pivot, last],
                [field, one],
            )
            if j == 0 and short:
                message, response = lax.optimization_barrier((message, response))
        else:
            (sums,) = stage(
                last_kernel,
                [(devices, wide)],
                [image, far_block, far, sums, *basis],
                [field],
            )
    sums = lax.all_to_all(sums, ("line", "patch"), 0, 0, tiled=True)
    (step,) = stage(finish_kernel, [field], [sums, *directions])
    return step.reshape(shape)


def solution(mesh):
    blocks = P("line", None, None, "patch", None)
    field = P("line", None, "patch", None)
    return jax.shard_map(
        per_device, mesh=mesh, in_specs=(field,) + (blocks,) * 6, out_specs=field, check_vma=False
    )
```

```python
import functools

import jax
import jax.numpy as jnp
from jax import lax
from jax.experimental import pallas as pl
from jax.experimental.pallas import tpu as pltpu
from jax.sharding import PartitionSpec as P

ITERS = 4
SUMS = 16
FETCH_ROOM = 56 << 20
LOAD_ROOM = 40 << 20
STAGE_ROOM = 16 << 20


def start_all(pairs, sems):
    copies = [
        pltpu.make_async_copy(source, target, sems.at[place])
        for place, (source, target) in enumerate(pairs)
    ]
    for copy in copies:
        copy.start()
    return copies


def turn_over(source, target):
    block = source.shape[0]
    high = 16 if block % 16 == 0 else block
    wide = 8 if block % 8 == 0 else block
    for i in range(0, block, wide):
        for j in range(0, block, high):
            part = source[i : i + wide, j : j + high].astype(jnp.float32)
            target[j : j + high, i : i + wide] = jnp.swapaxes(part, 0, 1)


def apply_plain(block_mat, value, target):
    block = target.shape[0]
    rows = 16 if block % 16 == 0 else block
    for start in range(0, block, rows):
        part = block_mat[start : start + rows].astype(jnp.float32)
        target[start : start + rows] = jnp.sum(part * value[None], axis=1)


def apply_turned(block_mat, vector):
    totals = [None, None]
    for j in range(block_mat.shape[0]):
        term = block_mat[j] * vector[j : j + 1]
        totals[j % 2] = term if totals[j % 2] is None else totals[j % 2] + term
    return totals[0] + totals[1]


def first_kernel(vector, lower, pivot, lower_held, pivot_held, out, field, middle, sems):
    count = vector.shape[0]
    pairs = [(vector, field), (pivot.at[0], pivot_held.at[0])]
    for k in range(1, count):
        pairs += [(lower.at[k], lower_held.at[k]), (pivot.at[k], pivot_held.at[k])]
    pairs.append((lower.at[0], lower_held.at[0]))
    copies = start_all(pairs, sems)
    copies[0].wait()
    copies[1].wait()
    apply_plain(pivot_held.at[0], field[0], out.at[0])
    for k in range(1, count):
        copies[2 * k].wait()
        apply_plain(lower_held.at[k], out[0], middle)
        copies[2 * k + 1].wait()
        apply_plain(pivot_held.at[k], field[k] - middle[...], out.at[0])
    copies[-1].wait()


def first_carry(vector, lower, pivot):
    count, block, wide = vector.shape
    return pl.pallas_call(
        first_kernel,
        out_shape=[
            pltpu.VMEM(lower.shape, lower.dtype),
            pltpu.VMEM(pivot.shape, pivot.dtype),
            pltpu.VMEM((1, block, wide), jnp.float32),
        ],
        in_specs=[pl.BlockSpec(memory_space=pl.ANY)] * 3,
        out_specs=[pl.BlockSpec(memory_space=pltpu.VMEM)] * 3,
        scratch_shapes=[
            pltpu.VMEM(vector.shape, jnp.float32),
            pltpu.VMEM((block, wide), jnp.float32),
            pltpu.SemaphoreType.DMA((1 + 2 * count,)),
        ],
        compiler_params=pltpu.CompilerParams(vmem_limit_bytes=FETCH_ROOM),
    )(vector, lower, pivot)


def turn_held_kernel(*refs):
    half = len(refs) // 2
    for source, target in zip(refs[:half], refs[half:]):
        for k in range(source.shape[0]):
            turn_over(source.at[k], target.at[k])


def turn_held(*blocks):
    vmem = pl.BlockSpec(memory_space=pltpu.VMEM)
    return pl.pallas_call(
        turn_held_kernel,
        out_shape=[pltpu.VMEM(block.shape, jnp.float32) for block in blocks],
        in_specs=[vmem] * len(blocks),
        out_specs=[vmem] * len(blocks),
        compiler_params=pltpu.CompilerParams(vmem_limit_bytes=STAGE_ROOM),
    )(*blocks)


def load_kernel(choose, *refs):
    *refs, held, sems = refs
    size = (len(refs) - 1) // 2
    sources, targets = refs[:size], refs[size + 1 :]

    def run(sources):
        copies = start_all([(s, held.at[place]) for place, s in enumerate(sources)], sems)
        for place, target in enumerate(targets):
            copies[place].wait()
            for k in range(target.shape[0]):
                turn_over(held.at[place, k], target.at[k])

    if choose:
        even = lax.axis_index("patch") % 2 == 0
        pl.when(even)(lambda: run(sources))
        pl.when(jnp.logical_not(even))(lambda: run((*sources[:-2], sources[-1], sources[-2])))
    else:
        run(sources)


def load(blocks, after, choose=False):
    shape = blocks[0].shape
    return pl.pallas_call(
        functools.partial(load_kernel, choose),
        out_shape=[pltpu.VMEM(shape, jnp.float32) for block in blocks],
        in_specs=[pl.BlockSpec(memory_space=pl.ANY)] * (len(blocks) + 1),
        out_specs=[pl.BlockSpec(memory_space=pltpu.VMEM)] * len(blocks),
        scratch_shapes=[
            pltpu.VMEM((len(blocks),) + shape, blocks[0].dtype),
            pltpu.SemaphoreType.DMA((len(blocks),)),
        ],
        compiler_params=pltpu.CompilerParams(vmem_limit_bytes=LOAD_ROOM),
    )(*blocks, after)


def stage(kernel, out_shapes, operands, scratch=()):
    vmem = pl.BlockSpec(memory_space=pltpu.VMEM)
    return pl.pallas_call(
        kernel,
        out_shape=[pltpu.VMEM(shape, jnp.float32) for shape in out_shapes],
        in_specs=[vmem] * len(operands),
        out_specs=[vmem] * len(out_shapes),
        scratch_shapes=[pltpu.VMEM(shape, jnp.float32) for shape in scratch],
        compiler_params=pltpu.CompilerParams(vmem_limit_bytes=STAGE_ROOM),
    )(*operands)


def run_down(vector, lower, pivot, entry, forward, work):
    for k in range(vector.shape[0]):
        if k > 0:
            work[...] = vector[k] - apply_turned(lower.at[k], forward.at[k - 1])
        elif entry is not None:
            work[...] = vector[k] + apply_turned(lower.at[k], entry)
        else:
            work[...] = vector[k]
        forward[k] = apply_turned(pivot.at[k], work)


def run_up(forward, upper, pivot, incoming, result, coupled):
    count = forward.shape[0]
    for k in reversed(range(count)):
        following = result.at[k + 1] if k < count - 1 else incoming
        if following is None:
            result[k] = forward[k]
        else:
            coupled[k] = apply_turned(upper.at[k], following)
            result[k] = forward[k] - apply_turned(pivot.at[k], coupled.at[k])


def add_up(parts, target):
    total = parts[0][...]
    for part in parts[1:]:
        total = total + part[...]
    target[...] = total


def set_entry(carried, entry):
    both = carried.shape[0] == 2
    entry[...] = carried[1] - carried[0] if both else -carried[0]


def hop_down_kernel(parts, has_last, vector, lower, pivot, *refs):
    carried_in, refs = refs[:parts], refs[parts:]
    if has_last:
        last, *refs = refs
    carried, message, forward, entry, work = refs
    add_up(carried_in, carried)
    set_entry(carried, entry)
    run_down(vector, lower, pivot, entry, forward, work)
    message[0] = forward[forward.shape[0] - 1]
    if has_last:
        message[1] = last[...]


def turn_kernel(parts, vector, lower, pivot, upper, *refs):
    carried_in = refs[:parts]
    carried, forward, outgoing, entry, work, result, coupled = refs[parts:]
    add_up(carried_in, carried)
    set_entry(carried, entry)
    run_down(vector, lower, pivot, entry, forward, work)
    run_up(forward, upper, pivot, None, result, coupled)
    outgoing[...] = result[0]


def hop_up_kernel(parts, forward, upper, pivot, *refs):
    carried_in = refs[:parts]
    carried, outgoing, result, coupled = refs[parts:]
    add_up(carried_in, carried)
    run_up(forward, upper, pivot, carried, result, coupled)
    outgoing[...] = result[0]


def end_kernel(parts, forward, upper, pivot, *refs):
    carried_in = refs[:parts]
    result, coupled, last, carried = refs[parts:]
    add_up(carried_in, carried)
    run_up(forward, upper, pivot, carried, result, coupled)
    last[...] = result[result.shape[0] - 1]


def multiply_lines(left, right, out):
    block = right.shape[0]
    group = max(g for g in (1, 2, 3, 4) if block % g == 0)
    unroll = max(u for u in (1, 2, 4, 8) if block % u == 0)

    def rows(step, carry):
        start = step * group

        def add(j, totals):
            row = right[j]
            return tuple(
                total + left[start + q, pl.ds(j, 1), :] * row for q, total in enumerate(totals)
            )

        zero = jnp.zeros(right.shape[1:], jnp.float32)
        totals = lax.fori_loop(0, block, add, (zero,) * group, unroll=unroll)
        for q, total in enumerate(totals):
            out[start + q] = total
        return carry

    lax.fori_loop(0, block // group, rows, 0)


def on_last(body):
    pl.when(lax.axis_index("line") == lax.axis_size("line") - 1)(body)


def factor_kernel(lower, pivot, after, factor, out):
    def body():
        multiply_lines(lower.at[0], pivot.at[0], factor)
        multiply_lines(factor, lower.at[1], out)

    on_last(body)


def response_kernel(factor, given, upper, pivot, after, out, work):
    def body():
        multiply_lines(given, pivot.at[1], out)
        multiply_lines(out, upper.at[0], work)
        multiply_lines(work, pivot.at[0], out)

        def row(i, carry):
            out[i] = out[i] + factor[i]
            return carry

        lax.fori_loop(0, out.shape[0], row, 0, unroll=4)

    on_last(body)


def alone_kernel(forward, upper, pivot, outgoing, result, coupled):
    run_up(forward, upper, pivot, None, result, coupled)
    outgoing[...] = result[0]


def short_turn_kernel(
    vector, lower, pivot, upper, response, alone, message, carried_in, received,
    carried, upward, outgoing, passed, forward, entry, work, result, coupled,
):
    carried[...] = carried_in[...] + received[...]
    set_entry(carried, entry)
    run_down(vector, lower, pivot, entry, forward, work)
    passed[...] = forward[forward.shape[0] - 1]
    entry[...] = message[0] - passed[...]
    upward[...] = alone[...] + apply_turned(response, entry)
    run_up(forward, upper, pivot, upward, result, coupled)
    outgoing[...] = result[0]


def short_end_kernel(
    vector, lower, pivot, upper, forward_in, carried, upward, received, onward,
    result, coupled, last, forward, entry, work,
):
    forward[...] = forward_in[...]

    def again():
        entry[...] = carried[1] - onward[...]
        run_down(vector, lower, pivot, entry, forward, work)

    on_last(again)
    entry[...] = upward[...] + received[...]
    run_up(forward, upper, pivot, entry, result, coupled)
    last[...] = result[result.shape[0] - 1]


def own_kernel(vector, carried, lower, diag_block, direction, coupled, whole, image):
    for k in range(vector.shape[0]):
        value = vector[k]
        if k == 0 and carried.shape[0] == 2:
            value = value + apply_turned(lower.at[0], carried.at[1])
        whole[k] = value
        value = coupled[k] - value + apply_turned(diag_block.at[k], direction.at[k])
        if k > 0:
            value = value + apply_turned(lower.at[k], direction.at[k - 1])
        image[k] = value


def near_kernel(image, near_block, near, *refs):
    *below, out = refs
    for k in range(image.shape[0]):
        out[k] = image[k] + apply_turned(near_block.at[k], near.at[k])
    if below:
        out[0] = out[0] + apply_turned(below[0].at[0], below[1])


def next_kernel(image, far_block, far, lower, pivot, last, out, message, forward, work):
    for k in range(image.shape[0]):
        out[k] = image[k] + apply_turned(far_block.at[k], far.at[k])
    run_down(out, lower, pivot, None, forward, work)
    message[0] = forward[forward.shape[0] - 1]
    message[1] = last[...]


def place_of(pair):
    low, high = sorted(pair)
    return high * (high + 1) // 2 + low


def pair_sum(left, right):
    total = left[0] * right[0]
    for k in range(1, left.shape[0]):
        total = total + left[k] * right[k]
    return jnp.sum(total, axis=0, keepdims=True)


def sums_kernel(*refs):
    *basis, out = refs
    row = lax.broadcasted_iota(jnp.int32, out.shape, 0)
    sums = jnp.zeros(out.shape, jnp.float32)
    for i in range(len(basis)):
        for j in range(i, len(basis)):
            sums = jnp.where(row == place_of((i, j)), pair_sum(basis[i], basis[j]), sums)
    out[...] = sums


def last_kernel(image, far_block, far, sums_in, *refs):
    *basis, out, newest = refs
    for k in range(image.shape[0]):
        newest[k] = image[k] + apply_turned(far_block.at[k], far.at[k])
    sums = sums_in[...]
    row = lax.broadcasted_iota(jnp.int32, sums.shape, 0)
    lane = lax.broadcasted_iota(jnp.int32, sums.shape, 1)
    high = len(basis)
    for i, member in enumerate((*basis, newest)):
        sums = jnp.where(row == place_of((i, high)), pair_sum(member, newest), sums)
    whole = jnp.sum(sums, axis=1, keepdims=True)
    sums = jnp.sum(jnp.where(lane == row, whole, 0.0), axis=0, keepdims=True)
    out[...] = jnp.broadcast_to(sums, out.shape)


def finish_kernel(parts_ref, *refs):
    directions, out = refs[:-1], refs[-1]
    width = len(directions)
    total = jnp.sum(parts_ref[...], axis=0, keepdims=True)
    shape = (SUMS, total.shape[1])
    row = lax.broadcasted_iota(jnp.int32, shape, 0)
    lane = lax.broadcasted_iota(jnp.int32, shape, 1)
    sums = jnp.sum(jnp.where(lane == row, total, 0.0), axis=1, keepdims=True)
    sums = jnp.broadcast_to(sums, shape)
    gram = {}
    for i in range(width + 1):
        for j in range(width + 1):
            place = place_of((i, j))
            gram[i, j] = sums[place : place + 1]
    half = [[gram[j + 1, i] + gram[j, i] for i in range(width + 1)] for j in range(width)]
    normal = [[half[j][i + 1] + half[j][i] for i in range(width)] for j in range(width)]
    right = [half[j][0] for j in range(width)]
    for i in range(width):
        inverse = 1.0 / normal[i][i]
        for j in range(i + 1, width):
            factor = normal[j][i] * inverse
            for k in range(i, width):
                normal[j][k] = normal[j][k] - factor * normal[i][k]
            right[j] = right[j] - factor * right[i]
    coeffs = [None] * width
    for i in reversed(range(width)):
        value = right[i]
        for k in range(i + 1, width):
            value = value - normal[i][k] * coeffs[k]
        coeffs[i] = value / normal[i][i]
    for k in range(out.shape[0]):
        step = coeffs[0] * directions[0][k]
        for j in range(1, width):
            step = step + coeffs[j] * directions[j][k]
        out[k] = step


def rows_beside(field, across):
    count = lax.axis_size("patch")
    even = [(i, i + 1) for i in range(0, count - 1, 2)]
    odd = [(i, i + 1) for i in range(1, count - 1, 2)]
    is_even = lax.axis_index("patch") % 2 == 0
    first, last = field[..., :across], field[..., -across:]
    several = field.shape[-1] > across
    to_far = jnp.where(is_even, first, last) if several else field
    to_near = jnp.where(is_even, last, first) if several else field
    far = lax.ppermute(to_far, "patch", odd + [(b, a) for a, b in odd])
    near = lax.ppermute(to_near, "patch", even + [(b, a) for a, b in even])
    if several:
        up = [jnp.concatenate([field[..., across:], row], axis=-1) for row in (near, far)]
        down = [jnp.concatenate([row, field[..., :-across]], axis=-1) for row in (near, far)]
        near = jnp.where(is_even, up[0], down[0])
        far = jnp.where(is_even, down[1], up[1])
    return near, far


def sweep_short(vector, message, last, lower, pivot, upper, response):
    field, one = vector.shape, last.shape
    received = lax.ppermute(message, "line", [(0, 1), (2, 3)])
    carried, onto, forward = stage(
        functools.partial(hop_down_kernel, 1, True),
        [message.shape, message.shape, field],
        [vector, lower, pivot, received, last],
        [one, one],
    )
    received = lax.ppermute(onto, "line", [(1, 2)])
    (alone,) = stage(alone_kernel, [one], [forward, upper, pivot], [field, field])
    alone = lax.ppermute(alone, "line", [(3, 2)])
    carried, upward, outgoing, passed, forward = stage(
        short_turn_kernel,
        [message.shape, one, one, one, field],
        [vector, lower, pivot, upper, response, alone, message, carried, received],
        [one, one, field, field],
    )
    received = lax.ppermute(outgoing, "line", [(2, 1)])
    upward, outgoing = stage(
        functools.partial(hop_up_kernel, 2),
        [one, one],
        [forward, upper, pivot, upward, received],
        [field, field],
    )
    outgoing, passed = lax.optimization_barrier((outgoing, passed))
    received = lax.ppermute(outgoing, "line", [(1, 0)])
    onward = lax.ppermute(passed, "line", [(2, 3)])
    direction, coupled, last = stage(
        short_end_kernel,
        [field, field, one],
        [vector, lower, pivot, upper, forward, carried, upward, received, onward],
        [field, one, one],
    )
    return direction, coupled, last, carried


def per_device(newton_residual, diag_block, lower, upper, west, east, pivot_inverse):
    shape = newton_residual.shape
    count, block, rows, across = shape
    wide = rows * across

    def flat(matrix):
        return matrix.reshape(count, block, block, wide)

    diag_block, lower, upper, west, east, pivot = map(
        flat, (diag_block, lower, upper, west, east, pivot_inverse)
    )
    line = lax.axis_size("line")
    devices = line * lax.axis_size("patch")
    one, field = (block, wide), (count, block, wide)
    vector = newton_residual.reshape(field)
    lower, pivot, message = first_carry(vector, lower, pivot)
    lower, pivot = turn_held(lower, pivot)
    basis = []
    directions = []
    last = None
    short = line == 4 and count == 2
    for j in range(ITERS):
        if j >= 2 and short:
            direction, coupled, last, carried_down = sweep_short(
                vector, message, last, lower, pivot, upper, response
            )
        else:
            parts = []
            for turn in range(line - 1):
                parts.append(lax.ppermute(message, "line", [(turn, turn + 1)]))
                if j == 0 and turn == 0:
                    (upper,) = load((upper,), message)
                if j == 0 and turn == line - 2 and short:
                    factor, response = stage(
                        factor_kernel, [(block,) + one] * 2, [lower, pivot, message]
                    )
                if turn < line - 2:
                    lasts = [] if last is None else [last]
                    carried, message = stage(
                        functools.partial(hop_down_kernel, len(parts), bool(lasts)),
                        [message.shape, message.shape],
                        [vector, lower, pivot, *parts, *lasts],
                        [field, one, one],
                    )
                    parts = [carried]
            parts = parts or [jnp.zeros_like(message)]
            carried_down, forward, outgoing = stage(
                functools.partial(turn_kernel, len(parts)),
                [message.shape, field, one],
                [vector, lower, pivot, upper, *parts],
                [one, one, field, field],
            )
            if j == 0 and short:
                outgoing, response = lax.optimization_barrier((outgoing, response))
            parts = []
            for turn in reversed(range(line - 1)):
                if j == 1 and turn == line - 3 and short:
                    outgoing, ready = lax.optimization_barrier((outgoing, response))
                    response = lax.ppermute(ready, "line", [(line - 1, line - 2)])
                parts.append(lax.ppermute(outgoing, "line", [(turn + 1, turn)]))
                if j == 0 and turn == line - 2:
                    diag_block, near_block, far_block = load(
                        (diag_block, east, west), outgoing, True
                    )
                if j == 0 and turn == line - 3 and short:
                    (response,) = stage(
                        response_kernel,
                        [(block,) + one],
                        [factor, response, upper, pivot, outgoing],
                        [(block,) + one],
                    )
                if turn > 0:
                    carried, outgoing = stage(
                        functools.partial(hop_up_kernel, len(parts)),
                        [one, one],
                        [forward, upper, pivot, *parts],
                        [field, field],
                    )
                    parts = [carried]
            parts = parts or [jnp.zeros_like(outgoing)]
            direction, coupled, last = stage(
                functools.partial(end_kernel, len(parts)),
                [field, field, one],
                [forward, upper, pivot, *parts],
                [one],
            )
        directions.append(direction)
        near, far = rows_beside(direction, across)
        whole, image = stage(
            own_kernel,
            [field, field],
            [vector, carried_down, lower, diag_block, direction, coupled],
        )
        basis.append(whole)
        beneath = []
        if j == ITERS - 1:
            (sums,) = stage(sums_kernel, [(SUMS, wide)], basis)
            below = lax.ppermute(last, "line", [(i, i + 1) for i in range(line - 1)])
            beneath = [lower, below]
        (image,) = stage(near_kernel, [field], [image, near_block, near, *beneath])
        if j < ITERS - 1:
            vector, message = stage(
                next_kernel,
                [field, (2,) + one],
                [image, far_block, far, lower, pivot, last],
                [field, one],
            )
            if j == 0 and short:
                message, response = lax.optimization_barrier((message, response))
        else:
            (sums,) = stage(
                last_kernel,
                [(devices, wide)],
                [image, far_block, far, sums, *basis],
                [field],
            )
    sums = lax.all_to_all(sums, ("line", "patch"), 0, 0, tiled=True)
    (step,) = stage(finish_kernel, [field], [sums, *directions])
    return step.reshape(shape)


def solution(mesh):
    blocks = P("line", None, None, "patch", None)
    field = P("line", None, "patch", None)
    return jax.shard_map(
        per_device, mesh=mesh, in_specs=(field,) + (blocks,) * 6, out_specs=field, check_vma=False
    )
```

```python
import functools

import jax
import jax.numpy as jnp
from jax import lax
from jax.experimental import pallas as pl
from jax.experimental.pallas import tpu as pltpu
from jax.sharding import PartitionSpec as P

ITERS = 4
SUMS = 16
FETCH_ROOM = 56 << 20
LOAD_ROOM = 40 << 20
STAGE_ROOM = 16 << 20


def start_all(pairs, sems):
    copies = [
        pltpu.make_async_copy(source, target, sems.at[place])
        for place, (source, target) in enumerate(pairs)
    ]
    for copy in copies:
        copy.start()
    return copies


def turn_over(source, target):
    block = source.shape[0]
    high = 16 if block % 16 == 0 else block
    wide = 8 if block % 8 == 0 else block
    for i in range(0, block, wide):
        for j in range(0, block, high):
            part = source[i : i + wide, j : j + high].astype(jnp.float32)
            target[j : j + high, i : i + wide] = jnp.swapaxes(part, 0, 1)


def apply_plain(block_mat, value, target):
    block = target.shape[0]
    rows = 16 if block % 16 == 0 else block
    for start in range(0, block, rows):
        part = block_mat[start : start + rows].astype(jnp.float32)
        target[start : start + rows] = jnp.sum(part * value[None], axis=1)


def apply_turned(block_mat, vector):
    totals = [None, None]
    for j in range(block_mat.shape[0]):
        term = block_mat[j] * vector[j : j + 1]
        totals[j % 2] = term if totals[j % 2] is None else totals[j % 2] + term
    return totals[0] + totals[1]


def first_kernel(vector, lower, pivot, lower_held, pivot_held, out, field, middle, sems):
    count = vector.shape[0]
    pairs = [(vector, field), (pivot.at[0], pivot_held.at[0])]
    for k in range(1, count):
        pairs += [(lower.at[k], lower_held.at[k]), (pivot.at[k], pivot_held.at[k])]
    pairs.append((lower.at[0], lower_held.at[0]))
    copies = start_all(pairs, sems)
    copies[0].wait()
    copies[1].wait()
    apply_plain(pivot_held.at[0], field[0], out.at[0])
    for k in range(1, count):
        copies[2 * k].wait()
        apply_plain(lower_held.at[k], out[0], middle)
        copies[2 * k + 1].wait()
        apply_plain(pivot_held.at[k], field[k] - middle[...], out.at[0])
    copies[-1].wait()


def first_carry(vector, lower, pivot):
    count, block, wide = vector.shape
    return pl.pallas_call(
        first_kernel,
        out_shape=[
            pltpu.VMEM(lower.shape, lower.dtype),
            pltpu.VMEM(pivot.shape, pivot.dtype),
            pltpu.VMEM((1, block, wide), jnp.float32),
        ],
        in_specs=[pl.BlockSpec(memory_space=pl.ANY)] * 3,
        out_specs=[pl.BlockSpec(memory_space=pltpu.VMEM)] * 3,
        scratch_shapes=[
            pltpu.VMEM(vector.shape, jnp.float32),
            pltpu.VMEM((block, wide), jnp.float32),
            pltpu.SemaphoreType.DMA((1 + 2 * count,)),
        ],
        compiler_params=pltpu.CompilerParams(vmem_limit_bytes=FETCH_ROOM),
    )(vector, lower, pivot)


def turn_held_kernel(*refs):
    half = len(refs) // 2
    for source, target in zip(refs[:half], refs[half:]):
        for k in range(source.shape[0]):
            turn_over(source.at[k], target.at[k])


def turn_held(*blocks):
    vmem = pl.BlockSpec(memory_space=pltpu.VMEM)
    return pl.pallas_call(
        turn_held_kernel,
        out_shape=[pltpu.VMEM(block.shape, jnp.float32) for block in blocks],
        in_specs=[vmem] * len(blocks),
        out_specs=[vmem] * len(blocks),
        compiler_params=pltpu.CompilerParams(vmem_limit_bytes=STAGE_ROOM),
    )(*blocks)


def load_kernel(choose, *refs):
    *refs, held, sems = refs
    size = (len(refs) - 1) // 2
    sources, targets = refs[:size], refs[size + 1 :]

    def run(sources):
        copies = start_all([(s, held.at[place]) for place, s in enumerate(sources)], sems)
        for place, target in enumerate(targets):
            copies[place].wait()
            for k in range(target.shape[0]):
                turn_over(held.at[place, k], target.at[k])

    if choose:
        even = lax.axis_index("patch") % 2 == 0
        pl.when(even)(lambda: run(sources))
        pl.when(jnp.logical_not(even))(lambda: run((*sources[:-2], sources[-1], sources[-2])))
    else:
        run(sources)


def load(blocks, after, choose=False):
    shape = blocks[0].shape
    return pl.pallas_call(
        functools.partial(load_kernel, choose),
        out_shape=[pltpu.VMEM(shape, jnp.float32) for block in blocks],
        in_specs=[pl.BlockSpec(memory_space=pl.ANY)] * (len(blocks) + 1),
        out_specs=[pl.BlockSpec(memory_space=pltpu.VMEM)] * len(blocks),
        scratch_shapes=[
            pltpu.VMEM((len(blocks),) + shape, blocks[0].dtype),
            pltpu.SemaphoreType.DMA((len(blocks),)),
        ],
        compiler_params=pltpu.CompilerParams(vmem_limit_bytes=LOAD_ROOM),
    )(*blocks, after)


def stage(kernel, out_shapes, operands, scratch=()):
    vmem = pl.BlockSpec(memory_space=pltpu.VMEM)
    return pl.pallas_call(
        kernel,
        out_shape=[pltpu.VMEM(shape, jnp.float32) for shape in out_shapes],
        in_specs=[vmem] * len(operands),
        out_specs=[vmem] * len(out_shapes),
        scratch_shapes=[pltpu.VMEM(shape, jnp.float32) for shape in scratch],
        compiler_params=pltpu.CompilerParams(vmem_limit_bytes=STAGE_ROOM),
    )(*operands)


def run_down(vector, lower, pivot, entry, forward, work):
    for k in range(vector.shape[0]):
        if k > 0:
            work[...] = vector[k] - apply_turned(lower.at[k], forward.at[k - 1])
        elif entry is not None:
            work[...] = vector[k] + apply_turned(lower.at[k], entry)
        else:
            work[...] = vector[k]
        forward[k] = apply_turned(pivot.at[k], work)


def run_up(forward, upper, pivot, incoming, result, coupled):
    count = forward.shape[0]
    for k in reversed(range(count)):
        following = result.at[k + 1] if k < count - 1 else incoming
        if following is None:
            result[k] = forward[k]
        else:
            coupled[k] = apply_turned(upper.at[k], following)
            result[k] = forward[k] - apply_turned(pivot.at[k], coupled.at[k])


def add_up(parts, target):
    total = parts[0][...]
    for part in parts[1:]:
        total = total + part[...]
    target[...] = total


def set_entry(carried, entry):
    both = carried.shape[0] == 2
    entry[...] = carried[1] - carried[0] if both else -carried[0]


def hop_down_kernel(parts, has_last, vector, lower, pivot, *refs):
    carried_in, refs = refs[:parts], refs[parts:]
    if has_last:
        last, *refs = refs
    carried, message, forward, entry, work = refs
    add_up(carried_in, carried)
    set_entry(carried, entry)
    run_down(vector, lower, pivot, entry, forward, work)
    message[0] = forward[forward.shape[0] - 1]
    if has_last:
        message[1] = last[...]


def turn_kernel(parts, vector, lower, pivot, upper, *refs):
    carried_in = refs[:parts]
    carried, forward, outgoing, entry, work, result, coupled = refs[parts:]
    add_up(carried_in, carried)
    set_entry(carried, entry)
    run_down(vector, lower, pivot, entry, forward, work)
    run_up(forward, upper, pivot, None, result, coupled)
    outgoing[...] = result[0]


def hop_up_kernel(parts, forward, upper, pivot, *refs):
    carried_in = refs[:parts]
    carried, outgoing, result, coupled = refs[parts:]
    add_up(carried_in, carried)
    run_up(forward, upper, pivot, carried, result, coupled)
    outgoing[...] = result[0]


def end_kernel(parts, forward, upper, pivot, *refs):
    carried_in = refs[:parts]
    result, coupled, last, carried = refs[parts:]
    add_up(carried_in, carried)
    run_up(forward, upper, pivot, carried, result, coupled)
    last[...] = result[result.shape[0] - 1]


def multiply_lines(left, right, out):
    block = right.shape[0]
    group = max(g for g in (1, 2, 3, 4) if block % g == 0)
    unroll = max(u for u in (1, 2, 4, 8) if block % u == 0)

    def rows(step, carry):
        start = step * group

        def add(j, totals):
            row = right[j]
            return tuple(
                total + left[start + q, pl.ds(j, 1), :] * row for q, total in enumerate(totals)
            )

        zero = jnp.zeros(right.shape[1:], jnp.float32)
        totals = lax.fori_loop(0, block, add, (zero,) * group, unroll=unroll)
        for q, total in enumerate(totals):
            out[start + q] = total
        return carry

    lax.fori_loop(0, block // group, rows, 0)


def on_last(body):
    pl.when(lax.axis_index("line") == lax.axis_size("line") - 1)(body)


def factor_kernel(lower, pivot, after, factor, out):
    def body():
        multiply_lines(lower.at[0], pivot.at[0], factor)
        multiply_lines(factor, lower.at[1], out)

    on_last(body)


def response_kernel(factor, given, upper, pivot, after, out, work):
    def body():
        multiply_lines(given, pivot.at[1], out)
        multiply_lines(out, upper.at[0], work)
        multiply_lines(work, pivot.at[0], out)

        def row(i, carry):
            out[i] = out[i] + factor[i]
            return carry

        lax.fori_loop(0, out.shape[0], row, 0, unroll=4)

    on_last(body)


def alone_kernel(forward, upper, pivot, outgoing, result, coupled):
    run_up(forward, upper, pivot, None, result, coupled)
    outgoing[...] = result[0]


def short_turn_kernel(
    vector, lower, pivot, upper, response, alone, message, carried_in, received,
    carried, upward, outgoing, passed, forward, entry, work, result, coupled,
):
    carried[...] = carried_in[...] + received[...]
    set_entry(carried, entry)
    run_down(vector, lower, pivot, entry, forward, work)
    passed[...] = forward[forward.shape[0] - 1]
    entry[...] = message[0] - passed[...]
    upward[...] = alone[...] + apply_turned(response, entry)
    run_up(forward, upper, pivot, upward, result, coupled)
    outgoing[...] = result[0]


def short_end_kernel(
    vector, lower, pivot, upper, forward_in, carried, upward, received, onward,
    result, coupled, last, forward, entry, work,
):
    forward[...] = forward_in[...]

    def again():
        entry[...] = carried[1] - onward[...]
        run_down(vector, lower, pivot, entry, forward, work)

    on_last(again)
    entry[...] = upward[...] + received[...]
    run_up(forward, upper, pivot, entry, result, coupled)
    last[...] = result[result.shape[0] - 1]


def own_kernel(vector, carried, lower, diag_block, direction, coupled, whole, image):
    for k in range(vector.shape[0]):
        value = vector[k]
        if k == 0 and carried.shape[0] == 2:
            value = value + apply_turned(lower.at[0], carried.at[1])
        whole[k] = value
        value = coupled[k] - value + apply_turned(diag_block.at[k], direction.at[k])
        if k > 0:
            value = value + apply_turned(lower.at[k], direction.at[k - 1])
        image[k] = value


def near_kernel(image, near_block, near, *refs):
    *below, out = refs
    for k in range(image.shape[0]):
        out[k] = image[k] + apply_turned(near_block.at[k], near.at[k])
    if below:
        out[0] = out[0] + apply_turned(below[0].at[0], below[1])


def next_kernel(image, far_block, far, lower, pivot, last, out, message, forward, work):
    for k in range(image.shape[0]):
        out[k] = image[k] + apply_turned(far_block.at[k], far.at[k])
    run_down(out, lower, pivot, None, forward, work)
    message[0] = forward[forward.shape[0] - 1]
    message[1] = last[...]


def place_of(pair):
    low, high = sorted(pair)
    return high * (high + 1) // 2 + low


def pair_sum(left, right):
    total = left[0] * right[0]
    for k in range(1, left.shape[0]):
        total = total + left[k] * right[k]
    return jnp.sum(total, axis=0, keepdims=True)


def sums_kernel(*refs):
    *basis, out = refs
    row = lax.broadcasted_iota(jnp.int32, out.shape, 0)
    sums = jnp.zeros(out.shape, jnp.float32)
    for i in range(len(basis)):
        for j in range(i, len(basis)):
            sums = jnp.where(row == place_of((i, j)), pair_sum(basis[i], basis[j]), sums)
    out[...] = sums


def last_kernel(image, far_block, far, sums_in, *refs):
    *basis, out, newest = refs
    for k in range(image.shape[0]):
        newest[k] = image[k] + apply_turned(far_block.at[k], far.at[k])
    sums = sums_in[...]
    row = lax.broadcasted_iota(jnp.int32, sums.shape, 0)
    lane = lax.broadcasted_iota(jnp.int32, sums.shape, 1)
    high = len(basis)
    for i, member in enumerate((*basis, newest)):
        sums = jnp.where(row == place_of((i, high)), pair_sum(member, newest), sums)
    whole = jnp.sum(sums, axis=1, keepdims=True)
    sums = jnp.sum(jnp.where(lane == row, whole, 0.0), axis=0, keepdims=True)
    out[...] = jnp.broadcast_to(sums, out.shape)


def finish_kernel(parts_ref, *refs):
    directions, out = refs[:-1], refs[-1]
    width = len(directions)
    total = jnp.sum(parts_ref[...], axis=0, keepdims=True)
    shape = (SUMS, total.shape[1])
    row = lax.broadcasted_iota(jnp.int32, shape, 0)
    lane = lax.broadcasted_iota(jnp.int32, shape, 1)
    sums = jnp.sum(jnp.where(lane == row, total, 0.0), axis=1, keepdims=True)
    sums = jnp.broadcast_to(sums, shape)
    gram = {}
    for i in range(width + 1):
        for j in range(width + 1):
            place = place_of((i, j))
            gram[i, j] = sums[place : place + 1]
    half = [[gram[j + 1, i] + gram[j, i] for i in range(width + 1)] for j in range(width)]
    normal = [[half[j][i + 1] + half[j][i] for i in range(width)] for j in range(width)]
    right = [half[j][0] for j in range(width)]
    for i in range(width):
        inverse = 1.0 / normal[i][i]
        for j in range(i + 1, width):
            factor = normal[j][i] * inverse
            for k in range(i, width):
                normal[j][k] = normal[j][k] - factor * normal[i][k]
            right[j] = right[j] - factor * right[i]
    coeffs = [None] * width
    for i in reversed(range(width)):
        value = right[i]
        for k in range(i + 1, width):
            value = value - normal[i][k] * coeffs[k]
        coeffs[i] = value / normal[i][i]
    for k in range(out.shape[0]):
        step = coeffs[0] * directions[0][k]
        for j in range(1, width):
            step = step + coeffs[j] * directions[j][k]
        out[k] = step


def rows_beside(field, across):
    count = lax.axis_size("patch")
    even = [(i, i + 1) for i in range(0, count - 1, 2)]
    odd = [(i, i + 1) for i in range(1, count - 1, 2)]
    is_even = lax.axis_index("patch") % 2 == 0
    first, last = field[..., :across], field[..., -across:]
    several = field.shape[-1] > across
    to_far = jnp.where(is_even, first, last) if several else field
    to_near = jnp.where(is_even, last, first) if several else field
    far = lax.ppermute(to_far, "patch", odd + [(b, a) for a, b in odd])
    near = lax.ppermute(to_near, "patch", even + [(b, a) for a, b in even])
    if several:
        up = [jnp.concatenate([field[..., across:], row], axis=-1) for row in (near, far)]
        down = [jnp.concatenate([row, field[..., :-across]], axis=-1) for row in (near, far)]
        near = jnp.where(is_even, up[0], down[0])
        far = jnp.where(is_even, down[1], up[1])
    return near, far


def sweep_short(vector, message, last, lower, pivot, upper, response):
    field, one = vector.shape, last.shape
    received = lax.ppermute(message, "line", [(0, 1), (2, 3)])
    carried, onto, forward = stage(
        functools.partial(hop_down_kernel, 1, True),
        [message.shape, message.shape, field],
        [vector, lower, pivot, received, last],
        [one, one],
    )
    received = lax.ppermute(onto, "line", [(1, 2)])
    (alone,) = stage(alone_kernel, [one], [forward, upper, pivot], [field, field])
    alone = lax.ppermute(alone, "line", [(3, 2)])
    carried, upward, outgoing, passed, forward = stage(
        short_turn_kernel,
        [message.shape, one, one, one, field],
        [vector, lower, pivot, upper, response, alone, message, carried, received],
        [one, one, field, field],
    )
    received = lax.ppermute(outgoing, "line", [(2, 1)])
    upward, outgoing = stage(
        functools.partial(hop_up_kernel, 2),
        [one, one],
        [forward, upper, pivot, upward, received],
        [field, field],
    )
    outgoing, passed = lax.optimization_barrier((outgoing, passed))
    received = lax.ppermute(outgoing, "line", [(1, 0)])
    onward = lax.ppermute(passed, "line", [(2, 3)])
    direction, coupled, last = stage(
        short_end_kernel,
        [field, field, one],
        [vector, lower, pivot, upper, forward, carried, upward, received, onward],
        [field, one, one],
    )
    return direction, coupled, last, carried


def per_device(newton_residual, diag_block, lower, upper, west, east, pivot_inverse):
    shape = newton_residual.shape
    count, block, rows, across = shape
    wide = rows * across

    def flat(matrix):
        return matrix.reshape(count, block, block, wide)

    diag_block, lower, upper, west, east, pivot = map(
        flat, (diag_block, lower, upper, west, east, pivot_inverse)
    )
    line = lax.axis_size("line")
    devices = line * lax.axis_size("patch")
    one, field = (block, wide), (count, block, wide)
    vector = newton_residual.reshape(field)
    lower, pivot, message = first_carry(vector, lower, pivot)
    lower, pivot = turn_held(lower, pivot)
    basis = []
    directions = []
    last = None
    short = line == 4 and count == 2
    for j in range(ITERS):
        if j >= 1 and short:
            direction, coupled, last, carried_down = sweep_short(
                vector, message, last, lower, pivot, upper, response
            )
        else:
            parts = []
            for turn in range(line - 1):
                parts.append(lax.ppermute(message, "line", [(turn, turn + 1)]))
                if j == 0 and turn == 0:
                    (upper,) = load((upper,), message)
                if j == 0 and turn == line - 2 and short:
                    factor, response = stage(
                        factor_kernel, [(block,) + one] * 2, [lower, pivot, message]
                    )
                if turn < line - 2:
                    lasts = [] if last is None else [last]
                    carried, message = stage(
                        functools.partial(hop_down_kernel, len(parts), bool(lasts)),
                        [message.shape, message.shape],
                        [vector, lower, pivot, *parts, *lasts],
                        [field, one, one],
                    )
                    parts = [carried]
            parts = parts or [jnp.zeros_like(message)]
            carried_down, forward, outgoing = stage(
                functools.partial(turn_kernel, len(parts)),
                [message.shape, field, one],
                [vector, lower, pivot, upper, *parts],
                [one, one, field, field],
            )
            if j == 0 and short:
                outgoing, response = lax.optimization_barrier((outgoing, response))
            parts = []
            for turn in reversed(range(line - 1)):
                parts.append(lax.ppermute(outgoing, "line", [(turn + 1, turn)]))
                if j == 0 and turn == line - 2:
                    diag_block, near_block, far_block = load(
                        (diag_block, east, west), outgoing, True
                    )
                if j == 0 and turn == line - 3 and short:
                    (response,) = stage(
                        response_kernel,
                        [(block,) + one],
                        [factor, response, upper, pivot, outgoing],
                        [(block,) + one],
                    )
                    response = lax.ppermute(response, "line", [(line - 1, line - 2)])
                if turn > 0:
                    carried, outgoing = stage(
                        functools.partial(hop_up_kernel, len(parts)),
                        [one, one],
                        [forward, upper, pivot, *parts],
                        [field, field],
                    )
                    parts = [carried]
            parts = parts or [jnp.zeros_like(outgoing)]
            direction, coupled, last = stage(
                functools.partial(end_kernel, len(parts)),
                [field, field, one],
                [forward, upper, pivot, *parts],
                [one],
            )
        directions.append(direction)
        near, far = rows_beside(direction, across)
        whole, image = stage(
            own_kernel,
            [field, field],
            [vector, carried_down, lower, diag_block, direction, coupled],
        )
        basis.append(whole)
        beneath = []
        if j == ITERS - 1:
            (sums,) = stage(sums_kernel, [(SUMS, wide)], basis)
            below = lax.ppermute(last, "line", [(i, i + 1) for i in range(line - 1)])
            beneath = [lower, below]
        (image,) = stage(near_kernel, [field], [image, near_block, near, *beneath])
        if j < ITERS - 1:
            vector, message = stage(
                next_kernel,
                [field, (2,) + one],
                [image, far_block, far, lower, pivot, last],
                [field, one],
            )
        else:
            (sums,) = stage(
                last_kernel,
                [(devices, wide)],
                [image, far_block, far, sums, *basis],
                [field],
            )
    sums = lax.all_to_all(sums, ("line", "patch"), 0, 0, tiled=True)
    (step,) = stage(finish_kernel, [field], [sums, *directions])
    return step.reshape(shape)


def solution(mesh):
    blocks = P("line", None, None, "patch", None)
    field = P("line", None, "patch", None)
    return jax.shard_map(
        per_device, mesh=mesh, in_specs=(field,) + (blocks,) * 6, out_specs=field, check_vma=False
    )
```

```python
import functools

import jax
import jax.numpy as jnp
from jax import lax
from jax.experimental import pallas as pl
from jax.experimental.pallas import tpu as pltpu
from jax.sharding import PartitionSpec as P

ITERS = 4
SUMS = 16
FETCH_ROOM = 56 << 20
LOAD_ROOM = 40 << 20
STAGE_ROOM = 16 << 20


def start_all(pairs, sems):
    copies = [
        pltpu.make_async_copy(source, target, sems.at[place])
        for place, (source, target) in enumerate(pairs)
    ]
    for copy in copies:
        copy.start()
    return copies


def turn_over(source, target):
    block = source.shape[0]
    high = 16 if block % 16 == 0 else block
    wide = 8 if block % 8 == 0 else block
    for i in range(0, block, wide):
        for j in range(0, block, high):
            part = source[i : i + wide, j : j + high].astype(jnp.float32)
            target[j : j + high, i : i + wide] = jnp.swapaxes(part, 0, 1)


def apply_plain(block_mat, value, target):
    block = target.shape[0]
    rows = 16 if block % 16 == 0 else block
    for start in range(0, block, rows):
        part = block_mat[start : start + rows].astype(jnp.float32)
        target[start : start + rows] = jnp.sum(part * value[None], axis=1)


def apply_turned(block_mat, vector):
    totals = [None, None]
    for j in range(block_mat.shape[0]):
        term = block_mat[j] * vector[j : j + 1]
        totals[j % 2] = term if totals[j % 2] is None else totals[j % 2] + term
    return totals[0] + totals[1]


def first_kernel(vector, lower, pivot, lower_held, pivot_held, out, field, middle, sems):
    count = vector.shape[0]
    pairs = [(vector, field), (pivot.at[0], pivot_held.at[0])]
    for k in range(1, count):
        pairs += [(lower.at[k], lower_held.at[k]), (pivot.at[k], pivot_held.at[k])]
    pairs.append((lower.at[0], lower_held.at[0]))
    copies = start_all(pairs, sems)
    copies[0].wait()
    copies[1].wait()
    apply_plain(pivot_held.at[0], field[0], out.at[0])
    for k in range(1, count):
        copies[2 * k].wait()
        apply_plain(lower_held.at[k], out[0], middle)
        copies[2 * k + 1].wait()
        apply_plain(pivot_held.at[k], field[k] - middle[...], out.at[0])
    copies[-1].wait()


def first_carry(vector, lower, pivot):
    count, block, wide = vector.shape
    return pl.pallas_call(
        first_kernel,
        out_shape=[
            pltpu.VMEM(lower.shape, lower.dtype),
            pltpu.VMEM(pivot.shape, pivot.dtype),
            pltpu.VMEM((1, block, wide), jnp.float32),
        ],
        in_specs=[pl.BlockSpec(memory_space=pl.ANY)] * 3,
        out_specs=[pl.BlockSpec(memory_space=pltpu.VMEM)] * 3,
        scratch_shapes=[
            pltpu.VMEM(vector.shape, jnp.float32),
            pltpu.VMEM((block, wide), jnp.float32),
            pltpu.SemaphoreType.DMA((1 + 2 * count,)),
        ],
        compiler_params=pltpu.CompilerParams(vmem_limit_bytes=FETCH_ROOM),
    )(vector, lower, pivot)


def turn_held_kernel(*refs):
    half = len(refs) // 2
    for source, target in zip(refs[:half], refs[half:]):
        for k in range(source.shape[0]):
            turn_over(source.at[k], target.at[k])


def turn_held(*blocks):
    vmem = pl.BlockSpec(memory_space=pltpu.VMEM)
    return pl.pallas_call(
        turn_held_kernel,
        out_shape=[pltpu.VMEM(block.shape, jnp.float32) for block in blocks],
        in_specs=[vmem] * len(blocks),
        out_specs=[vmem] * len(blocks),
        compiler_params=pltpu.CompilerParams(vmem_limit_bytes=STAGE_ROOM),
    )(*blocks)


def load_kernel(choose, *refs):
    *refs, held, sems = refs
    size = (len(refs) - 1) // 2
    sources, targets = refs[:size], refs[size + 1 :]

    def run(sources):
        copies = start_all([(s, held.at[place]) for place, s in enumerate(sources)], sems)
        for place, target in enumerate(targets):
            copies[place].wait()
            for k in range(target.shape[0]):
                turn_over(held.at[place, k], target.at[k])

    if choose:
        even = lax.axis_index("patch") % 2 == 0
        pl.when(even)(lambda: run(sources))
        pl.when(jnp.logical_not(even))(lambda: run((*sources[:-2], sources[-1], sources[-2])))
    else:
        run(sources)


def load(blocks, after, choose=False):
    shape = blocks[0].shape
    return pl.pallas_call(
        functools.partial(load_kernel, choose),
        out_shape=[pltpu.VMEM(shape, jnp.float32) for block in blocks],
        in_specs=[pl.BlockSpec(memory_space=pl.ANY)] * (len(blocks) + 1),
        out_specs=[pl.BlockSpec(memory_space=pltpu.VMEM)] * len(blocks),
        scratch_shapes=[
            pltpu.VMEM((len(blocks),) + shape, blocks[0].dtype),
            pltpu.SemaphoreType.DMA((len(blocks),)),
        ],
        compiler_params=pltpu.CompilerParams(vmem_limit_bytes=LOAD_ROOM),
    )(*blocks, after)


def stage(kernel, out_shapes, operands, scratch=()):
    vmem = pl.BlockSpec(memory_space=pltpu.VMEM)
    return pl.pallas_call(
        kernel,
        out_shape=[pltpu.VMEM(shape, jnp.float32) for shape in out_shapes],
        in_specs=[vmem] * len(operands),
        out_specs=[vmem] * len(out_shapes),
        scratch_shapes=[pltpu.VMEM(shape, jnp.float32) for shape in scratch],
        compiler_params=pltpu.CompilerParams(vmem_limit_bytes=STAGE_ROOM),
    )(*operands)


def run_down(vector, lower, pivot, entry, forward, work):
    for k in range(vector.shape[0]):
        if k > 0:
            work[...] = vector[k] - apply_turned(lower.at[k], forward.at[k - 1])
        elif entry is not None:
            work[...] = vector[k] + apply_turned(lower.at[k], entry)
        else:
            work[...] = vector[k]
        forward[k] = apply_turned(pivot.at[k], work)


def run_up(forward, upper, pivot, incoming, result, coupled):
    count = forward.shape[0]
    for k in reversed(range(count)):
        following = result.at[k + 1] if k < count - 1 else incoming
        if following is None:
            result[k] = forward[k]
        else:
            coupled[k] = apply_turned(upper.at[k], following)
            result[k] = forward[k] - apply_turned(pivot.at[k], coupled.at[k])


def add_up(parts, target):
    total = parts[0][...]
    for part in parts[1:]:
        total = total + part[...]
    target[...] = total


def set_entry(carried, entry):
    both = carried.shape[0] == 2
    entry[...] = carried[1] - carried[0] if both else -carried[0]


def hop_down_kernel(parts, has_last, vector, lower, pivot, *refs):
    carried_in, refs = refs[:parts], refs[parts:]
    if has_last:
        last, *refs = refs
    carried, message, forward, entry, work = refs
    add_up(carried_in, carried)
    set_entry(carried, entry)
    run_down(vector, lower, pivot, entry, forward, work)
    message[0] = forward[forward.shape[0] - 1]
    if has_last:
        message[1] = last[...]


def turn_kernel(parts, vector, lower, pivot, upper, *refs):
    carried_in = refs[:parts]
    carried, forward, outgoing, entry, work, result, coupled = refs[parts:]
    add_up(carried_in, carried)
    set_entry(carried, entry)
    run_down(vector, lower, pivot, entry, forward, work)
    run_up(forward, upper, pivot, None, result, coupled)
    outgoing[...] = result[0]


def hop_up_kernel(parts, forward, upper, pivot, *refs):
    carried_in = refs[:parts]
    carried, outgoing, result, coupled = refs[parts:]
    add_up(carried_in, carried)
    run_up(forward, upper, pivot, carried, result, coupled)
    outgoing[...] = result[0]


def end_kernel(parts, forward, upper, pivot, *refs):
    carried_in = refs[:parts]
    result, coupled, last, carried = refs[parts:]
    add_up(carried_in, carried)
    run_up(forward, upper, pivot, carried, result, coupled)
    last[...] = result[result.shape[0] - 1]


def multiply_lines(left, right, out):
    block = right.shape[0]
    group = max(g for g in (1, 2, 3, 4) if block % g == 0)
    unroll = max(u for u in (1, 2, 4, 8) if block % u == 0)

    def rows(step, carry):
        start = step * group

        def add(j, totals):
            row = right[j]
            return tuple(
                total + left[start + q, pl.ds(j, 1), :] * row for q, total in enumerate(totals)
            )

        zero = jnp.zeros(right.shape[1:], jnp.float32)
        totals = lax.fori_loop(0, block, add, (zero,) * group, unroll=unroll)
        for q, total in enumerate(totals):
            out[start + q] = total
        return carry

    lax.fori_loop(0, block // group, rows, 0)


def on_last(body):
    pl.when(lax.axis_index("line") == lax.axis_size("line") - 1)(body)


def factor_kernel(lower, pivot, after, factor, out):
    def body():
        multiply_lines(lower.at[0], pivot.at[0], factor)
        multiply_lines(factor, lower.at[1], out)

    on_last(body)


def response_kernel(factor, given, upper, pivot, after, out, work):
    def body():
        multiply_lines(given, pivot.at[1], out)
        multiply_lines(out, upper.at[0], work)
        multiply_lines(work, pivot.at[0], out)

        def row(i, carry):
            out[i] = out[i] + factor[i]
            return carry

        lax.fori_loop(0, out.shape[0], row, 0, unroll=4)

    on_last(body)


def alone_kernel(forward, upper, pivot, outgoing, result, coupled):
    run_up(forward, upper, pivot, None, result, coupled)
    outgoing[...] = result[0]


def short_turn_kernel(
    vector, lower, pivot, upper, response, alone, message, carried_in, received,
    carried, upward, outgoing, passed, forward, entry, work, result, coupled,
):
    carried[...] = carried_in[...] + received[...]
    set_entry(carried, entry)
    run_down(vector, lower, pivot, entry, forward, work)
    passed[...] = forward[forward.shape[0] - 1]
    entry[...] = message[0] - passed[...]
    upward[...] = alone[...] + apply_turned(response, entry)
    run_up(forward, upper, pivot, upward, result, coupled)
    outgoing[...] = result[0]


def short_end_kernel(
    vector, lower, pivot, upper, forward_in, carried, upward, received, onward,
    result, coupled, last, forward, entry, work,
):
    forward[...] = forward_in[...]

    def again():
        entry[...] = carried[1] - onward[...]
        run_down(vector, lower, pivot, entry, forward, work)

    on_last(again)
    entry[...] = upward[...] + received[...]
    run_up(forward, upper, pivot, entry, result, coupled)
    last[...] = result[result.shape[0] - 1]


def own_kernel(vector, carried, lower, diag_block, direction, coupled, whole, image):
    for k in range(vector.shape[0]):
        value = vector[k]
        if k == 0 and carried.shape[0] == 2:
            value = value + apply_turned(lower.at[0], carried.at[1])
        whole[k] = value
        value = coupled[k] - value + apply_turned(diag_block.at[k], direction.at[k])
        if k > 0:
            value = value + apply_turned(lower.at[k], direction.at[k - 1])
        image[k] = value


def near_kernel(image, near_block, near, *refs):
    *below, out = refs
    for k in range(image.shape[0]):
        out[k] = image[k] + apply_turned(near_block.at[k], near.at[k])
    if below:
        out[0] = out[0] + apply_turned(below[0].at[0], below[1])


def next_kernel(image, far_block, far, lower, pivot, last, out, message, forward, work):
    for k in range(image.shape[0]):
        out[k] = image[k] + apply_turned(far_block.at[k], far.at[k])
    run_down(out, lower, pivot, None, forward, work)
    message[0] = forward[forward.shape[0] - 1]
    message[1] = last[...]


def place_of(pair):
    low, high = sorted(pair)
    return high * (high + 1) // 2 + low


def pair_sum(left, right):
    total = left[0] * right[0]
    for k in range(1, left.shape[0]):
        total = total + left[k] * right[k]
    return jnp.sum(total, axis=0, keepdims=True)


def sums_kernel(*refs):
    *basis, out = refs
    row = lax.broadcasted_iota(jnp.int32, out.shape, 0)
    sums = jnp.zeros(out.shape, jnp.float32)
    for i in range(len(basis)):
        for j in range(i, len(basis)):
            sums = jnp.where(row == place_of((i, j)), pair_sum(basis[i], basis[j]), sums)
    out[...] = sums


def last_kernel(image, far_block, far, sums_in, *refs):
    *basis, out, newest = refs
    for k in range(image.shape[0]):
        newest[k] = image[k] + apply_turned(far_block.at[k], far.at[k])
    sums = sums_in[...]
    row = lax.broadcasted_iota(jnp.int32, sums.shape, 0)
    lane = lax.broadcasted_iota(jnp.int32, sums.shape, 1)
    high = len(basis)
    for i, member in enumerate((*basis, newest)):
        sums = jnp.where(row == place_of((i, high)), pair_sum(member, newest), sums)
    whole = jnp.sum(sums, axis=1, keepdims=True)
    sums = jnp.sum(jnp.where(lane == row, whole, 0.0), axis=0, keepdims=True)
    out[...] = jnp.broadcast_to(sums, out.shape)


def finish_kernel(parts_ref, *refs):
    *directions, final, out, sem = refs
    width = len(directions)
    total = jnp.sum(parts_ref[...], axis=0, keepdims=True)
    shape = (SUMS, total.shape[1])
    row = lax.broadcasted_iota(jnp.int32, shape, 0)
    lane = lax.broadcasted_iota(jnp.int32, shape, 1)
    sums = jnp.sum(jnp.where(lane == row, total, 0.0), axis=1, keepdims=True)
    sums = jnp.broadcast_to(sums, shape)
    gram = {}
    for i in range(width + 1):
        for j in range(width + 1):
            place = place_of((i, j))
            gram[i, j] = sums[place : place + 1]
    half = [[gram[j + 1, i] + gram[j, i] for i in range(width + 1)] for j in range(width)]
    normal = [[half[j][i + 1] + half[j][i] for i in range(width)] for j in range(width)]
    right = [half[j][0] for j in range(width)]
    for i in range(width):
        inverse = 1.0 / normal[i][i]
        for j in range(i + 1, width):
            factor = normal[j][i] * inverse
            for k in range(i, width):
                normal[j][k] = normal[j][k] - factor * normal[i][k]
            right[j] = right[j] - factor * right[i]
    coeffs = [None] * width
    for i in reversed(range(width)):
        value = right[i]
        for k in range(i + 1, width):
            value = value - normal[i][k] * coeffs[k]
        coeffs[i] = value / normal[i][i]
    for k in range(out.shape[0]):
        step = coeffs[0] * directions[0][k]
        for j in range(1, width):
            step = step + coeffs[j] * directions[j][k]
        out[k] = step
    copy = pltpu.make_async_copy(out, final, sem)
    copy.start()
    copy.wait()


def rows_beside(field, across):
    count = lax.axis_size("patch")
    even = [(i, i + 1) for i in range(0, count - 1, 2)]
    odd = [(i, i + 1) for i in range(1, count - 1, 2)]
    is_even = lax.axis_index("patch") % 2 == 0
    first, last = field[..., :across], field[..., -across:]
    several = field.shape[-1] > across
    to_far = jnp.where(is_even, first, last) if several else field
    to_near = jnp.where(is_even, last, first) if several else field
    far = lax.ppermute(to_far, "patch", odd + [(b, a) for a, b in odd])
    near = lax.ppermute(to_near, "patch", even + [(b, a) for a, b in even])
    if several:
        up = [jnp.concatenate([field[..., across:], row], axis=-1) for row in (near, far)]
        down = [jnp.concatenate([row, field[..., :-across]], axis=-1) for row in (near, far)]
        near = jnp.where(is_even, up[0], down[0])
        far = jnp.where(is_even, down[1], up[1])
    return near, far


def sweep_short(vector, message, last, lower, pivot, upper, response):
    field, one = vector.shape, last.shape
    received = lax.ppermute(message, "line", [(0, 1), (2, 3)])
    carried, onto, forward = stage(
        functools.partial(hop_down_kernel, 1, True),
        [message.shape, message.shape, field],
        [vector, lower, pivot, received, last],
        [one, one],
    )
    received = lax.ppermute(onto, "line", [(1, 2)])
    (alone,) = stage(alone_kernel, [one], [forward, upper, pivot], [field, field])
    alone = lax.ppermute(alone, "line", [(3, 2)])
    carried, upward, outgoing, passed, forward = stage(
        short_turn_kernel,
        [message.shape, one, one, one, field],
        [vector, lower, pivot, upper, response, alone, message, carried, received],
        [one, one, field, field],
    )
    received = lax.ppermute(outgoing, "line", [(2, 1)])
    upward, outgoing = stage(
        functools.partial(hop_up_kernel, 2),
        [one, one],
        [forward, upper, pivot, upward, received],
        [field, field],
    )
    received = lax.ppermute(outgoing, "line", [(1, 0)])
    onward = lax.ppermute(passed, "line", [(2, 3)])
    direction, coupled, last = stage(
        short_end_kernel,
        [field, field, one],
        [vector, lower, pivot, upper, forward, carried, upward, received, onward],
        [field, one, one],
    )
    return direction, coupled, last, carried


def per_device(newton_residual, diag_block, lower, upper, west, east, pivot_inverse):
    shape = newton_residual.shape
    count, block, rows, across = shape
    wide = rows * across

    def flat(matrix):
        return matrix.reshape(count, block, block, wide)

    diag_block, lower, upper, west, east, pivot = map(
        flat, (diag_block, lower, upper, west, east, pivot_inverse)
    )
    line = lax.axis_size("line")
    devices = line * lax.axis_size("patch")
    one, field = (block, wide), (count, block, wide)
    vector = newton_residual.reshape(field)
    lower, pivot, message = first_carry(vector, lower, pivot)
    lower, pivot = turn_held(lower, pivot)
    basis = []
    directions = []
    last = None
    short = line == 4 and count == 2
    for j in range(ITERS):
        if j >= 2 and short:
            direction, coupled, last, carried_down = sweep_short(
                vector, message, last, lower, pivot, upper, response
            )
        else:
            parts = []
            for turn in range(line - 1):
                parts.append(lax.ppermute(message, "line", [(turn, turn + 1)]))
                if j == 0 and turn == 0:
                    (upper,) = load((upper,), message)
                if j == 0 and turn == line - 2 and short:
                    factor, response = stage(
                        factor_kernel, [(block,) + one] * 2, [lower, pivot, message]
                    )
                if turn < line - 2:
                    lasts = [] if last is None else [last]
                    carried, message = stage(
                        functools.partial(hop_down_kernel, len(parts), bool(lasts)),
                        [message.shape, message.shape],
                        [vector, lower, pivot, *parts, *lasts],
                        [field, one, one],
                    )
                    parts = [carried]
            parts = parts or [jnp.zeros_like(message)]
            carried_down, forward, outgoing = stage(
                functools.partial(turn_kernel, len(parts)),
                [message.shape, field, one],
                [vector, lower, pivot, upper, *parts],
                [one, one, field, field],
            )
            if j == 0 and short:
                outgoing, response = lax.optimization_barrier((outgoing, response))
            parts = []
            for turn in reversed(range(line - 1)):
                if j == 1 and turn == line - 3 and short:
                    outgoing, ready = lax.optimization_barrier((outgoing, response))
                    response = lax.ppermute(ready, "line", [(line - 1, line - 2)])
                parts.append(lax.ppermute(outgoing, "line", [(turn + 1, turn)]))
                if j == 0 and turn == line - 2:
                    diag_block, near_block, far_block = load(
                        (diag_block, east, west), outgoing, True
                    )
                if j == 0 and turn == line - 3 and short:
                    (response,) = stage(
                        response_kernel,
                        [(block,) + one],
                        [factor, response, upper, pivot, outgoing],
                        [(block,) + one],
                    )
                if turn > 0:
                    carried, outgoing = stage(
                        functools.partial(hop_up_kernel, len(parts)),
                        [one, one],
                        [forward, upper, pivot, *parts],
                        [field, field],
                    )
                    parts = [carried]
            parts = parts or [jnp.zeros_like(outgoing)]
            direction, coupled, last = stage(
                functools.partial(end_kernel, len(parts)),
                [field, field, one],
                [forward, upper, pivot, *parts],
                [one],
            )
        directions.append(direction)
        near, far = rows_beside(direction, across)
        whole, image = stage(
            own_kernel,
            [field, field],
            [vector, carried_down, lower, diag_block, direction, coupled],
        )
        basis.append(whole)
        beneath = []
        if j == ITERS - 1:
            (sums,) = stage(sums_kernel, [(SUMS, wide)], basis)
            below = lax.ppermute(last, "line", [(i, i + 1) for i in range(line - 1)])
            beneath = [lower, below]
        (image,) = stage(near_kernel, [field], [image, near_block, near, *beneath])
        if j < ITERS - 1:
            vector, message = stage(
                next_kernel,
                [field, (2,) + one],
                [image, far_block, far, lower, pivot, last],
                [field, one],
            )
            if j == 0 and short:
                message, response = lax.optimization_barrier((message, response))
        else:
            (sums,) = stage(
                last_kernel,
                [(devices, wide)],
                [image, far_block, far, sums, *basis],
                [field],
            )
    sums = lax.all_to_all(sums, ("line", "patch"), 0, 0, tiled=True)
    step = pl.pallas_call(
        finish_kernel,
        out_shape=jax.ShapeDtypeStruct(field, jnp.float32),
        in_specs=[pl.BlockSpec(memory_space=pltpu.VMEM)] * (1 + len(directions)),
        out_specs=pl.BlockSpec(memory_space=pl.ANY),
        scratch_shapes=[pltpu.VMEM(field, jnp.float32), pltpu.SemaphoreType.DMA],
        compiler_params=pltpu.CompilerParams(vmem_limit_bytes=STAGE_ROOM),
    )(sums, *directions)
    return step.reshape(shape)


def solution(mesh):
    blocks = P("line", None, None, "patch", None)
    field = P("line", None, "patch", None)
    return jax.shard_map(
        per_device, mesh=mesh, in_specs=(field,) + (blocks,) * 6, out_specs=field, check_vma=False
    )
```

```python
import functools

import jax
import jax.numpy as jnp
from jax import lax
from jax.experimental import pallas as pl
from jax.experimental.pallas import tpu as pltpu
from jax.sharding import PartitionSpec as P

ITERS = 4
SUMS = 16
FETCH_ROOM = 56 << 20
LOAD_ROOM = 40 << 20
STAGE_ROOM = 16 << 20


def start_all(pairs, sems):
    copies = [
        pltpu.make_async_copy(source, target, sems.at[place])
        for place, (source, target) in enumerate(pairs)
    ]
    for copy in copies:
        copy.start()
    return copies


def turn_over(source, target):
    block = source.shape[0]
    high = 16 if block % 16 == 0 else block
    wide = 8 if block % 8 == 0 else block
    for i in range(0, block, wide):
        for j in range(0, block, high):
            part = source[i : i + wide, j : j + high].astype(jnp.float32)
            target[j : j + high, i : i + wide] = jnp.swapaxes(part, 0, 1)


def apply_plain(block_mat, value, target):
    block = target.shape[0]
    rows = 16 if block % 16 == 0 else block
    for start in range(0, block, rows):
        part = block_mat[start : start + rows].astype(jnp.float32)
        target[start : start + rows] = jnp.sum(part * value[None], axis=1)


def apply_turned(block_mat, vector):
    totals = [None, None]
    for j in range(block_mat.shape[0]):
        term = block_mat[j] * vector[j : j + 1]
        totals[j % 2] = term if totals[j % 2] is None else totals[j % 2] + term
    return totals[0] + totals[1]


def first_kernel(vector, lower, pivot, lower_held, pivot_held, out, field, middle, sems):
    count = vector.shape[0]
    pairs = [(vector, field), (pivot.at[0], pivot_held.at[0])]
    for k in range(1, count):
        pairs += [(lower.at[k], lower_held.at[k]), (pivot.at[k], pivot_held.at[k])]
    pairs.append((lower.at[0], lower_held.at[0]))
    copies = start_all(pairs, sems)
    copies[0].wait()
    copies[1].wait()
    apply_plain(pivot_held.at[0], field[0], out.at[0])
    for k in range(1, count):
        copies[2 * k].wait()
        apply_plain(lower_held.at[k], out[0], middle)
        copies[2 * k + 1].wait()
        apply_plain(pivot_held.at[k], field[k] - middle[...], out.at[0])
    copies[-1].wait()


def first_carry(vector, lower, pivot):
    count, block, wide = vector.shape
    return pl.pallas_call(
        first_kernel,
        out_shape=[
            pltpu.VMEM(lower.shape, lower.dtype),
            pltpu.VMEM(pivot.shape, pivot.dtype),
            pltpu.VMEM((1, block, wide), jnp.float32),
        ],
        in_specs=[pl.BlockSpec(memory_space=pl.ANY)] * 3,
        out_specs=[pl.BlockSpec(memory_space=pltpu.VMEM)] * 3,
        scratch_shapes=[
            pltpu.VMEM(vector.shape, jnp.float32),
            pltpu.VMEM((block, wide), jnp.float32),
            pltpu.SemaphoreType.DMA((1 + 2 * count,)),
        ],
        compiler_params=pltpu.CompilerParams(vmem_limit_bytes=FETCH_ROOM),
    )(vector, lower, pivot)


def turn_held_kernel(*refs):
    half = len(refs) // 2
    for source, target in zip(refs[:half], refs[half:]):
        for k in range(source.shape[0]):
            turn_over(source.at[k], target.at[k])


def turn_held(*blocks):
    vmem = pl.BlockSpec(memory_space=pltpu.VMEM)
    return pl.pallas_call(
        turn_held_kernel,
        out_shape=[pltpu.VMEM(block.shape, jnp.float32) for block in blocks],
        in_specs=[vmem] * len(blocks),
        out_specs=[vmem] * len(blocks),
        compiler_params=pltpu.CompilerParams(vmem_limit_bytes=STAGE_ROOM),
    )(*blocks)


def load_kernel(choose, *refs):
    *refs, held, sems = refs
    size = (len(refs) - 1) // 2
    sources, targets = refs[:size], refs[size + 1 :]

    def run(sources):
        copies = start_all([(s, held.at[place]) for place, s in enumerate(sources)], sems)
        for place, target in enumerate(targets):
            copies[place].wait()
            for k in range(target.shape[0]):
                turn_over(held.at[place, k], target.at[k])

    if choose:
        even = lax.axis_index("patch") % 2 == 0
        pl.when(even)(lambda: run(sources))
        pl.when(jnp.logical_not(even))(lambda: run((*sources[:-2], sources[-1], sources[-2])))
    else:
        run(sources)


def load(blocks, after, choose=False):
    shape = blocks[0].shape
    return pl.pallas_call(
        functools.partial(load_kernel, choose),
        out_shape=[pltpu.VMEM(shape, jnp.float32) for block in blocks],
        in_specs=[pl.BlockSpec(memory_space=pl.ANY)] * (len(blocks) + 1),
        out_specs=[pl.BlockSpec(memory_space=pltpu.VMEM)] * len(blocks),
        scratch_shapes=[
            pltpu.VMEM((len(blocks),) + shape, blocks[0].dtype),
            pltpu.SemaphoreType.DMA((len(blocks),)),
        ],
        compiler_params=pltpu.CompilerParams(vmem_limit_bytes=LOAD_ROOM),
    )(*blocks, after)


def stage(kernel, out_shapes, operands, scratch=()):
    vmem = pl.BlockSpec(memory_space=pltpu.VMEM)
    return pl.pallas_call(
        kernel,
        out_shape=[pltpu.VMEM(shape, jnp.float32) for shape in out_shapes],
        in_specs=[vmem] * len(operands),
        out_specs=[vmem] * len(out_shapes),
        scratch_shapes=[pltpu.VMEM(shape, jnp.float32) for shape in scratch],
        compiler_params=pltpu.CompilerParams(vmem_limit_bytes=STAGE_ROOM),
    )(*operands)


def run_down(vector, lower, pivot, entry, forward, work):
    for k in range(vector.shape[0]):
        if k > 0:
            work[...] = vector[k] - apply_turned(lower.at[k], forward.at[k - 1])
        elif entry is not None:
            work[...] = vector[k] + apply_turned(lower.at[k], entry)
        else:
            work[...] = vector[k]
        forward[k] = apply_turned(pivot.at[k], work)


def run_up(forward, upper, pivot, incoming, result, coupled):
    count = forward.shape[0]
    for k in reversed(range(count)):
        following = result.at[k + 1] if k < count - 1 else incoming
        if following is None:
            result[k] = forward[k]
        else:
            coupled[k] = apply_turned(upper.at[k], following)
            result[k] = forward[k] - apply_turned(pivot.at[k], coupled.at[k])


def add_up(parts, target):
    total = parts[0][...]
    for part in parts[1:]:
        total = total + part[...]
    target[...] = total


def set_entry(carried, entry):
    both = carried.shape[0] == 2
    entry[...] = carried[1] - carried[0] if both else -carried[0]


def hop_down_kernel(parts, has_last, vector, lower, pivot, *refs):
    carried_in, refs = refs[:parts], refs[parts:]
    if has_last:
        last, *refs = refs
    carried, message, forward, entry, work = refs
    add_up(carried_in, carried)
    set_entry(carried, entry)
    run_down(vector, lower, pivot, entry, forward, work)
    message[0] = forward[forward.shape[0] - 1]
    if has_last:
        message[1] = last[...]


def turn_kernel(parts, vector, lower, pivot, upper, *refs):
    carried_in = refs[:parts]
    carried, forward, outgoing, entry, work, result, coupled = refs[parts:]
    add_up(carried_in, carried)
    set_entry(carried, entry)
    run_down(vector, lower, pivot, entry, forward, work)
    run_up(forward, upper, pivot, None, result, coupled)
    outgoing[...] = result[0]


def hop_up_kernel(parts, forward, upper, pivot, *refs):
    carried_in = refs[:parts]
    carried, outgoing, result, coupled = refs[parts:]
    add_up(carried_in, carried)
    run_up(forward, upper, pivot, carried, result, coupled)
    outgoing[...] = result[0]


def end_kernel(parts, forward, upper, pivot, *refs):
    carried_in = refs[:parts]
    result, coupled, last, carried = refs[parts:]
    add_up(carried_in, carried)
    run_up(forward, upper, pivot, carried, result, coupled)
    last[...] = result[result.shape[0] - 1]


def multiply_lines(left, right, out):
    block = right.shape[0]
    group = max(g for g in (1, 2, 3, 4) if block % g == 0)
    unroll = max(u for u in (1, 2, 4, 8) if block % u == 0)

    def rows(step, carry):
        start = step * group

        def add(j, totals):
            row = right[j]
            return tuple(
                total + left[start + q, pl.ds(j, 1), :] * row for q, total in enumerate(totals)
            )

        zero = jnp.zeros(right.shape[1:], jnp.float32)
        totals = lax.fori_loop(0, block, add, (zero,) * group, unroll=unroll)
        for q, total in enumerate(totals):
            out[start + q] = total
        return carry

    lax.fori_loop(0, block // group, rows, 0)


def on_last(body):
    pl.when(lax.axis_index("line") == lax.axis_size("line") - 1)(body)


def factor_kernel(lower, pivot, after, factor, out):
    def body():
        multiply_lines(lower.at[0], pivot.at[0], factor)
        multiply_lines(factor, lower.at[1], out)

    on_last(body)


def response_kernel(factor, given, upper, pivot, after, out, work):
    def body():
        multiply_lines(given, pivot.at[1], out)
        multiply_lines(out, upper.at[0], work)
        multiply_lines(work, pivot.at[0], out)

        def row(i, carry):
            out[i] = out[i] + factor[i]
            return carry

        lax.fori_loop(0, out.shape[0], row, 0, unroll=4)

    on_last(body)


def alone_kernel(forward, upper, pivot, outgoing, result, coupled):
    run_up(forward, upper, pivot, None, result, coupled)
    outgoing[...] = result[0]


def short_turn_kernel(
    vector, lower, pivot, upper, response, alone, message, carried_in, received,
    carried, upward, outgoing, passed, forward, entry, work, result, coupled,
):
    carried[...] = carried_in[...] + received[...]
    set_entry(carried, entry)
    run_down(vector, lower, pivot, entry, forward, work)
    passed[...] = forward[forward.shape[0] - 1]
    entry[...] = message[0] - passed[...]
    upward[...] = alone[...] + apply_turned(response, entry)
    run_up(forward, upper, pivot, upward, result, coupled)
    outgoing[...] = result[0]


def short_end_kernel(
    vector, lower, pivot, upper, forward_in, carried, upward, received, onward,
    result, coupled, last, forward, entry, work,
):
    forward[...] = forward_in[...]

    def again():
        entry[...] = carried[1] - onward[...]
        run_down(vector, lower, pivot, entry, forward, work)

    on_last(again)
    entry[...] = upward[...] + received[...]
    run_up(forward, upper, pivot, entry, result, coupled)
    last[...] = result[result.shape[0] - 1]


def own_kernel(vector, carried, lower, diag_block, direction, coupled, whole, image):
    for k in range(vector.shape[0]):
        value = vector[k]
        if k == 0 and carried.shape[0] == 2:
            value = value + apply_turned(lower.at[0], carried.at[1])
        whole[k] = value
        value = coupled[k] - value + apply_turned(diag_block.at[k], direction.at[k])
        if k > 0:
            value = value + apply_turned(lower.at[k], direction.at[k - 1])
        image[k] = value


def near_kernel(image, near_block, near, *refs):
    *below, out = refs
    for k in range(image.shape[0]):
        out[k] = image[k] + apply_turned(near_block.at[k], near.at[k])
    if below:
        out[0] = out[0] + apply_turned(below[0].at[0], below[1])


def next_kernel(image, far_block, far, lower, pivot, last, out, message, forward, work):
    for k in range(image.shape[0]):
        out[k] = image[k] + apply_turned(far_block.at[k], far.at[k])
    run_down(out, lower, pivot, None, forward, work)
    message[0] = forward[forward.shape[0] - 1]
    message[1] = last[...]


def place_of(pair):
    low, high = sorted(pair)
    return high * (high + 1) // 2 + low


def pair_sum(left, right):
    total = left[0] * right[0]
    for k in range(1, left.shape[0]):
        total = total + left[k] * right[k]
    return jnp.sum(total, axis=0, keepdims=True)


def sums_kernel(*refs):
    *basis, out = refs
    row = lax.broadcasted_iota(jnp.int32, out.shape, 0)
    sums = jnp.zeros(out.shape, jnp.float32)
    for i in range(len(basis)):
        for j in range(i, len(basis)):
            sums = jnp.where(row == place_of((i, j)), pair_sum(basis[i], basis[j]), sums)
    out[...] = sums


def last_kernel(image, far_block, far, sums_in, *refs):
    *basis, out, newest = refs
    for k in range(image.shape[0]):
        newest[k] = image[k] + apply_turned(far_block.at[k], far.at[k])
    sums = sums_in[...]
    row = lax.broadcasted_iota(jnp.int32, sums.shape, 0)
    lane = lax.broadcasted_iota(jnp.int32, sums.shape, 1)
    high = len(basis)
    for i, member in enumerate((*basis, newest)):
        sums = jnp.where(row == place_of((i, high)), pair_sum(member, newest), sums)
    whole = jnp.sum(sums, axis=1, keepdims=True)
    sums = jnp.sum(jnp.where(lane == row, whole, 0.0), axis=0, keepdims=True)
    out[...] = jnp.broadcast_to(sums, out.shape)


def finish_kernel(parts_ref, *refs):
    *directions, final, sound, out, sem = refs
    width = len(directions)
    total = jnp.sum(parts_ref[...], axis=0, keepdims=True)
    shape = (SUMS, total.shape[1])
    row = lax.broadcasted_iota(jnp.int32, shape, 0)
    lane = lax.broadcasted_iota(jnp.int32, shape, 1)
    sums = jnp.sum(jnp.where(lane == row, total, 0.0), axis=1, keepdims=True)
    sums = jnp.broadcast_to(sums, shape)
    gram = {}
    for i in range(width + 1):
        for j in range(width + 1):
            place = place_of((i, j))
            gram[i, j] = sums[place : place + 1]
    rest = {pair: value for pair, value in gram.items()}
    good = jnp.ones_like(gram[0, 0])
    for i in range(width + 1):
        good = jnp.where(rest[i, i] > gram[i, i] * (1.0 / 256.0), good, 0.0)
        good = jnp.where(gram[i, i] < 1e37, good, 0.0)
        inverse = 1.0 / rest[i, i]
        for j in range(i + 1, width + 1):
            factor = rest[i, j] * inverse
            for k in range(j, width + 1):
                rest[j, k] = rest[j, k] - factor * rest[i, k]
    sound[...] = good
    half = [[gram[j + 1, i] + gram[j, i] for i in range(width + 1)] for j in range(width)]
    normal = [[half[j][i + 1] + half[j][i] for i in range(width)] for j in range(width)]
    right = [half[j][0] for j in range(width)]
    for i in range(width):
        inverse = 1.0 / normal[i][i]
        for j in range(i + 1, width):
            factor = normal[j][i] * inverse
            for k in range(i, width):
                normal[j][k] = normal[j][k] - factor * normal[i][k]
            right[j] = right[j] - factor * right[i]
    coeffs = [None] * width
    for i in reversed(range(width)):
        value = right[i]
        for k in range(i + 1, width):
            value = value - normal[i][k] * coeffs[k]
        coeffs[i] = value / normal[i][i]
    for k in range(out.shape[0]):
        step = coeffs[0] * directions[0][k]
        for j in range(1, width):
            step = step + coeffs[j] * directions[j][k]
        out[k] = step
    copy = pltpu.make_async_copy(out, final, sem)
    copy.start()
    copy.wait()


def rows_beside(field, across):
    count = lax.axis_size("patch")
    even = [(i, i + 1) for i in range(0, count - 1, 2)]
    odd = [(i, i + 1) for i in range(1, count - 1, 2)]
    is_even = lax.axis_index("patch") % 2 == 0
    first, last = field[..., :across], field[..., -across:]
    several = field.shape[-1] > across
    to_far = jnp.where(is_even, first, last) if several else field
    to_near = jnp.where(is_even, last, first) if several else field
    far = lax.ppermute(to_far, "patch", odd + [(b, a) for a, b in odd])
    near = lax.ppermute(to_near, "patch", even + [(b, a) for a, b in even])
    if several:
        up = [jnp.concatenate([field[..., across:], row], axis=-1) for row in (near, far)]
        down = [jnp.concatenate([row, field[..., :-across]], axis=-1) for row in (near, far)]
        near = jnp.where(is_even, up[0], down[0])
        far = jnp.where(is_even, down[1], up[1])
    return near, far


def sweep_short(vector, message, last, lower, pivot, upper, response):
    field, one = vector.shape, last.shape
    received = lax.ppermute(message, "line", [(0, 1), (2, 3)])
    carried, onto, forward = stage(
        functools.partial(hop_down_kernel, 1, True),
        [message.shape, message.shape, field],
        [vector, lower, pivot, received, last],
        [one, one],
    )
    received = lax.ppermute(onto, "line", [(1, 2)])
    (alone,) = stage(alone_kernel, [one], [forward, upper, pivot], [field, field])
    alone = lax.ppermute(alone, "line", [(3, 2)])
    carried, upward, outgoing, passed, forward = stage(
        short_turn_kernel,
        [message.shape, one, one, one, field],
        [vector, lower, pivot, upper, response, alone, message, carried, received],
        [one, one, field, field],
    )
    received = lax.ppermute(outgoing, "line", [(2, 1)])
    upward, outgoing = stage(
        functools.partial(hop_up_kernel, 2),
        [one, one],
        [forward, upper, pivot, upward, received],
        [field, field],
    )
    received = lax.ppermute(outgoing, "line", [(1, 0)])
    onward = lax.ppermute(passed, "line", [(2, 3)])
    direction, coupled, last = stage(
        short_end_kernel,
        [field, field, one],
        [vector, lower, pivot, upper, forward, carried, upward, received, onward],
        [field, one, one],
    )
    return direction, coupled, last, carried


def plain_halo(block, sides, width):
    for axis, dim in sides:
        count = lax.axis_size(axis)
        forward = [(i, i + 1) for i in range(count - 1)]
        backward = [(target, source) for source, target in forward]
        low = lax.ppermute(
            lax.slice_in_dim(block, block.shape[dim] - width, None, axis=dim), axis, forward
        )
        high = lax.ppermute(lax.slice_in_dim(block, 0, width, axis=dim), axis, backward)
        block = jnp.concatenate([low, block, high], axis=dim)
    return block


def plain_passed(block, axis, distance):
    devices = range(lax.axis_size(axis))
    route = [(i - distance, i) for i in devices if i - distance in devices]
    return lax.ppermute(block, axis, route)


def plain_block_apply(block_mat, vector):
    return jnp.sum(block_mat.astype(jnp.float32) * vector[:, None], axis=2)


def plain_apply(block_mat, vector):
    return jnp.sum(block_mat.astype(jnp.float32) * vector[None], axis=1)


def plain_operator(field, diag_block, lower, upper, west, east):
    padded = plain_halo(field, (("line", 0), ("patch", 2)), 1)
    total = plain_block_apply(diag_block, field) + plain_block_apply(lower, padded[:-2, :, 1:-1])
    total = total + plain_block_apply(upper, padded[2:, :, 1:-1])
    return total + plain_block_apply(west, padded[1:-1, :, :-2]) + plain_block_apply(east, padded[1:-1, :, 2:])


def plain_sweep_down(vector, lower, pivot, incoming):
    previous = incoming
    forward = []
    for k in range(vector.shape[0]):
        previous = plain_apply(pivot[k], vector[k] - plain_apply(lower[k], previous))
        forward.append(previous)
    return jnp.stack(forward)


def plain_sweep_up(forward, upper, pivot, incoming):
    count = forward.shape[0]
    following = incoming
    result = [None] * count
    for k in reversed(range(count)):
        following = forward[k] - plain_apply(pivot[k], plain_apply(upper[k], following))
        result[k] = following
    return jnp.stack(result)


def plain_precondition(vector, lower, upper, pivot):
    zero_carry = jnp.zeros_like(vector[0])
    count = lax.axis_size("line")
    incoming = zero_carry
    for turn in range(count - 1):
        outgoing_down = plain_sweep_down(vector, lower, pivot, incoming)[-1]
        incoming = plain_passed(outgoing_down, "line", 1)
    forward = plain_sweep_down(vector, lower, pivot, incoming)
    outgoing = zero_carry
    for turn in range(count - 1):
        first_up = plain_sweep_up(forward, upper, pivot, outgoing)[0]
        outgoing = plain_passed(first_up, "line", -1)
    return plain_sweep_up(forward, upper, pivot, outgoing)


def plain_norm_squared(vector):
    return lax.psum(jnp.sum(vector * vector), ("line", "patch"))


def least_squares(hess, beta):
    width = hess.shape[1]
    hess_rows = [hess[i] for i in range(width + 1)]
    target = [beta] + [jnp.zeros((), jnp.float32) for i in range(width)]
    for j in range(width):
        first = hess_rows[j][j]
        second = hess_rows[j + 1][j]
        radius = jnp.sqrt(first * first + second * second)
        cosine = first / radius
        sine_part = second / radius
        upper_row = cosine * hess_rows[j] + sine_part * hess_rows[j + 1]
        lower_row = cosine * hess_rows[j + 1] - sine_part * hess_rows[j]
        hess_rows[j] = upper_row
        hess_rows[j + 1] = lower_row
        top_value = cosine * target[j] + sine_part * target[j + 1]
        low_value = cosine * target[j + 1] - sine_part * target[j]
        target[j] = top_value
        target[j + 1] = low_value
    solution = [None] * width
    for i in reversed(range(width)):
        accum_value = target[i]
        for k in range(i + 1, width):
            accum_value = accum_value - hess_rows[i][k] * solution[k]
        solution[i] = accum_value / hess_rows[i][i]
    return solution


def normalised(newton_residual, diag_block, lower, upper, west, east, pivot_inverse):
    beta = jnp.sqrt(plain_norm_squared(newton_residual))
    basis = [newton_residual / beta]
    directions = []
    columns = []
    for j in range(ITERS):
        direction = plain_precondition(basis[j], lower, upper, pivot_inverse)
        directions.append(direction)
        image = plain_operator(direction, diag_block, lower, upper, west, east)
        projections = lax.psum(
            jnp.stack([jnp.sum(member * image) for member in basis]), ("line", "patch")
        )
        for i in range(j + 1):
            image = image - projections[i] * basis[i]
        new_norm = jnp.sqrt(plain_norm_squared(image))
        basis.append(image / new_norm)
        columns.append(
            jnp.concatenate([projections, new_norm[None], jnp.zeros((ITERS - 1 - j,), jnp.float32)])
        )
    hess = jnp.stack(columns, axis=1)
    coeffs = least_squares(hess, beta)
    newton_step = coeffs[0] * directions[0]
    for j in range(1, ITERS):
        newton_step = newton_step + coeffs[j] * directions[j]
    return newton_step


def per_device(*given):
    newton_residual, diag_block, lower, upper, west, east, pivot_inverse = given
    shape = newton_residual.shape
    count, block, rows, across = shape
    wide = rows * across

    def flat(matrix):
        return matrix.reshape(count, block, block, wide)

    diag_block, lower, upper, west, east, pivot = map(
        flat, (diag_block, lower, upper, west, east, pivot_inverse)
    )
    line = lax.axis_size("line")
    devices = line * lax.axis_size("patch")
    one, field = (block, wide), (count, block, wide)
    vector = newton_residual.reshape(field)
    lower, pivot, message = first_carry(vector, lower, pivot)
    lower, pivot = turn_held(lower, pivot)
    basis = []
    directions = []
    last = None
    short = line == 4 and count == 2
    for j in range(ITERS):
        if j >= 2 and short:
            direction, coupled, last, carried_down = sweep_short(
                vector, message, last, lower, pivot, upper, response
            )
        else:
            parts = []
            for turn in range(line - 1):
                parts.append(lax.ppermute(message, "line", [(turn, turn + 1)]))
                if j == 0 and turn == 0:
                    (upper,) = load((upper,), message)
                if j == 0 and turn == line - 2 and short:
                    factor, response = stage(
                        factor_kernel, [(block,) + one] * 2, [lower, pivot, message]
                    )
                if turn < line - 2:
                    lasts = [] if last is None else [last]
                    carried, message = stage(
                        functools.partial(hop_down_kernel, len(parts), bool(lasts)),
                        [message.shape, message.shape],
                        [vector, lower, pivot, *parts, *lasts],
                        [field, one, one],
                    )
                    parts = [carried]
            parts = parts or [jnp.zeros_like(message)]
            carried_down, forward, outgoing = stage(
                functools.partial(turn_kernel, len(parts)),
                [message.shape, field, one],
                [vector, lower, pivot, upper, *parts],
                [one, one, field, field],
            )
            if j == 0 and short:
                outgoing, response = lax.optimization_barrier((outgoing, response))
            parts = []
            for turn in reversed(range(line - 1)):
                if j == 1 and turn == line - 3 and short:
                    outgoing, ready = lax.optimization_barrier((outgoing, response))
                    response = lax.ppermute(ready, "line", [(line - 1, line - 2)])
                parts.append(lax.ppermute(outgoing, "line", [(turn + 1, turn)]))
                if j == 0 and turn == line - 2:
                    diag_block, near_block, far_block = load(
                        (diag_block, east, west), outgoing, True
                    )
                if j == 0 and turn == line - 3 and short:
                    (response,) = stage(
                        response_kernel,
                        [(block,) + one],
                        [factor, response, upper, pivot, outgoing],
                        [(block,) + one],
                    )
                if turn > 0:
                    carried, outgoing = stage(
                        functools.partial(hop_up_kernel, len(parts)),
                        [one, one],
                        [forward, upper, pivot, *parts],
                        [field, field],
                    )
                    parts = [carried]
            parts = parts or [jnp.zeros_like(outgoing)]
            direction, coupled, last = stage(
                functools.partial(end_kernel, len(parts)),
                [field, field, one],
                [forward, upper, pivot, *parts],
                [one],
            )
        directions.append(direction)
        near, far = rows_beside(direction, across)
        whole, image = stage(
            own_kernel,
            [field, field],
            [vector, carried_down, lower, diag_block, direction, coupled],
        )
        basis.append(whole)
        beneath = []
        if j == ITERS - 1:
            (sums,) = stage(sums_kernel, [(SUMS, wide)], basis)
            below = lax.ppermute(last, "line", [(i, i + 1) for i in range(line - 1)])
            beneath = [lower, below]
        (image,) = stage(near_kernel, [field], [image, near_block, near, *beneath])
        if j < ITERS - 1:
            vector, message = stage(
                next_kernel,
                [field, (2,) + one],
                [image, far_block, far, lower, pivot, last],
                [field, one],
            )
            if j == 0 and short:
                message, response = lax.optimization_barrier((message, response))
        else:
            (sums,) = stage(
                last_kernel,
                [(devices, wide)],
                [image, far_block, far, sums, *basis],
                [field],
            )
    sums = lax.all_to_all(sums, ("line", "patch"), 0, 0, tiled=True)
    step, sound = pl.pallas_call(
        finish_kernel,
        out_shape=[
            jax.ShapeDtypeStruct(field, jnp.float32),
            jax.ShapeDtypeStruct((1, wide), jnp.float32),
        ],
        in_specs=[pl.BlockSpec(memory_space=pltpu.VMEM)] * (1 + len(directions)),
        out_specs=[pl.BlockSpec(memory_space=pl.ANY), pl.BlockSpec(memory_space=pltpu.VMEM)],
        scratch_shapes=[pltpu.VMEM(field, jnp.float32), pltpu.SemaphoreType.DMA],
        compiler_params=pltpu.CompilerParams(vmem_limit_bytes=STAGE_ROOM),
    )(sums, *directions)
    return lax.cond(
        sound[0, 0] > 0.5,
        lambda step, *given: step,
        lambda step, *given: normalised(*given),
        step.reshape(shape),
        *given,
    )


def solution(mesh):
    blocks = P("line", None, None, "patch", None)
    field = P("line", None, "patch", None)
    return jax.shard_map(
        per_device, mesh=mesh, in_specs=(field,) + (blocks,) * 6, out_specs=field, check_vma=False
    )
```

```python
import functools

import jax
import jax.numpy as jnp
from jax import lax
from jax.experimental import pallas as pl
from jax.experimental.pallas import tpu as pltpu
from jax.sharding import PartitionSpec as P

ITERS = 4
SUMS = 16
FETCH_ROOM = 56 << 20
LOAD_ROOM = 40 << 20
STAGE_ROOM = 16 << 20


def start_all(pairs, sems):
    copies = [
        pltpu.make_async_copy(source, target, sems.at[place])
        for place, (source, target) in enumerate(pairs)
    ]
    for copy in copies:
        copy.start()
    return copies


def turn_over(source, target):
    block = source.shape[0]
    high = 16 if block % 16 == 0 else block
    wide = 8 if block % 8 == 0 else block
    for i in range(0, block, wide):
        for j in range(0, block, high):
            part = source[i : i + wide, j : j + high].astype(jnp.float32)
            target[j : j + high, i : i + wide] = jnp.swapaxes(part, 0, 1)


def apply_plain(block_mat, value, target):
    block = target.shape[0]
    rows = 16 if block % 16 == 0 else block
    for start in range(0, block, rows):
        part = block_mat[start : start + rows].astype(jnp.float32)
        target[start : start + rows] = jnp.sum(part * value[None], axis=1)


def apply_turned(block_mat, vector):
    totals = [None, None]
    for j in range(block_mat.shape[0]):
        term = block_mat[j] * vector[j : j + 1]
        totals[j % 2] = term if totals[j % 2] is None else totals[j % 2] + term
    return totals[0] + totals[1]


def first_kernel(vector, lower, pivot, lower_held, pivot_held, out, field, middle, sems):
    count = vector.shape[0]
    pairs = [(vector, field), (pivot.at[0], pivot_held.at[0])]
    for k in range(1, count):
        pairs += [(lower.at[k], lower_held.at[k]), (pivot.at[k], pivot_held.at[k])]
    pairs.append((lower.at[0], lower_held.at[0]))
    copies = start_all(pairs, sems)
    copies[0].wait()
    copies[1].wait()
    apply_plain(pivot_held.at[0], field[0], out.at[0])
    for k in range(1, count):
        copies[2 * k].wait()
        apply_plain(lower_held.at[k], out[0], middle)
        copies[2 * k + 1].wait()
        apply_plain(pivot_held.at[k], field[k] - middle[...], out.at[0])
    copies[-1].wait()


def first_carry(vector, lower, pivot):
    count, block, wide = vector.shape
    return pl.pallas_call(
        first_kernel,
        out_shape=[
            pltpu.VMEM(lower.shape, lower.dtype),
            pltpu.VMEM(pivot.shape, pivot.dtype),
            pltpu.VMEM((1, block, wide), jnp.float32),
        ],
        in_specs=[pl.BlockSpec(memory_space=pl.ANY)] * 3,
        out_specs=[pl.BlockSpec(memory_space=pltpu.VMEM)] * 3,
        scratch_shapes=[
            pltpu.VMEM(vector.shape, jnp.float32),
            pltpu.VMEM((block, wide), jnp.float32),
            pltpu.SemaphoreType.DMA((1 + 2 * count,)),
        ],
        compiler_params=pltpu.CompilerParams(vmem_limit_bytes=FETCH_ROOM),
    )(vector, lower, pivot)


def turn_held_kernel(*refs):
    half = len(refs) // 2
    for source, target in zip(refs[:half], refs[half:]):
        for k in range(source.shape[0]):
            turn_over(source.at[k], target.at[k])


def turn_held(*blocks):
    vmem = pl.BlockSpec(memory_space=pltpu.VMEM)
    return pl.pallas_call(
        turn_held_kernel,
        out_shape=[pltpu.VMEM(block.shape, jnp.float32) for block in blocks],
        in_specs=[vmem] * len(blocks),
        out_specs=[vmem] * len(blocks),
        compiler_params=pltpu.CompilerParams(vmem_limit_bytes=STAGE_ROOM),
    )(*blocks)


def load_kernel(choose, *refs):
    *refs, held, sems = refs
    size = (len(refs) - 1) // 2
    sources, targets = refs[:size], refs[size + 1 :]

    def run(sources):
        copies = start_all([(s, held.at[place]) for place, s in enumerate(sources)], sems)
        for place, target in enumerate(targets):
            copies[place].wait()
            for k in range(target.shape[0]):
                turn_over(held.at[place, k], target.at[k])

    if choose:
        even = lax.axis_index("patch") % 2 == 0
        pl.when(even)(lambda: run(sources))
        pl.when(jnp.logical_not(even))(lambda: run((*sources[:-2], sources[-1], sources[-2])))
    else:
        run(sources)


def load(blocks, after, choose=False):
    shape = blocks[0].shape
    return pl.pallas_call(
        functools.partial(load_kernel, choose),
        out_shape=[pltpu.VMEM(shape, jnp.float32) for block in blocks],
        in_specs=[pl.BlockSpec(memory_space=pl.ANY)] * (len(blocks) + 1),
        out_specs=[pl.BlockSpec(memory_space=pltpu.VMEM)] * len(blocks),
        scratch_shapes=[
            pltpu.VMEM((len(blocks),) + shape, blocks[0].dtype),
            pltpu.SemaphoreType.DMA((len(blocks),)),
        ],
        compiler_params=pltpu.CompilerParams(vmem_limit_bytes=LOAD_ROOM),
    )(*blocks, after)


def stage(kernel, out_shapes, operands, scratch=()):
    vmem = pl.BlockSpec(memory_space=pltpu.VMEM)
    return pl.pallas_call(
        kernel,
        out_shape=[pltpu.VMEM(shape, jnp.float32) for shape in out_shapes],
        in_specs=[vmem] * len(operands),
        out_specs=[vmem] * len(out_shapes),
        scratch_shapes=[pltpu.VMEM(shape, jnp.float32) for shape in scratch],
        compiler_params=pltpu.CompilerParams(vmem_limit_bytes=STAGE_ROOM),
    )(*operands)


def run_down(vector, lower, pivot, entry, forward, work):
    for k in range(vector.shape[0]):
        if k > 0:
            work[...] = vector[k] - apply_turned(lower.at[k], forward.at[k - 1])
        elif entry is not None:
            work[...] = vector[k] + apply_turned(lower.at[k], entry)
        else:
            work[...] = vector[k]
        forward[k] = apply_turned(pivot.at[k], work)


def run_up(forward, upper, pivot, incoming, result, coupled):
    count = forward.shape[0]
    for k in reversed(range(count)):
        following = result.at[k + 1] if k < count - 1 else incoming
        if following is None:
            result[k] = forward[k]
        else:
            coupled[k] = apply_turned(upper.at[k], following)
            result[k] = forward[k] - apply_turned(pivot.at[k], coupled.at[k])


def add_up(parts, target):
    total = parts[0][...]
    for part in parts[1:]:
        total = total + part[...]
    target[...] = total


def set_entry(carried, entry):
    both = carried.shape[0] == 2
    entry[...] = carried[1] - carried[0] if both else -carried[0]


def hop_down_kernel(parts, has_last, vector, lower, pivot, *refs):
    carried_in, refs = refs[:parts], refs[parts:]
    if has_last:
        last, *refs = refs
    carried, message, forward, entry, work = refs
    add_up(carried_in, carried)
    set_entry(carried, entry)
    run_down(vector, lower, pivot, entry, forward, work)
    message[0] = forward[forward.shape[0] - 1]
    if has_last:
        message[1] = last[...]


def turn_kernel(parts, vector, lower, pivot, upper, *refs):
    carried_in = refs[:parts]
    carried, forward, outgoing, entry, work, result, coupled = refs[parts:]
    add_up(carried_in, carried)
    set_entry(carried, entry)
    run_down(vector, lower, pivot, entry, forward, work)
    run_up(forward, upper, pivot, None, result, coupled)
    outgoing[...] = result[0]


def hop_up_kernel(parts, forward, upper, pivot, *refs):
    carried_in = refs[:parts]
    carried, outgoing, result, coupled = refs[parts:]
    add_up(carried_in, carried)
    run_up(forward, upper, pivot, carried, result, coupled)
    outgoing[...] = result[0]


def end_kernel(parts, forward, upper, pivot, *refs):
    carried_in = refs[:parts]
    result, coupled, last, carried = refs[parts:]
    add_up(carried_in, carried)
    run_up(forward, upper, pivot, carried, result, coupled)
    last[...] = result[result.shape[0] - 1]


def multiply_lines(left, right, out):
    block = right.shape[0]
    group = max(g for g in (1, 2, 3, 4) if block % g == 0)
    unroll = max(u for u in (1, 2, 4, 8) if block % u == 0)

    def rows(step, carry):
        start = step * group

        def add(j, totals):
            row = right[j]
            return tuple(
                total + left[start + q, pl.ds(j, 1), :] * row for q, total in enumerate(totals)
            )

        zero = jnp.zeros(right.shape[1:], jnp.float32)
        totals = lax.fori_loop(0, block, add, (zero,) * group, unroll=unroll)
        for q, total in enumerate(totals):
            out[start + q] = total
        return carry

    lax.fori_loop(0, block // group, rows, 0)


def on_last(body):
    pl.when(lax.axis_index("line") == lax.axis_size("line") - 1)(body)


def factor_kernel(lower, pivot, after, factor, out):
    def body():
        multiply_lines(lower.at[0], pivot.at[0], factor)
        multiply_lines(factor, lower.at[1], out)

    on_last(body)


def response_kernel(factor, given, upper, pivot, after, out, work):
    def body():
        multiply_lines(given, pivot.at[1], out)
        multiply_lines(out, upper.at[0], work)
        multiply_lines(work, pivot.at[0], out)

        def row(i, carry):
            out[i] = out[i] + factor[i]
            return carry

        lax.fori_loop(0, out.shape[0], row, 0, unroll=4)

    on_last(body)


def alone_kernel(forward, upper, pivot, outgoing, result, coupled):
    run_up(forward, upper, pivot, None, result, coupled)
    outgoing[...] = result[0]


def short_turn_kernel(
    vector, lower, pivot, upper, response, alone, message, carried_in, received,
    carried, upward, outgoing, passed, forward, entry, work, result, coupled,
):
    carried[...] = carried_in[...] + received[...]
    set_entry(carried, entry)
    run_down(vector, lower, pivot, entry, forward, work)
    passed[...] = forward[forward.shape[0] - 1]
    entry[...] = message[0] - passed[...]
    upward[...] = alone[...] + apply_turned(response, entry)
    run_up(forward, upper, pivot, upward, result, coupled)
    outgoing[...] = result[0]


def short_end_kernel(
    vector, lower, pivot, upper, forward_in, carried, upward, received, onward,
    result, coupled, last, forward, entry, work,
):
    forward[...] = forward_in[...]

    def again():
        entry[...] = carried[1] - onward[...]
        run_down(vector, lower, pivot, entry, forward, work)

    on_last(again)
    entry[...] = upward[...] + received[...]
    run_up(forward, upper, pivot, entry, result, coupled)
    last[...] = result[result.shape[0] - 1]


def own_kernel(vector, carried, lower, diag_block, direction, coupled, whole, image):
    for k in range(vector.shape[0]):
        value = vector[k]
        if k == 0 and carried.shape[0] == 2:
            value = value + apply_turned(lower.at[0], carried.at[1])
        whole[k] = value
        value = coupled[k] - value + apply_turned(diag_block.at[k], direction.at[k])
        if k > 0:
            value = value + apply_turned(lower.at[k], direction.at[k - 1])
        image[k] = value


def near_kernel(image, near_block, near, out):
    for k in range(image.shape[0]):
        out[k] = image[k] + apply_turned(near_block.at[k], near.at[k])


def next_kernel(image, far_block, far, lower, pivot, last, out, message, forward, work):
    for k in range(image.shape[0]):
        out[k] = image[k] + apply_turned(far_block.at[k], far.at[k])
    run_down(out, lower, pivot, None, forward, work)
    message[0] = forward[forward.shape[0] - 1]
    message[1] = last[...]


def place_of(pair):
    low, high = sorted(pair)
    return high * (high + 1) // 2 + low


def pair_sum(left, right):
    total = left[0] * right[0]
    for k in range(1, left.shape[0]):
        total = total + left[k] * right[k]
    return jnp.sum(total, axis=0, keepdims=True)


def sums_kernel(*refs):
    *basis, out = refs
    row = lax.broadcasted_iota(jnp.int32, out.shape, 0)
    sums = jnp.zeros(out.shape, jnp.float32)
    for i in range(len(basis)):
        for j in range(i, len(basis)):
            sums = jnp.where(row == place_of((i, j)), pair_sum(basis[i], basis[j]), sums)
    out[...] = sums


def last_kernel(lower, below, image, far_block, far, sums_in, *refs):
    *basis, out, newest = refs
    for k in range(image.shape[0]):
        newest[k] = image[k] + apply_turned(far_block.at[k], far.at[k])
    newest[0] = newest[0] + apply_turned(lower.at[0], below)
    sums = sums_in[...]
    row = lax.broadcasted_iota(jnp.int32, sums.shape, 0)
    lane = lax.broadcasted_iota(jnp.int32, sums.shape, 1)
    high = len(basis)
    for i, member in enumerate((*basis, newest)):
        sums = jnp.where(row == place_of((i, high)), pair_sum(member, newest), sums)
    whole = jnp.sum(sums, axis=1, keepdims=True)
    sums = jnp.sum(jnp.where(lane == row, whole, 0.0), axis=0, keepdims=True)
    out[...] = jnp.broadcast_to(sums, out.shape)


def finish_kernel(parts_ref, *refs):
    *directions, final, sound, out, sem = refs
    width = len(directions)
    total = jnp.sum(parts_ref[...], axis=0, keepdims=True)
    shape = (SUMS, total.shape[1])
    row = lax.broadcasted_iota(jnp.int32, shape, 0)
    lane = lax.broadcasted_iota(jnp.int32, shape, 1)
    sums = jnp.sum(jnp.where(lane == row, total, 0.0), axis=1, keepdims=True)
    sums = jnp.broadcast_to(sums, shape)
    gram = {}
    for i in range(width + 1):
        for j in range(width + 1):
            place = place_of((i, j))
            gram[i, j] = sums[place : place + 1]
    rest = {pair: value for pair, value in gram.items()}
    good = jnp.ones_like(gram[0, 0])
    for i in range(width + 1):
        good = jnp.where(rest[i, i] > gram[i, i] * (1.0 / 256.0), good, 0.0)
        good = jnp.where(gram[i, i] < 1e37, good, 0.0)
        inverse = 1.0 / rest[i, i]
        for j in range(i + 1, width + 1):
            factor = rest[i, j] * inverse
            for k in range(j, width + 1):
                rest[j, k] = rest[j, k] - factor * rest[i, k]
    sound[...] = good
    half = [[gram[j + 1, i] + gram[j, i] for i in range(width + 1)] for j in range(width)]
    normal = [[half[j][i + 1] + half[j][i] for i in range(width)] for j in range(width)]
    right = [half[j][0] for j in range(width)]
    for i in range(width):
        inverse = 1.0 / normal[i][i]
        for j in range(i + 1, width):
            factor = normal[j][i] * inverse
            for k in range(i, width):
                normal[j][k] = normal[j][k] - factor * normal[i][k]
            right[j] = right[j] - factor * right[i]
    coeffs = [None] * width
    for i in reversed(range(width)):
        value = right[i]
        for k in range(i + 1, width):
            value = value - normal[i][k] * coeffs[k]
        coeffs[i] = value / normal[i][i]
    for k in range(out.shape[0]):
        step = coeffs[0] * directions[0][k]
        for j in range(1, width):
            step = step + coeffs[j] * directions[j][k]
        out[k] = step
    copy = pltpu.make_async_copy(out, final, sem)
    copy.start()
    copy.wait()


def rows_beside(field, across):
    count = lax.axis_size("patch")
    even = [(i, i + 1) for i in range(0, count - 1, 2)]
    odd = [(i, i + 1) for i in range(1, count - 1, 2)]
    is_even = lax.axis_index("patch") % 2 == 0
    first, last = field[..., :across], field[..., -across:]
    several = field.shape[-1] > across
    to_far = jnp.where(is_even, first, last) if several else field
    to_near = jnp.where(is_even, last, first) if several else field
    far = lax.ppermute(to_far, "patch", odd + [(b, a) for a, b in odd])
    near = lax.ppermute(to_near, "patch", even + [(b, a) for a, b in even])
    if several:
        up = [jnp.concatenate([field[..., across:], row], axis=-1) for row in (near, far)]
        down = [jnp.concatenate([row, field[..., :-across]], axis=-1) for row in (near, far)]
        near = jnp.where(is_even, up[0], down[0])
        far = jnp.where(is_even, down[1], up[1])
    return near, far


def sweep_short(vector, message, last, lower, pivot, upper, response):
    field, one = vector.shape, last.shape
    received = lax.ppermute(message, "line", [(0, 1), (2, 3)])
    carried, onto, forward = stage(
        functools.partial(hop_down_kernel, 1, True),
        [message.shape, message.shape, field],
        [vector, lower, pivot, received, last],
        [one, one],
    )
    received = lax.ppermute(onto, "line", [(1, 2)])
    (alone,) = stage(alone_kernel, [one], [forward, upper, pivot], [field, field])
    alone = lax.ppermute(alone, "line", [(3, 2)])
    carried, upward, outgoing, passed, forward = stage(
        short_turn_kernel,
        [message.shape, one, one, one, field],
        [vector, lower, pivot, upper, response, alone, message, carried, received],
        [one, one, field, field],
    )
    received = lax.ppermute(outgoing, "line", [(2, 1)])
    upward, outgoing = stage(
        functools.partial(hop_up_kernel, 2),
        [one, one],
        [forward, upper, pivot, upward, received],
        [field, field],
    )
    received = lax.ppermute(outgoing, "line", [(1, 0)])
    onward = lax.ppermute(passed, "line", [(2, 3)])
    direction, coupled, last = stage(
        short_end_kernel,
        [field, field, one],
        [vector, lower, pivot, upper, forward, carried, upward, received, onward],
        [field, one, one],
    )
    return direction, coupled, last, carried


def plain_halo(block, sides, width):
    for axis, dim in sides:
        count = lax.axis_size(axis)
        forward = [(i, i + 1) for i in range(count - 1)]
        backward = [(target, source) for source, target in forward]
        low = lax.ppermute(
            lax.slice_in_dim(block, block.shape[dim] - width, None, axis=dim), axis, forward
        )
        high = lax.ppermute(lax.slice_in_dim(block, 0, width, axis=dim), axis, backward)
        block = jnp.concatenate([low, block, high], axis=dim)
    return block


def plain_passed(block, axis, distance):
    devices = range(lax.axis_size(axis))
    route = [(i - distance, i) for i in devices if i - distance in devices]
    return lax.ppermute(block, axis, route)


def plain_block_apply(block_mat, vector):
    return jnp.sum(block_mat.astype(jnp.float32) * vector[:, None], axis=2)


def plain_apply(block_mat, vector):
    return jnp.sum(block_mat.astype(jnp.float32) * vector[None], axis=1)


def plain_operator(field, diag_block, lower, upper, west, east):
    padded = plain_halo(field, (("line", 0), ("patch", 2)), 1)
    total = plain_block_apply(diag_block, field) + plain_block_apply(lower, padded[:-2, :, 1:-1])
    total = total + plain_block_apply(upper, padded[2:, :, 1:-1])
    return total + plain_block_apply(west, padded[1:-1, :, :-2]) + plain_block_apply(east, padded[1:-1, :, 2:])


def plain_sweep_down(vector, lower, pivot, incoming):
    previous = incoming
    forward = []
    for k in range(vector.shape[0]):
        previous = plain_apply(pivot[k], vector[k] - plain_apply(lower[k], previous))
        forward.append(previous)
    return jnp.stack(forward)


def plain_sweep_up(forward, upper, pivot, incoming):
    count = forward.shape[0]
    following = incoming
    result = [None] * count
    for k in reversed(range(count)):
        following = forward[k] - plain_apply(pivot[k], plain_apply(upper[k], following))
        result[k] = following
    return jnp.stack(result)


def plain_precondition(vector, lower, upper, pivot):
    zero_carry = jnp.zeros_like(vector[0])
    count = lax.axis_size("line")
    incoming = zero_carry
    for turn in range(count - 1):
        outgoing_down = plain_sweep_down(vector, lower, pivot, incoming)[-1]
        incoming = plain_passed(outgoing_down, "line", 1)
    forward = plain_sweep_down(vector, lower, pivot, incoming)
    outgoing = zero_carry
    for turn in range(count - 1):
        first_up = plain_sweep_up(forward, upper, pivot, outgoing)[0]
        outgoing = plain_passed(first_up, "line", -1)
    return plain_sweep_up(forward, upper, pivot, outgoing)


def plain_norm_squared(vector):
    return lax.psum(jnp.sum(vector * vector), ("line", "patch"))


def least_squares(hess, beta):
    width = hess.shape[1]
    hess_rows = [hess[i] for i in range(width + 1)]
    target = [beta] + [jnp.zeros((), jnp.float32) for i in range(width)]
    for j in range(width):
        first = hess_rows[j][j]
        second = hess_rows[j + 1][j]
        radius = jnp.sqrt(first * first + second * second)
        cosine = first / radius
        sine_part = second / radius
        upper_row = cosine * hess_rows[j] + sine_part * hess_rows[j + 1]
        lower_row = cosine * hess_rows[j + 1] - sine_part * hess_rows[j]
        hess_rows[j] = upper_row
        hess_rows[j + 1] = lower_row
        top_value = cosine * target[j] + sine_part * target[j + 1]
        low_value = cosine * target[j + 1] - sine_part * target[j]
        target[j] = top_value
        target[j + 1] = low_value
    solution = [None] * width
    for i in reversed(range(width)):
        accum_value = target[i]
        for k in range(i + 1, width):
            accum_value = accum_value - hess_rows[i][k] * solution[k]
        solution[i] = accum_value / hess_rows[i][i]
    return solution


def normalised(newton_residual, diag_block, lower, upper, west, east, pivot_inverse):
    beta = jnp.sqrt(plain_norm_squared(newton_residual))
    basis = [newton_residual / beta]
    directions = []
    columns = []
    for j in range(ITERS):
        direction = plain_precondition(basis[j], lower, upper, pivot_inverse)
        directions.append(direction)
        image = plain_operator(direction, diag_block, lower, upper, west, east)
        projections = lax.psum(
            jnp.stack([jnp.sum(member * image) for member in basis]), ("line", "patch")
        )
        for i in range(j + 1):
            image = image - projections[i] * basis[i]
        new_norm = jnp.sqrt(plain_norm_squared(image))
        basis.append(image / new_norm)
        columns.append(
            jnp.concatenate([projections, new_norm[None], jnp.zeros((ITERS - 1 - j,), jnp.float32)])
        )
    hess = jnp.stack(columns, axis=1)
    coeffs = least_squares(hess, beta)
    newton_step = coeffs[0] * directions[0]
    for j in range(1, ITERS):
        newton_step = newton_step + coeffs[j] * directions[j]
    return newton_step


def per_device(*given):
    newton_residual, diag_block, lower, upper, west, east, pivot_inverse = given
    shape = newton_residual.shape
    count, block, rows, across = shape
    wide = rows * across

    def flat(matrix):
        return matrix.reshape(count, block, block, wide)

    diag_block, lower, upper, west, east, pivot = map(
        flat, (diag_block, lower, upper, west, east, pivot_inverse)
    )
    line = lax.axis_size("line")
    devices = line * lax.axis_size("patch")
    one, field = (block, wide), (count, block, wide)
    vector = newton_residual.reshape(field)
    lower, pivot, message = first_carry(vector, lower, pivot)
    lower, pivot = turn_held(lower, pivot)
    basis = []
    directions = []
    last = None
    short = line == 4 and count == 2
    for j in range(ITERS):
        if j >= 2 and short:
            direction, coupled, last, carried_down = sweep_short(
                vector, message, last, lower, pivot, upper, response
            )
        else:
            parts = []
            for turn in range(line - 1):
                parts.append(lax.ppermute(message, "line", [(turn, turn + 1)]))
                if j == 0 and turn == 0:
                    (upper,) = load((upper,), message)
                if j == 0 and turn == line - 2 and short:
                    factor, response = stage(
                        factor_kernel, [(block,) + one] * 2, [lower, pivot, message]
                    )
                if turn < line - 2:
                    lasts = [] if last is None else [last]
                    carried, message = stage(
                        functools.partial(hop_down_kernel, len(parts), bool(lasts)),
                        [message.shape, message.shape],
                        [vector, lower, pivot, *parts, *lasts],
                        [field, one, one],
                    )
                    parts = [carried]
            parts = parts or [jnp.zeros_like(message)]
            carried_down, forward, outgoing = stage(
                functools.partial(turn_kernel, len(parts)),
                [message.shape, field, one],
                [vector, lower, pivot, upper, *parts],
                [one, one, field, field],
            )
            if j == 0 and short:
                outgoing, response = lax.optimization_barrier((outgoing, response))
            parts = []
            for turn in reversed(range(line - 1)):
                if j == 1 and turn == line - 3 and short:
                    outgoing, ready = lax.optimization_barrier((outgoing, response))
                    response = lax.ppermute(ready, "line", [(line - 1, line - 2)])
                parts.append(lax.ppermute(outgoing, "line", [(turn + 1, turn)]))
                if j == 0 and turn == line - 2:
                    diag_block, near_block, far_block = load(
                        (diag_block, east, west), outgoing, True
                    )
                if j == 0 and turn == line - 3 and short:
                    (response,) = stage(
                        response_kernel,
                        [(block,) + one],
                        [factor, response, upper, pivot, outgoing],
                        [(block,) + one],
                    )
                if turn > 0:
                    carried, outgoing = stage(
                        functools.partial(hop_up_kernel, len(parts)),
                        [one, one],
                        [forward, upper, pivot, *parts],
                        [field, field],
                    )
                    parts = [carried]
            parts = parts or [jnp.zeros_like(outgoing)]
            direction, coupled, last = stage(
                functools.partial(end_kernel, len(parts)),
                [field, field, one],
                [forward, upper, pivot, *parts],
                [one],
            )
        directions.append(direction)
        near, far = rows_beside(direction, across)
        whole, image = stage(
            own_kernel,
            [field, field],
            [vector, carried_down, lower, diag_block, direction, coupled],
        )
        basis.append(whole)
        if j == ITERS - 1:
            (sums,) = stage(sums_kernel, [(SUMS, wide)], basis)
            below = lax.ppermute(last, "line", [(i, i + 1) for i in range(line - 1)])
        (image,) = stage(near_kernel, [field], [image, near_block, near])
        if j < ITERS - 1:
            vector, message = stage(
                next_kernel,
                [field, (2,) + one],
                [image, far_block, far, lower, pivot, last],
                [field, one],
            )
            if j == 0 and short:
                message, response = lax.optimization_barrier((message, response))
        else:
            (sums,) = stage(
                last_kernel,
                [(devices, wide)],
                [lower, below, image, far_block, far, sums, *basis],
                [field],
            )
    sums = lax.all_to_all(sums, ("line", "patch"), 0, 0, tiled=True)
    step, sound = pl.pallas_call(
        finish_kernel,
        out_shape=[
            jax.ShapeDtypeStruct(field, jnp.float32),
            jax.ShapeDtypeStruct((1, wide), jnp.float32),
        ],
        in_specs=[pl.BlockSpec(memory_space=pltpu.VMEM)] * (1 + len(directions)),
        out_specs=[pl.BlockSpec(memory_space=pl.ANY), pl.BlockSpec(memory_space=pltpu.VMEM)],
        scratch_shapes=[pltpu.VMEM(field, jnp.float32), pltpu.SemaphoreType.DMA],
        compiler_params=pltpu.CompilerParams(vmem_limit_bytes=STAGE_ROOM),
    )(sums, *directions)
    return lax.cond(
        sound[0, 0] > 0.5,
        lambda step, *given: step,
        lambda step, *given: normalised(*given),
        step.reshape(shape),
        *given,
    )


def solution(mesh):
    blocks = P("line", None, None, "patch", None)
    field = P("line", None, "patch", None)
    return jax.shard_map(
        per_device, mesh=mesh, in_specs=(field,) + (blocks,) * 6, out_specs=field, check_vma=False
    )
```

```python
import functools

import jax
import jax.numpy as jnp
from jax import lax
from jax.experimental import pallas as pl
from jax.experimental.pallas import tpu as pltpu
from jax.sharding import PartitionSpec as P

ITERS = 4
SUMS = 16
FETCH_ROOM = 56 << 20
LOAD_ROOM = 40 << 20
STAGE_ROOM = 16 << 20


def start_all(pairs, sems):
    copies = [
        pltpu.make_async_copy(source, target, sems.at[place])
        for place, (source, target) in enumerate(pairs)
    ]
    for copy in copies:
        copy.start()
    return copies


def turn_over(source, target):
    block = source.shape[0]
    high = 16 if block % 16 == 0 else block
    wide = 8 if block % 8 == 0 else block
    for i in range(0, block, wide):
        for j in range(0, block, high):
            part = source[i : i + wide, j : j + high].astype(jnp.float32)
            target[j : j + high, i : i + wide] = jnp.swapaxes(part, 0, 1)


def apply_plain(block_mat, value, target):
    block = target.shape[0]
    rows = 16 if block % 16 == 0 else block
    for start in range(0, block, rows):
        part = block_mat[start : start + rows].astype(jnp.float32)
        target[start : start + rows] = jnp.sum(part * value[None], axis=1)


def apply_turned(block_mat, vector):
    totals = [None, None]
    for j in range(block_mat.shape[0]):
        term = block_mat[j] * vector[j : j + 1]
        totals[j % 2] = term if totals[j % 2] is None else totals[j % 2] + term
    return totals[0] + totals[1]


def first_kernel(vector, lower, pivot, lower_held, pivot_held, out, field, middle, sems):
    count = vector.shape[0]
    pairs = [(vector, field), (pivot.at[0], pivot_held.at[0])]
    for k in range(1, count):
        pairs += [(lower.at[k], lower_held.at[k]), (pivot.at[k], pivot_held.at[k])]
    pairs.append((lower.at[0], lower_held.at[0]))
    copies = start_all(pairs, sems)
    copies[0].wait()
    copies[1].wait()
    apply_plain(pivot_held.at[0], field[0], out.at[0])
    for k in range(1, count):
        copies[2 * k].wait()
        apply_plain(lower_held.at[k], out[0], middle)
        copies[2 * k + 1].wait()
        apply_plain(pivot_held.at[k], field[k] - middle[...], out.at[0])
    copies[-1].wait()


def first_carry(vector, lower, pivot):
    count, block, wide = vector.shape
    return pl.pallas_call(
        first_kernel,
        out_shape=[
            pltpu.VMEM(lower.shape, lower.dtype),
            pltpu.VMEM(pivot.shape, pivot.dtype),
            pltpu.VMEM((1, block, wide), jnp.float32),
        ],
        in_specs=[pl.BlockSpec(memory_space=pl.ANY)] * 3,
        out_specs=[pl.BlockSpec(memory_space=pltpu.VMEM)] * 3,
        scratch_shapes=[
            pltpu.VMEM(vector.shape, jnp.float32),
            pltpu.VMEM((block, wide), jnp.float32),
            pltpu.SemaphoreType.DMA((1 + 2 * count,)),
        ],
        compiler_params=pltpu.CompilerParams(vmem_limit_bytes=FETCH_ROOM),
    )(vector, lower, pivot)


def turn_held_kernel(*refs):
    half = len(refs) // 2
    for source, target in zip(refs[:half], refs[half:]):
        for k in range(source.shape[0]):
            turn_over(source.at[k], target.at[k])


def turn_held(*blocks):
    vmem = pl.BlockSpec(memory_space=pltpu.VMEM)
    return pl.pallas_call(
        turn_held_kernel,
        out_shape=[pltpu.VMEM(block.shape, jnp.float32) for block in blocks],
        in_specs=[vmem] * len(blocks),
        out_specs=[vmem] * len(blocks),
        compiler_params=pltpu.CompilerParams(vmem_limit_bytes=STAGE_ROOM),
    )(*blocks)


def load_kernel(choose, *refs):
    *refs, held, sems = refs
    size = (len(refs) - 1) // 2
    sources, targets = refs[:size], refs[size + 1 :]

    def run(sources):
        copies = start_all([(s, held.at[place]) for place, s in enumerate(sources)], sems)
        for place, target in enumerate(targets):
            copies[place].wait()
            for k in range(target.shape[0]):
                turn_over(held.at[place, k], target.at[k])

    if choose:
        even = lax.axis_index("patch") % 2 == 0
        pl.when(even)(lambda: run(sources))
        pl.when(jnp.logical_not(even))(lambda: run((*sources[:-2], sources[-1], sources[-2])))
    else:
        run(sources)


def load(blocks, after, choose=False):
    shape = blocks[0].shape
    return pl.pallas_call(
        functools.partial(load_kernel, choose),
        out_shape=[pltpu.VMEM(shape, jnp.float32) for block in blocks],
        in_specs=[pl.BlockSpec(memory_space=pl.ANY)] * (len(blocks) + 1),
        out_specs=[pl.BlockSpec(memory_space=pltpu.VMEM)] * len(blocks),
        scratch_shapes=[
            pltpu.VMEM((len(blocks),) + shape, blocks[0].dtype),
            pltpu.SemaphoreType.DMA((len(blocks),)),
        ],
        compiler_params=pltpu.CompilerParams(vmem_limit_bytes=LOAD_ROOM),
    )(*blocks, after)


def stage(kernel, out_shapes, operands, scratch=()):
    vmem = pl.BlockSpec(memory_space=pltpu.VMEM)
    return pl.pallas_call(
        kernel,
        out_shape=[pltpu.VMEM(shape, jnp.float32) for shape in out_shapes],
        in_specs=[vmem] * len(operands),
        out_specs=[vmem] * len(out_shapes),
        scratch_shapes=[pltpu.VMEM(shape, jnp.float32) for shape in scratch],
        compiler_params=pltpu.CompilerParams(vmem_limit_bytes=STAGE_ROOM),
    )(*operands)


def run_down(vector, lower, pivot, entry, forward, work):
    for k in range(vector.shape[0]):
        if k > 0:
            work[...] = vector[k] - apply_turned(lower.at[k], forward.at[k - 1])
        elif entry is not None:
            work[...] = vector[k] + apply_turned(lower.at[k], entry)
        else:
            work[...] = vector[k]
        forward[k] = apply_turned(pivot.at[k], work)


def run_up(forward, upper, pivot, incoming, result, coupled):
    count = forward.shape[0]
    for k in reversed(range(count)):
        following = result.at[k + 1] if k < count - 1 else incoming
        if following is None:
            result[k] = forward[k]
        else:
            coupled[k] = apply_turned(upper.at[k], following)
            result[k] = forward[k] - apply_turned(pivot.at[k], coupled.at[k])


def add_up(parts, target):
    total = parts[0][...]
    for part in parts[1:]:
        total = total + part[...]
    target[...] = total


def set_entry(carried, entry):
    both = carried.shape[0] == 2
    entry[...] = carried[1] - carried[0] if both else -carried[0]


def hop_down_kernel(parts, has_last, vector, lower, pivot, *refs):
    carried_in, refs = refs[:parts], refs[parts:]
    if has_last:
        last, *refs = refs
    carried, message, forward, entry, work = refs
    add_up(carried_in, carried)
    set_entry(carried, entry)
    run_down(vector, lower, pivot, entry, forward, work)
    message[0] = forward[forward.shape[0] - 1]
    if has_last:
        message[1] = last[...]


def turn_kernel(parts, vector, lower, pivot, upper, *refs):
    carried_in = refs[:parts]
    carried, forward, outgoing, entry, work, result, coupled = refs[parts:]
    add_up(carried_in, carried)
    set_entry(carried, entry)
    run_down(vector, lower, pivot, entry, forward, work)
    run_up(forward, upper, pivot, None, result, coupled)
    outgoing[...] = result[0]


def hop_up_kernel(parts, forward, upper, pivot, *refs):
    carried_in = refs[:parts]
    carried, outgoing, result, coupled = refs[parts:]
    add_up(carried_in, carried)
    run_up(forward, upper, pivot, carried, result, coupled)
    outgoing[...] = result[0]


def end_kernel(parts, forward, upper, pivot, *refs):
    carried_in = refs[:parts]
    result, coupled, last, carried = refs[parts:]
    add_up(carried_in, carried)
    run_up(forward, upper, pivot, carried, result, coupled)
    last[...] = result[result.shape[0] - 1]


def multiply_lines(left, right, out):
    block = right.shape[0]
    group = max(g for g in (1, 2, 3, 4) if block % g == 0)
    unroll = max(u for u in (1, 2, 4, 8) if block % u == 0)

    def rows(step, carry):
        start = step * group

        def add(j, totals):
            row = right[j]
            return tuple(
                total + left[start + q, pl.ds(j, 1), :] * row for q, total in enumerate(totals)
            )

        zero = jnp.zeros(right.shape[1:], jnp.float32)
        totals = lax.fori_loop(0, block, add, (zero,) * group, unroll=unroll)
        for q, total in enumerate(totals):
            out[start + q] = total
        return carry

    lax.fori_loop(0, block // group, rows, 0)


def on_last(body):
    pl.when(lax.axis_index("line") == lax.axis_size("line") - 1)(body)


def factor_kernel(lower, pivot, after, factor, out):
    def body():
        multiply_lines(lower.at[0], pivot.at[0], factor)
        multiply_lines(factor, lower.at[1], out)

    on_last(body)


def response_kernel(factor, given, upper, pivot, after, out, work):
    def body():
        multiply_lines(given, pivot.at[1], out)
        multiply_lines(out, upper.at[0], work)
        multiply_lines(work, pivot.at[0], out)

        def row(i, carry):
            out[i] = out[i] + factor[i]
            return carry

        lax.fori_loop(0, out.shape[0], row, 0, unroll=4)

    on_last(body)


def alone_kernel(forward, upper, pivot, outgoing, result, coupled):
    run_up(forward, upper, pivot, None, result, coupled)
    outgoing[...] = result[0]


def short_turn_kernel(
    vector, lower, pivot, upper, response, alone, message, carried_in, received,
    carried, upward, outgoing, passed, forward, entry, work, result, coupled,
):
    carried[...] = carried_in[...] + received[...]
    set_entry(carried, entry)
    run_down(vector, lower, pivot, entry, forward, work)
    passed[...] = forward[forward.shape[0] - 1]
    entry[...] = message[0] - passed[...]
    upward[...] = alone[...] + apply_turned(response, entry)
    run_up(forward, upper, pivot, upward, result, coupled)
    outgoing[...] = result[0]


def short_end_kernel(
    vector, lower, pivot, upper, forward_in, carried, upward, received, onward,
    result, coupled, last, forward, entry, work,
):
    forward[...] = forward_in[...]

    def again():
        entry[...] = carried[1] - onward[...]
        run_down(vector, lower, pivot, entry, forward, work)

    on_last(again)
    entry[...] = upward[...] + received[...]
    run_up(forward, upper, pivot, entry, result, coupled)
    last[...] = result[result.shape[0] - 1]


def own_kernel(vector, carried, lower, diag_block, direction, coupled, whole, image):
    for k in range(vector.shape[0]):
        value = vector[k]
        if k == 0 and carried.shape[0] == 2:
            value = value + apply_turned(lower.at[0], carried.at[1])
        whole[k] = value
        value = coupled[k] - value + apply_turned(diag_block.at[k], direction.at[k])
        if k > 0:
            value = value + apply_turned(lower.at[k], direction.at[k - 1])
        image[k] = value


def near_kernel(image, near_block, near, *refs):
    *below, out = refs
    for k in range(image.shape[0]):
        out[k] = image[k] + apply_turned(near_block.at[k], near.at[k])
    if below:
        out[0] = out[0] + apply_turned(below[0].at[0], below[1])


def next_kernel(image, far_block, far, lower, pivot, last, out, message, forward, work):
    for k in range(image.shape[0]):
        out[k] = image[k] + apply_turned(far_block.at[k], far.at[k])
    run_down(out, lower, pivot, None, forward, work)
    message[0] = forward[forward.shape[0] - 1]
    message[1] = last[...]


def place_of(pair):
    low, high = sorted(pair)
    return high * (high + 1) // 2 + low


def pair_sum(left, right):
    total = left[0] * right[0]
    for k in range(1, left.shape[0]):
        total = total + left[k] * right[k]
    return jnp.sum(total, axis=0, keepdims=True)


def sums_kernel(*refs):
    *basis, out = refs
    row = lax.broadcasted_iota(jnp.int32, out.shape, 0)
    sums = jnp.zeros(out.shape, jnp.float32)
    for i in range(len(basis)):
        for j in range(i, len(basis)):
            sums = jnp.where(row == place_of((i, j)), pair_sum(basis[i], basis[j]), sums)
    out[...] = sums


def last_kernel(image, far_block, far, sums_in, *refs):
    *basis, out, newest = refs
    for k in range(image.shape[0]):
        newest[k] = image[k] + apply_turned(far_block.at[k], far.at[k])
    sums = sums_in[...]
    row = lax.broadcasted_iota(jnp.int32, sums.shape, 0)
    lane = lax.broadcasted_iota(jnp.int32, sums.shape, 1)
    high = len(basis)
    for i, member in enumerate((*basis, newest)):
        sums = jnp.where(row == place_of((i, high)), pair_sum(member, newest), sums)
    whole = jnp.sum(sums, axis=1, keepdims=True)
    sums = jnp.sum(jnp.where(lane == row, whole, 0.0), axis=0, keepdims=True)
    out[...] = jnp.broadcast_to(sums, out.shape)


def finish_kernel(parts_ref, *refs):
    *directions, final, sound, out, sem = refs
    width = len(directions)
    total = jnp.sum(parts_ref[...], axis=0, keepdims=True)
    shape = (SUMS, total.shape[1])
    row = lax.broadcasted_iota(jnp.int32, shape, 0)
    lane = lax.broadcasted_iota(jnp.int32, shape, 1)
    sums = jnp.sum(jnp.where(lane == row, total, 0.0), axis=1, keepdims=True)
    sums = jnp.broadcast_to(sums, shape)
    gram = {}
    for i in range(width + 1):
        for j in range(width + 1):
            place = place_of((i, j))
            gram[i, j] = sums[place : place + 1]
    rest = {pair: value for pair, value in gram.items()}
    good = jnp.ones_like(gram[0, 0])
    for i in range(width + 1):
        good = jnp.where(rest[i, i] > gram[i, i] * (1.0 / 256.0), good, 0.0)
        good = jnp.where(gram[i, i] < 1e37, good, 0.0)
        inverse = 1.0 / rest[i, i]
        for j in range(i + 1, width + 1):
            factor = rest[i, j] * inverse
            for k in range(j, width + 1):
                rest[j, k] = rest[j, k] - factor * rest[i, k]
    sound[...] = good
    half = [[gram[j + 1, i] + gram[j, i] for i in range(width + 1)] for j in range(width)]
    normal = [[half[j][i + 1] + half[j][i] for i in range(width)] for j in range(width)]
    right = [half[j][0] for j in range(width)]
    for i in range(width):
        inverse = 1.0 / normal[i][i]
        for j in range(i + 1, width):
            factor = normal[j][i] * inverse
            for k in range(i, width):
                normal[j][k] = normal[j][k] - factor * normal[i][k]
            right[j] = right[j] - factor * right[i]
    coeffs = [None] * width
    for i in reversed(range(width)):
        value = right[i]
        for k in range(i + 1, width):
            value = value - normal[i][k] * coeffs[k]
        coeffs[i] = value / normal[i][i]
    for k in range(out.shape[0]):
        step = coeffs[0] * directions[0][k]
        for j in range(1, width):
            step = step + coeffs[j] * directions[j][k]
        out[k] = step
    copy = pltpu.make_async_copy(out, final, sem)
    copy.start()
    copy.wait()


def rows_beside(field, across):
    count = lax.axis_size("patch")
    even = [(i, i + 1) for i in range(0, count - 1, 2)]
    odd = [(i, i + 1) for i in range(1, count - 1, 2)]
    is_even = lax.axis_index("patch") % 2 == 0
    first, last = field[..., :across], field[..., -across:]
    several = field.shape[-1] > across
    to_far = jnp.where(is_even, first, last) if several else field
    to_near = jnp.where(is_even, last, first) if several else field
    far = lax.ppermute(to_far, "patch", odd + [(b, a) for a, b in odd])
    near = lax.ppermute(to_near, "patch", even + [(b, a) for a, b in even])
    if several:
        up = [jnp.concatenate([field[..., across:], row], axis=-1) for row in (near, far)]
        down = [jnp.concatenate([row, field[..., :-across]], axis=-1) for row in (near, far)]
        near = jnp.where(is_even, up[0], down[0])
        far = jnp.where(is_even, down[1], up[1])
    return near, far


def sweep_short(vector, message, last, lower, pivot, upper, response):
    field, one = vector.shape, last.shape
    received = lax.ppermute(message, "line", [(0, 1), (2, 3)])
    carried, onto, forward = stage(
        functools.partial(hop_down_kernel, 1, True),
        [message.shape, message.shape, field],
        [vector, lower, pivot, received, last],
        [one, one],
    )
    received = lax.ppermute(onto, "line", [(1, 2)])
    (alone,) = stage(alone_kernel, [one], [forward, upper, pivot], [field, field])
    alone = lax.ppermute(alone, "line", [(3, 2)])
    carried, upward, outgoing, passed, forward = stage(
        short_turn_kernel,
        [message.shape, one, one, one, field],
        [vector, lower, pivot, upper, response, alone, message, carried, received],
        [one, one, field, field],
    )
    received = lax.ppermute(outgoing, "line", [(2, 1)])
    upward, outgoing = stage(
        functools.partial(hop_up_kernel, 2),
        [one, one],
        [forward, upper, pivot, upward, received],
        [field, field],
    )
    received = lax.ppermute(outgoing, "line", [(1, 0)])
    onward = lax.ppermute(passed, "line", [(2, 3)])
    direction, coupled, last = stage(
        short_end_kernel,
        [field, field, one],
        [vector, lower, pivot, upper, forward, carried, upward, received, onward],
        [field, one, one],
    )
    return direction, coupled, last, carried


def plain_halo(block, sides, width):
    for axis, dim in sides:
        count = lax.axis_size(axis)
        forward = [(i, i + 1) for i in range(count - 1)]
        backward = [(target, source) for source, target in forward]
        low = lax.ppermute(
            lax.slice_in_dim(block, block.shape[dim] - width, None, axis=dim), axis, forward
        )
        high = lax.ppermute(lax.slice_in_dim(block, 0, width, axis=dim), axis, backward)
        block = jnp.concatenate([low, block, high], axis=dim)
    return block


def plain_passed(block, axis, distance):
    devices = range(lax.axis_size(axis))
    route = [(i - distance, i) for i in devices if i - distance in devices]
    return lax.ppermute(block, axis, route)


def plain_block_apply(block_mat, vector):
    return jnp.sum(block_mat.astype(jnp.float32) * vector[:, None], axis=2)


def plain_apply(block_mat, vector):
    return jnp.sum(block_mat.astype(jnp.float32) * vector[None], axis=1)


def plain_operator(field, diag_block, lower, upper, west, east):
    padded = plain_halo(field, (("line", 0), ("patch", 2)), 1)
    total = plain_block_apply(diag_block, field) + plain_block_apply(lower, padded[:-2, :, 1:-1])
    total = total + plain_block_apply(upper, padded[2:, :, 1:-1])
    return total + plain_block_apply(west, padded[1:-1, :, :-2]) + plain_block_apply(east, padded[1:-1, :, 2:])


def plain_sweep_down(vector, lower, pivot, incoming):
    previous = incoming
    forward = []
    for k in range(vector.shape[0]):
        previous = plain_apply(pivot[k], vector[k] - plain_apply(lower[k], previous))
        forward.append(previous)
    return jnp.stack(forward)


def plain_sweep_up(forward, upper, pivot, incoming):
    count = forward.shape[0]
    following = incoming
    result = [None] * count
    for k in reversed(range(count)):
        following = forward[k] - plain_apply(pivot[k], plain_apply(upper[k], following))
        result[k] = following
    return jnp.stack(result)


def plain_precondition(vector, lower, upper, pivot):
    zero_carry = jnp.zeros_like(vector[0])
    count = lax.axis_size("line")
    incoming = zero_carry
    for turn in range(count - 1):
        outgoing_down = plain_sweep_down(vector, lower, pivot, incoming)[-1]
        incoming = plain_passed(outgoing_down, "line", 1)
    forward = plain_sweep_down(vector, lower, pivot, incoming)
    outgoing = zero_carry
    for turn in range(count - 1):
        first_up = plain_sweep_up(forward, upper, pivot, outgoing)[0]
        outgoing = plain_passed(first_up, "line", -1)
    return plain_sweep_up(forward, upper, pivot, outgoing)


def plain_norm_squared(vector):
    return lax.psum(jnp.sum(vector * vector), ("line", "patch"))


def least_squares(hess, beta):
    width = hess.shape[1]
    hess_rows = [hess[i] for i in range(width + 1)]
    target = [beta] + [jnp.zeros((), jnp.float32) for i in range(width)]
    for j in range(width):
        first = hess_rows[j][j]
        second = hess_rows[j + 1][j]
        radius = jnp.sqrt(first * first + second * second)
        cosine = first / radius
        sine_part = second / radius
        upper_row = cosine * hess_rows[j] + sine_part * hess_rows[j + 1]
        lower_row = cosine * hess_rows[j + 1] - sine_part * hess_rows[j]
        hess_rows[j] = upper_row
        hess_rows[j + 1] = lower_row
        top_value = cosine * target[j] + sine_part * target[j + 1]
        low_value = cosine * target[j + 1] - sine_part * target[j]
        target[j] = top_value
        target[j + 1] = low_value
    solution = [None] * width
    for i in reversed(range(width)):
        accum_value = target[i]
        for k in range(i + 1, width):
            accum_value = accum_value - hess_rows[i][k] * solution[k]
        solution[i] = accum_value / hess_rows[i][i]
    return solution


def normalised(newton_residual, diag_block, lower, upper, west, east, pivot_inverse):
    beta = jnp.sqrt(plain_norm_squared(newton_residual))
    basis = [newton_residual / beta]
    directions = []
    columns = []
    for j in range(ITERS):
        direction = plain_precondition(basis[j], lower, upper, pivot_inverse)
        directions.append(direction)
        image = plain_operator(direction, diag_block, lower, upper, west, east)
        projections = lax.psum(
            jnp.stack([jnp.sum(member * image) for member in basis]), ("line", "patch")
        )
        for i in range(j + 1):
            image = image - projections[i] * basis[i]
        new_norm = jnp.sqrt(plain_norm_squared(image))
        basis.append(image / new_norm)
        columns.append(
            jnp.concatenate([projections, new_norm[None], jnp.zeros((ITERS - 1 - j,), jnp.float32)])
        )
    hess = jnp.stack(columns, axis=1)
    coeffs = least_squares(hess, beta)
    newton_step = coeffs[0] * directions[0]
    for j in range(1, ITERS):
        newton_step = newton_step + coeffs[j] * directions[j]
    return newton_step


def per_device(*given):
    newton_residual, diag_block, lower, upper, west, east, pivot_inverse = given
    shape = newton_residual.shape
    count, block, rows, across = shape
    wide = rows * across

    def flat(matrix):
        return matrix.reshape(count, block, block, wide)

    diag_block, lower, upper, west, east, pivot = map(
        flat, (diag_block, lower, upper, west, east, pivot_inverse)
    )
    line = lax.axis_size("line")
    devices = line * lax.axis_size("patch")
    one, field = (block, wide), (count, block, wide)
    vector = newton_residual.reshape(field)
    lower, pivot, message = first_carry(vector, lower, pivot)
    lower, pivot = turn_held(lower, pivot)
    basis = []
    directions = []
    last = None
    short = line == 4 and count == 2
    for j in range(ITERS):
        if j >= 2 and short:
            direction, coupled, last, carried_down = sweep_short(
                vector, message, last, lower, pivot, upper, response
            )
        else:
            parts = []
            for turn in range(line - 1):
                parts.append(lax.ppermute(message, "line", [(turn, turn + 1)]))
                if j == 0 and turn == 0:
                    (upper,) = load((upper,), message)
                if j == 0 and turn == line - 2 and short:
                    factor, response = stage(
                        factor_kernel, [(block,) + one] * 2, [lower, pivot, message]
                    )
                if turn < line - 2:
                    lasts = [] if last is None else [last]
                    carried, message = stage(
                        functools.partial(hop_down_kernel, len(parts), bool(lasts)),
                        [message.shape, message.shape],
                        [vector, lower, pivot, *parts, *lasts],
                        [field, one, one],
                    )
                    parts = [carried]
            parts = parts or [jnp.zeros_like(message)]
            carried_down, forward, outgoing = stage(
                functools.partial(turn_kernel, len(parts)),
                [message.shape, field, one],
                [vector, lower, pivot, upper, *parts],
                [one, one, field, field],
            )
            if j == 0 and short:
                outgoing, response = lax.optimization_barrier((outgoing, response))
            parts = []
            for turn in reversed(range(line - 1)):
                parts.append(lax.ppermute(outgoing, "line", [(turn + 1, turn)]))
                if j == 1 and turn == line - 2 and short:
                    parts[-1], ready = lax.optimization_barrier((parts[-1], response))
                    response = lax.ppermute(ready, "line", [(line - 1, line - 2)])
                if j == 0 and turn == line - 2:
                    diag_block, near_block, far_block = load(
                        (diag_block, east, west), outgoing, True
                    )
                if j == 0 and turn == line - 3 and short:
                    (response,) = stage(
                        response_kernel,
                        [(block,) + one],
                        [factor, response, upper, pivot, outgoing],
                        [(block,) + one],
                    )
                if turn > 0:
                    carried, outgoing = stage(
                        functools.partial(hop_up_kernel, len(parts)),
                        [one, one],
                        [forward, upper, pivot, *parts],
                        [field, field],
                    )
                    parts = [carried]
            parts = parts or [jnp.zeros_like(outgoing)]
            direction, coupled, last = stage(
                functools.partial(end_kernel, len(parts)),
                [field, field, one],
                [forward, upper, pivot, *parts],
                [one],
            )
        directions.append(direction)
        near, far = rows_beside(direction, across)
        whole, image = stage(
            own_kernel,
            [field, field],
            [vector, carried_down, lower, diag_block, direction, coupled],
        )
        basis.append(whole)
        beneath = []
        if j == ITERS - 1:
            (sums,) = stage(sums_kernel, [(SUMS, wide)], basis)
            below = lax.ppermute(last, "line", [(i, i + 1) for i in range(line - 1)])
            beneath = [lower, below]
        (image,) = stage(near_kernel, [field], [image, near_block, near, *beneath])
        if j < ITERS - 1:
            vector, message = stage(
                next_kernel,
                [field, (2,) + one],
                [image, far_block, far, lower, pivot, last],
                [field, one],
            )
            if j == 0 and short:
                message, response = lax.optimization_barrier((message, response))
        else:
            (sums,) = stage(
                last_kernel,
                [(devices, wide)],
                [image, far_block, far, sums, *basis],
                [field],
            )
    sums = lax.all_to_all(sums, ("line", "patch"), 0, 0, tiled=True)
    step, sound = pl.pallas_call(
        finish_kernel,
        out_shape=[
            jax.ShapeDtypeStruct(field, jnp.float32),
            jax.ShapeDtypeStruct((1, wide), jnp.float32),
        ],
        in_specs=[pl.BlockSpec(memory_space=pltpu.VMEM)] * (1 + len(directions)),
        out_specs=[pl.BlockSpec(memory_space=pl.ANY), pl.BlockSpec(memory_space=pltpu.VMEM)],
        scratch_shapes=[pltpu.VMEM(field, jnp.float32), pltpu.SemaphoreType.DMA],
        compiler_params=pltpu.CompilerParams(vmem_limit_bytes=STAGE_ROOM),
    )(sums, *directions)
    return lax.cond(
        sound[0, 0] > 0.5,
        lambda step, *given: step,
        lambda step, *given: normalised(*given),
        step.reshape(shape),
        *given,
    )


def solution(mesh):
    blocks = P("line", None, None, "patch", None)
    field = P("line", None, "patch", None)
    return jax.shard_map(
        per_device, mesh=mesh, in_specs=(field,) + (blocks,) * 6, out_specs=field, check_vma=False
    )
```
